256 devices in a mesh: row: 16 (over y, z_lo, core), col: 16 (over x, z_hi).
Axes of the slice: x: 4, y: 4, z: 8 (z_hi: 4, z_lo: 2; z = z_hi * 2 + z_lo), core: 2. Of those that a mesh axis runs over, the one named last changes fastest.
Arguments:
- query_single: bfloat16 [1024, 384], P('row'), may hold values from -6 to 6
- key_single: bfloat16 [4096, 384], P('col'), may hold values from -6 to 6
- query_weight: bfloat16 [384, 336], replicated, may hold values from -0.3125 to 0.3125
- key_weight: bfloat16 [384, 816], replicated, may hold values from -0.3125 to 0.3125
- pair_weight: bfloat16 [128, 12], replicated, may hold values from -1 to 1
- head_weight: float32 [12], replicated, may hold values from 0.2 to 2
- chain_bias: float32 [12], replicated, may hold values from -2 to 2
- pair: bfloat16 [1024, 4096, 128], P('row', 'col'), may hold values from -1000 to 1000
- residue_mask: int32 [4096], replicated, may hold values 0 or 1
- chain_index: int32 [4096], replicated, may hold values from 0 to 7, never falling along the last dimension, each value on 1 to 1024 neighbouring positions
- strip_offsets: int32 [16], replicated, may hold values from 0 to 4032, as said below
- grad_single_out: bfloat16 [1024, 192], P('row'), may hold values from -4 to 4
- grad_point_out: bfloat16 [1024, 288], P('row'), may hold values from -3 to 3
- grad_pair_out: bfloat16 [1024, 1536], P('row'), may hold values from -1 to 1
Outputs:
- grad_query_single: float32 [1024, 384], P('row')
- grad_key_single: float32 [4096, 384], P('col')
- grad_query_weight: float32 [384, 336], replicated
- grad_key_weight: float32 [384, 816], replicated
- grad_pair_weight: float32 [128, 12], replicated
- grad_pair: bfloat16 [1024, 4096, 128], P('row', 'col')
The draws below stay inside these ranges and needn't reach their ends.
Inputs may be any that keep to these rules, and one draw needn't show every extreme that they name: `strip_offsets`: distinct multiples of 64; the first and the last strip of 64 residues are both among them.
All inputs are finite; a program needn't handle non-finite values.
Results may differ from the reference program's by a relative error of at most 0.012.
Values sent between devices are 32-bit elements; how exact they have to be, the bound alone decides.
No kernel may reach another device: no remote copies, remote signals or barrier semaphores. Data moves between devices by JAX's collectives and lax.ppermute only.
A program may use at most 64 MiB of HBM per device.

```python
import math
import jax
import jax.numpy as jnp
import numpy as np
from jax import lax

H = 12
C = 16
P_SIZE = 4
PV = 8
DS = 384
DZ = 128
QB = 64
N = 4096
NSTRIP = 16
Q = 1024
QF = 336
KF = 816


def pair_weight_values(key):
    values = jax.random.normal(jax.random.fold_in(key, 71), (DZ, H), jnp.float32) * DZ ** (-0.5)
    return jnp.clip(values, -1.0, 1.0)


def draw_pair_weight(key, part):
    return pair_weight_values(key).astype(jnp.bfloat16)


def draw_pair(key, part):
    inner_key = jax.random.fold_in(key, 29)
    field = jnp.clip(jax.random.normal(inner_key, (Q, N, DZ), jnp.float32), -6.0, 6.0)
    return jnp.clip(field, -1000.0, 1000.0).astype(jnp.bfloat16)


def draw_grad_pair_out(key, part):
    inner_key = jax.random.fold_in(key, 41)
    values = jnp.clip(jax.random.normal(inner_key, (Q, H * DZ), jnp.float32), -6.0, 6.0) * 0.09
    return values.astype(jnp.bfloat16)


def draw_strip_offsets(key, part):
    strip_count = N // QB
    inner_starts = jax.random.permutation(jax.random.fold_in(key, 5), strip_count - 2) + 1
    all_starts = jnp.concatenate([jnp.array([0, strip_count - 1], jnp.int32), inner_starts[:NSTRIP - 2].astype(jnp.int32)])
    shuffle = jax.random.permutation(jax.random.fold_in(key, 6), NSTRIP)
    return (all_starts[shuffle] * QB).astype(jnp.int32)


def set_ends(values, rng, smallest, high):
    longest = values.shape.index(max(values.shape))
    spots = []
    for shift in (0, 1):
        where = [jax.random.randint(jax.random.fold_in(rng, axis), (), 0, length) for axis, length in enumerate(values.shape)]
        where[longest] = (where[longest] + shift) % values.shape[longest]
        spots.append(tuple(where))
    return values.at[spots[0]].set(smallest).at[spots[1]].set(high)


def steps_of(own_key, dims, cuts, low, largest):
    loudness, own = 1.0, jax.random.fold_in(own_key, 6)
    for position, shards_of in cuts:
        heights = jnp.exp(jax.random.uniform(jax.random.fold_in(own, position), (shards_of,), jnp.float32, low / len(cuts), largest / len(cuts)))
        loudness = loudness * jnp.repeat(heights, dims[position] // shards_of).reshape([-1 if axis == position else 1 for axis in range(len(dims))])
    return loudness


def length_profile(count, total, most, skew):
    loads = [(1 << 20) // math.isqrt(rank ** skew) + 1 for rank in range(2, count + 1)]
    spare, holding = total - most - (count - 1), [1] * (count - 1)
    while spare > 0:
        movable = [i for i in range(count - 1) if holding[i] < most]
        mass, remaining = sum([loads[i] for i in movable]), spare
        for i in movable:
            extra = min(most - holding[i], max(1, remaining * loads[i] // mass), spare)
            holding[i] = holding[i] + extra
            spare = spare - extra
    return np.array([most] + holding)


def uneven_parts(own_key, count, total, limit, skew):
    if count == 2:
        one = jax.random.randint(own_key, (), max(1, total - limit), min(limit, total - 1) + 1)
        return jnp.stack([one, total - one])
    sizes = jnp.asarray(length_profile(count, total, limit, skew), jnp.int32)
    pairs = (count - 1) // 2
    donor, taker = sizes[1:1 + 2 * pairs:2], sizes[2:2 + 2 * pairs:2]
    slack = jnp.minimum(donor - 1, limit - taker)
    moved = jax.random.randint(jax.random.fold_in(own_key, 1), (pairs,), 0, 1 << 20) % (slack + 1)
    sizes = sizes.at[1:1 + 2 * pairs:2].set(donor - moved).at[2:2 + 2 * pairs:2].set(taker + moved)
    return sizes[jax.random.permutation(jax.random.fold_in(own_key, 2), count)]


def bell_draw(own_key, dims, deviation, reach, cuts=(), kind=jnp.bfloat16):
    values = jax.random.normal(own_key, dims, jnp.float32) * deviation
    if len(cuts) > 0:
        values = steps_of(own_key, dims, cuts, -0.22, 0.18) * values
    return jnp.clip(values, min=-reach, max=reach).astype(kind)


def setup_inputs(seed: int = 0) -> dict:
    key_of = jax.random.split(jax.random.key(seed), 15)
    return {
        "query_single": bell_draw(key_of[0], (Q, DS), 1.0, 6.0, ((0, 16),)),
        "key_single": bell_draw(key_of[1], (N, DS), 1.0, 6.0, ((0, 16),)),
        "query_weight": bell_draw(key_of[2], (DS, QF), DS ** -0.5, 0.3125),
        "key_weight": bell_draw(key_of[3], (DS, KF), DS ** -0.5, 0.3125),
        "pair_weight": draw_pair_weight(jax.random.fold_in(key_of[14], 71), 0),
        "head_weight": jnp.clip(jnp.exp(jax.random.uniform(key_of[5], (H,), jnp.float32, math.log(0.2), math.log(2.0))), 0.2, 2.0),
        "chain_bias": jnp.clip(jax.random.uniform(key_of[6], (H,), jnp.float32, -2.0, 2.0), -2.0, 2.0),
        "pair": draw_pair(jax.random.fold_in(key_of[14], 71), 0),
        "residue_mask": set_ends((jax.random.randint(key_of[8], (N,), 0, 8) < 7).astype(jnp.int32), jax.random.fold_in(key_of[8], 1), 0, 1),
        "chain_index": jnp.searchsorted(jnp.cumsum(uneven_parts(key_of[9], 8, N, N // 4, 2)), jnp.arange(N), side="right").astype(jnp.int32),
        "strip_offsets": draw_strip_offsets(jax.random.fold_in(key_of[14], 71), 0),
        "grad_single_out": bell_draw(key_of[11], (Q, H * C), 0.25, 4.0, ((0, 16),)),
        "grad_point_out": bell_draw(key_of[12], (Q, 3 * H * PV), 0.2, 3.0, ((0, 16),)),
        "grad_pair_out": draw_grad_pair_out(jax.random.fold_in(key_of[14], 71), 0),
    }


LOGIT_WEIGHT = math.sqrt(1.0 / 3.0)
MASKED_LOGIT = -100000.0

def as_float(array):
    return array.astype(jnp.float32)

def to_bfloat(array):
    return as_float(lax.optimization_barrier(array.astype(jnp.bfloat16)))

def strip_backward(query_feats, key_feats, pair_strip, live_pairs, same_chain, head_weight, chain_bias, pair_weight, grad_single, grad_point, grad_pairs_in):
    query_rows = query_feats.shape[0]
    key_rows = key_feats.shape[0]
    head_cols = H * C
    point_cols = 3 * H * P_SIZE
    query_feats = as_float(query_feats)
    key_feats = as_float(key_feats)
    query_vec = query_feats[:, :head_cols].reshape(query_rows, H, C)
    query_pts = query_feats[:, head_cols:].reshape(query_rows, 3, H, P_SIZE)
    key_vec = key_feats[:, :head_cols].reshape(key_rows, H, C)
    value_vec = key_feats[:, head_cols:2 * head_cols].reshape(key_rows, H, C)
    key_pts = key_feats[:, 2 * head_cols:2 * head_cols + point_cols].reshape(key_rows, 3, H, P_SIZE)
    value_pts = key_feats[:, 2 * head_cols + point_cols:].reshape(key_rows, 3, H, PV)
    pair_float = as_float(pair_strip)
    bias_weight = as_float(pair_weight)
    grad_vec = as_float(grad_single).reshape(query_rows, H, C)
    grad_pts = as_float(grad_point).reshape(query_rows, 3, H, PV)
    grad_pairs = as_float(grad_pairs_in).reshape(query_rows, H, DZ)
    scalar = jnp.einsum('ihc,jhc->hij', query_vec, key_vec, preferred_element_type=jnp.float32)
    cross_term = jnp.einsum('ixhp,jxhp->hij', query_pts, key_pts, preferred_element_type=jnp.float32)
    query_norm = lax.optimization_barrier(jnp.sum(query_pts * query_pts, axis=(1, 3))).T
    key_norm = lax.optimization_barrier(jnp.sum(key_pts * key_pts, axis=(1, 3))).T
    distance = query_norm[:, :, None] + key_norm[:, None, :] - 2.0 * cross_term
    pair_bias = jnp.einsum('ijc,ch->hij', pair_float, bias_weight, preferred_element_type=jnp.float32)
    point_coef = head_weight * (math.sqrt(2.0 / (9.0 * P_SIZE)) / 2.0)
    logits = LOGIT_WEIGHT * (scalar * C ** (-0.5) + pair_bias - point_coef[:, None, None] * distance)
    logits = logits + chain_bias[:, None, None] * same_chain[None]
    logits = jnp.where(live_pairs[None], logits, MASKED_LOGIT)
    upstream = jnp.einsum('ihc,jhc->hij', grad_vec, value_vec, preferred_element_type=jnp.float32)
    upstream = upstream + jnp.einsum('ixhv,jxhv->hij', grad_pts, value_pts, preferred_element_type=jnp.float32)
    upstream = upstream + jnp.einsum('ihc,ijc->hij', grad_pairs, pair_float, preferred_element_type=jnp.float32)
    row_top = lax.optimization_barrier(jnp.max(logits, axis=2, keepdims=True))
    exp_terms = jnp.exp(logits - row_top)
    row_total = lax.optimization_barrier(jnp.sum(exp_terms, axis=2, keepdims=True))
    weights = exp_terms / row_total
    centre = lax.optimization_barrier(jnp.sum(exp_terms * upstream, axis=2, keepdims=True)) / row_total
    score_grad = jnp.where(live_pairs[None], weights * (upstream - centre), 0.0)
    weight_bf = to_bfloat(weights)
    score_bf = to_bfloat(score_grad)
    scale_qk = LOGIT_WEIGHT * C ** (-0.5)
    grad_coef = -2.0 * LOGIT_WEIGHT * point_coef
    row_score = lax.optimization_barrier(jnp.sum(score_bf, axis=2))
    col_score = lax.optimization_barrier(jnp.sum(score_bf, axis=1))
    grad_qvec = scale_qk * jnp.einsum('hij,jhc->ihc', score_bf, key_vec, preferred_element_type=jnp.float32)
    grad_qpts = grad_coef[None, None, :, None] * (query_pts * row_score.T[:, None, :, None] - jnp.einsum('hij,jxhp->ixhp', score_bf, key_pts, preferred_element_type=jnp.float32))
    grad_kvec = scale_qk * jnp.einsum('hij,ihc->jhc', score_bf, query_vec, preferred_element_type=jnp.float32)
    grad_vvec = jnp.einsum('hij,ihc->jhc', weight_bf, grad_vec, preferred_element_type=jnp.float32)
    grad_kpts = grad_coef[None, None, :, None] * (key_pts * col_score.T[:, None, :, None] - jnp.einsum('hij,ixhp->jxhp', score_bf, query_pts, preferred_element_type=jnp.float32))
    grad_vpts = jnp.einsum('hij,ixhv->jxhv', weight_bf, grad_pts, preferred_element_type=jnp.float32)
    pair_grad = LOGIT_WEIGHT * jnp.einsum('hij,ch->ijc', score_bf, bias_weight, preferred_element_type=jnp.float32) + jnp.einsum('hij,ihc->ijc', weight_bf, grad_pairs, preferred_element_type=jnp.float32)
    bias_grad = LOGIT_WEIGHT * jnp.einsum('ijc,hij->ch', pair_float, score_bf, preferred_element_type=jnp.float32)
    query_grad = jnp.concatenate([grad_qvec.reshape(query_rows, -1), grad_qpts.reshape(query_rows, -1)], axis=1)
    key_grad = jnp.concatenate([grad_kvec.reshape(key_rows, -1), grad_vvec.reshape(key_rows, -1), grad_kpts.reshape(key_rows, -1), grad_vpts.reshape(key_rows, -1)], axis=1)
    return (query_grad, key_grad, pair_grad.astype(jnp.bfloat16), bias_grad)

def reference(query_single, key_single, query_weight, key_weight, pair_weight, head_weight, chain_bias, pair, residue_mask, chain_index, strip_offsets, grad_single_out, grad_point_out, grad_pair_out):
    query_feats = to_bfloat(jnp.dot(query_single, query_weight, preferred_element_type=jnp.float32))
    key_feats = to_bfloat(jnp.dot(key_single, key_weight, preferred_element_type=jnp.float32))
    key_live = residue_mask == 1

    def one_strip(running, strip_number):
        key_sum, bias_sum = running
        strip_begin = strip_offsets[strip_number].astype(jnp.int32)
        row_start = (strip_number * QB).astype(jnp.int32)
        query_part = lax.dynamic_slice_in_dim(query_feats, row_start, QB, 0)
        pair_strip = lax.dynamic_slice_in_dim(pair, row_start, QB, 0)
        grad_single = lax.dynamic_slice_in_dim(grad_single_out, row_start, QB, 0)
        grad_point = lax.dynamic_slice_in_dim(grad_point_out, row_start, QB, 0)
        grad_pairs_in = lax.dynamic_slice_in_dim(grad_pair_out, row_start, QB, 0)
        query_live = lax.dynamic_slice_in_dim(residue_mask, strip_begin, QB, 0) == 1
        query_chain = lax.dynamic_slice_in_dim(chain_index, strip_begin, QB, 0)
        live_pairs = query_live[:, None] & key_live[None, :]
        same_chain = (query_chain[:, None] == chain_index[None, :]).astype(jnp.float32)
        query_grad, key_grad, pair_grad, bias_grad = strip_backward(query_part, key_feats, pair_strip, live_pairs, same_chain, head_weight, chain_bias, pair_weight, grad_single, grad_point, grad_pairs_in)
        return ((key_sum + key_grad, bias_sum + bias_grad), (query_grad, pair_grad))
    start_state = (jnp.zeros((N, KF), jnp.float32), jnp.zeros((DZ, H), jnp.float32))
    finals, stacked = lax.scan(one_strip, start_state, jnp.arange(NSTRIP, dtype=jnp.int32))
    key_grad, grad_pair_weight = finals
    query_grad = stacked[0].reshape(Q, QF)
    grad_pair = stacked[1].reshape(Q, N, DZ)
    highest = lax.Precision.HIGHEST
    grad_query_single = jnp.dot(query_grad, as_float(query_weight).T, precision=highest)
    grad_query_weight = jnp.dot(as_float(query_single).T, query_grad, precision=highest)
    grad_key_single = jnp.dot(key_grad, as_float(key_weight).T, precision=highest)
    grad_key_weight = jnp.dot(as_float(key_single).T, key_grad, precision=highest)
    return (grad_query_single, grad_key_single, grad_query_weight, grad_key_weight, grad_pair_weight, grad_pair)
```

```python
import math

import jax
import jax.numpy as jnp
from jax import lax
from jax.sharding import PartitionSpec as P

H = 12
C = 16
P_SIZE = 4
PV = 8
DZ = 128
QF = 336
KF = 816
ROWS = 16
COLS = 16

LOGIT_WEIGHT = math.sqrt(1.0 / 3.0)
MASKED_LOGIT = -100000.0


def exchange(values, axis):
    return lax.all_to_all(values, axis, 0, 0)


def gather(values, axis, parts):
    return exchange(jnp.broadcast_to(values[None], (parts, *values.shape)), axis)


def sum_over_col(values):
    for step in (1, 4):
        others = [
            lax.ppermute(values, "col", [(i, i ^ (step * k)) for i in range(COLS)])
            for k in (1, 2, 3)
        ]
        values = (values + others[0]) + (others[1] + others[2])
    return values


def local(
    query_single,
    key_single,
    query_weight,
    key_weight,
    pair_weight,
    head_weight,
    chain_bias,
    pair,
    residue_mask,
    chain_index,
    strip_offsets,
    grad_single_out,
    grad_point_out,
    grad_pair_out,
):
    query_rows = query_single.shape[0]
    key_rows = key_single.shape[0]
    head_cols = H * C
    point_cols = 3 * H * P_SIZE
    highest = lax.Precision.HIGHEST
    query_feats = jnp.dot(query_single, query_weight, preferred_element_type=jnp.float32).astype(
        jnp.bfloat16
    )
    key_feats = jnp.dot(key_single, key_weight, preferred_element_type=jnp.float32).astype(
        jnp.bfloat16
    )
    query_vec = query_feats[:, :head_cols].reshape(query_rows, H, C)
    query_pts = query_feats[:, head_cols:].reshape(query_rows, 3, H, P_SIZE)
    key_vec = key_feats[:, :head_cols].reshape(key_rows, H, C)
    value_vec = key_feats[:, head_cols : 2 * head_cols].reshape(key_rows, H, C)
    key_pts = key_feats[:, 2 * head_cols : 2 * head_cols + point_cols].reshape(
        key_rows, 3, H, P_SIZE
    )
    value_pts = key_feats[:, 2 * head_cols + point_cols :].reshape(key_rows, 3, H, PV)
    grad_vec = grad_single_out.reshape(query_rows, H, C)
    grad_pts = grad_point_out.reshape(query_rows, 3, H, PV)
    grad_pairs = grad_pair_out.reshape(query_rows, H, DZ)
    strip_begin = lax.dynamic_index_in_dim(strip_offsets, lax.axis_index("row"), 0, keepdims=False)
    key_begin = lax.axis_index("col") * key_rows
    query_live = lax.dynamic_slice_in_dim(residue_mask, strip_begin, query_rows, 0) == 1
    query_chain = lax.dynamic_slice_in_dim(chain_index, strip_begin, query_rows, 0)
    key_live = lax.dynamic_slice_in_dim(residue_mask, key_begin, key_rows, 0) == 1
    key_chain = lax.dynamic_slice_in_dim(chain_index, key_begin, key_rows, 0)
    live_pairs = query_live[:, None] & key_live[None, :]
    same_chain = (query_chain[:, None] == key_chain[None, :]).astype(jnp.float32)
    scalar = jnp.einsum("ihc,jhc->hij", query_vec, key_vec, preferred_element_type=jnp.float32)
    cross_term = jnp.einsum(
        "ixhp,jxhp->hij", query_pts, key_pts, preferred_element_type=jnp.float32
    )
    query_float = query_pts.astype(jnp.float32)
    key_float = key_pts.astype(jnp.float32)
    query_norm = jnp.sum(query_float * query_float, axis=(1, 3)).T
    key_norm = jnp.sum(key_float * key_float, axis=(1, 3)).T
    distance = query_norm[:, :, None] + key_norm[:, None, :] - 2.0 * cross_term
    pair_bias = jnp.einsum("ijc,ch->hij", pair, pair_weight, preferred_element_type=jnp.float32)
    point_coef = head_weight * (math.sqrt(2.0 / (9.0 * P_SIZE)) / 2.0)
    logits = LOGIT_WEIGHT * (
        scalar * C ** (-0.5) + pair_bias - point_coef[:, None, None] * distance
    )
    logits = logits + chain_bias[:, None, None] * same_chain[None]
    logits = jnp.where(live_pairs[None], logits, MASKED_LOGIT)
    upstream = jnp.einsum("ihc,jhc->hij", grad_vec, value_vec, preferred_element_type=jnp.float32)
    upstream = upstream + jnp.einsum(
        "ixhv,jxhv->hij", grad_pts, value_pts, preferred_element_type=jnp.float32
    )
    upstream = upstream + jnp.einsum(
        "ihc,ijc->hij", grad_pairs, pair, preferred_element_type=jnp.float32
    )
    own_top = jnp.max(logits, axis=2)
    exp_terms = jnp.exp(logits - own_top[:, :, None])
    own_total = jnp.sum(exp_terms, axis=2)
    own_moment = jnp.sum(exp_terms * upstream, axis=2)
    with jax.named_scope("row_statistics"):
        parts = jnp.stack([own_top, own_total, own_moment]).reshape(3, 6, 128)
        parts = gather(parts, "col", COLS).reshape(COLS, 3, H, query_rows)
        row_top = jnp.max(parts[:, 0], axis=0)
        shares = jnp.exp(parts[:, 0] - row_top[None])
        row_total = jnp.sum(shares * parts[:, 1], axis=0)
        moment = jnp.sum(shares * parts[:, 2], axis=0)
    weights = exp_terms * (jnp.exp(own_top - row_top) / row_total)[:, :, None]
    centre = moment / row_total
    score_grad = jnp.where(live_pairs[None], weights * (upstream - centre[:, :, None]), 0.0)
    weight_bf = weights.astype(jnp.bfloat16)
    score_bf = score_grad.astype(jnp.bfloat16)
    scale_qk = LOGIT_WEIGHT * C ** (-0.5)
    grad_coef = -2.0 * LOGIT_WEIGHT * point_coef
    row_score = jnp.sum(score_bf, axis=2, dtype=jnp.float32)
    col_score = jnp.sum(score_bf, axis=1, dtype=jnp.float32)
    grad_qvec = scale_qk * jnp.einsum(
        "hij,jhc->ihc", score_bf, key_vec, preferred_element_type=jnp.float32
    )
    grad_qpts = grad_coef[None, None, :, None] * (
        query_float * row_score.T[:, None, :, None]
        - jnp.einsum("hij,jxhp->ixhp", score_bf, key_pts, preferred_element_type=jnp.float32)
    )
    query_part = jnp.concatenate(
        [grad_qvec.reshape(query_rows, -1), grad_qpts.reshape(query_rows, -1)], axis=1
    )
    with jax.named_scope("query_sum"):
        query_grad = sum_over_col(query_part)
    grad_kvec = scale_qk * jnp.einsum(
        "hij,ihc->hcj", score_bf, query_vec, preferred_element_type=jnp.float32
    )
    grad_vvec = jnp.einsum("hij,ihc->hcj", weight_bf, grad_vec, preferred_element_type=jnp.float32)
    grad_kpts = grad_coef[None, :, None, None] * (
        key_float.transpose(1, 2, 3, 0) * col_score[None, :, None, :]
        - jnp.einsum("hij,ixhp->xhpj", score_bf, query_pts, preferred_element_type=jnp.float32)
    )
    grad_vpts = jnp.einsum(
        "hij,ixhv->xhvj", weight_bf, grad_pts, preferred_element_type=jnp.float32
    )
    key_part = jnp.concatenate(
        [
            grad_kvec.reshape(-1, key_rows),
            grad_vvec.reshape(-1, key_rows),
            grad_kpts.reshape(-1, key_rows),
            grad_vpts.reshape(-1, key_rows),
        ],
        axis=0,
    )
    bias_part = LOGIT_WEIGHT * jnp.einsum(
        "ijc,hij->hc", pair, score_bf, preferred_element_type=jnp.float32
    )
    key_single_part = jnp.dot(key_weight.astype(jnp.float32), key_part, precision=highest)
    with jax.named_scope("key_sum"):
        sent = jnp.concatenate(
            [
                key_part.reshape(ROWS, KF // ROWS, key_rows),
                jnp.pad(bias_part, ((0, ROWS - H), (0, key_rows - DZ)))[:, None],
                key_single_part.reshape(ROWS, -1, key_rows),
            ],
            axis=1,
        )
        summed = jnp.sum(exchange(sent, "row"), axis=0)
    feats = KF // ROWS
    key_share = jnp.dot(
        summed[:feats], key_single.astype(jnp.float32), precision=highest
    )
    share = jnp.concatenate(
        [key_share, jnp.pad(summed[feats : feats + 1], ((0, 0), (0, 384 - key_rows)))], axis=0
    )
    with jax.named_scope("key_weight_sum"):
        share = sum_over_col(share)
    grad_query_single = jnp.dot(query_grad, query_weight.astype(jnp.float32).T, precision=highest)
    query_weight_part = lax.dot_general(
        query_grad, query_single.astype(jnp.float32), (((0,), (0,)), ((), ())), precision=highest
    )
    with jax.named_scope("query_weight_sum"):
        single = summed[feats + 1 :]
        lanes = [
            query_weight_part[:, 128 * k : 128 * (k + 1)].reshape(ROWS, QF // ROWS, 128)
            for k in range(3)
        ] + [
            jnp.broadcast_to(single[None, :, 128 * k : 128 * (k + 1)], (ROWS, 24, 128))
            for k in range(2)
        ]
        got = exchange(jnp.concatenate(lanes, axis=1), "row")
        step = QF // ROWS
        query_share = jnp.sum(got[:, : 3 * step], axis=0)
        query_share = jnp.concatenate(
            [query_share[step * k : step * (k + 1)] for k in range(3)], axis=1
        )
        grad_key_single = jnp.concatenate(
            [got[:, 3 * step : 3 * step + 24].reshape(384, 128), got[:, 3 * step + 24 :].reshape(384, 128)],
            axis=1,
        ).T
    with jax.named_scope("weight_gather"):
        full = gather(jnp.concatenate([share, query_share], axis=0), "row", ROWS)
        grad_key_weight = full[:, :feats].reshape(KF, -1).T
        grad_pair_weight = full[:H, feats, :DZ].T
        grad_query_weight = full[:, feats + 1 :].reshape(QF, -1).T
    pair_grad = LOGIT_WEIGHT * jnp.einsum(
        "hij,ch->ijc", score_bf, pair_weight, preferred_element_type=jnp.float32
    )
    pair_grad = pair_grad + jnp.einsum(
        "hij,ihc->ijc", weight_bf, grad_pairs, preferred_element_type=jnp.float32
    )
    grad_pair = pair_grad.astype(jnp.bfloat16)
    return (
        grad_query_single,
        grad_key_single,
        grad_query_weight,
        grad_key_weight,
        grad_pair_weight,
        grad_pair,
    )


def solution(mesh):
    in_specs = (
        P("row", None),
        P("col", None),
        P(),
        P(),
        P(),
        P(),
        P(),
        P("row", "col", None),
        P(),
        P(),
        P(),
        P("row", None),
        P("row", None),
        P("row", None),
    )
    out_specs = (P("row", None), P("col", None), P(), P(), P(), P("row", "col", None))
    return jax.shard_map(local, mesh=mesh, in_specs=in_specs, out_specs=out_specs, check_vma=False)
```

```python
import math

import jax
import jax.numpy as jnp
from jax import lax
from jax.experimental import pallas as pl
from jax.experimental.pallas import tpu as pltpu
from jax.sharding import PartitionSpec as P

H = 12
C = 16
P_SIZE = 4
PV = 8
DZ = 128
DS = 384
QB = 64
KB = 256
QF = 336
KF = 816
VEC = H * C
QPTS = 3 * H * P_SIZE
VPTS = 3 * H * PV
ROWS = 16
COLS = 16
HP = 16
STEP = 16
STEPS = QB // STEP
SLAB = STEP * HP
ALL = QB * HP
FEATS = 56
SHARE = 232

LOGIT_WEIGHT = math.sqrt(1.0 / 3.0)
MASKED_LOGIT = -100000.0
SCALE_QK = LOGIT_WEIGHT * C ** (-0.5)
POINT_SCALE = math.sqrt(2.0 / (9.0 * P_SIZE)) / 2.0
F32 = jnp.float32
BF16 = jnp.bfloat16
HIGHEST = lax.Precision.HIGHEST

NN = (((1,), (0,)), ((), ()))
NT = (((1,), (1,)), ((), ()))
TN = (((0,), (0,)), ((), ()))


def dot(a, b, dims=NN, precision=None):
    return lax.dot_general(a, b, dims, precision=precision, preferred_element_type=F32)


def two_part_dot(fixed, values, dims, values_first=False):
    high = values.astype(BF16)
    low = (values - high.astype(F32)).astype(BF16)
    if values_first:
        return dot(high, fixed, dims) + dot(low, fixed, dims)
    return dot(fixed, high, dims) + dot(fixed, low, dims)


def head_mask(count, group, size, offset=0, axis=1):
    shape = (HP, count) if axis == 1 else (count, HP)
    feature = lax.broadcasted_iota(jnp.int32, shape, axis)
    head = lax.broadcasted_iota(jnp.int32, shape, 1 - axis)
    return jnp.where(lax.div(lax.rem(feature, group), size) == head, 1.0, 0.0).astype(F32)


def query_mask():
    shape = (HP, QF)
    feature = lax.broadcasted_iota(jnp.int32, shape, 1)
    head = lax.broadcasted_iota(jnp.int32, shape, 0)
    of = jnp.where(
        feature < VEC,
        lax.div(feature, C),
        lax.div(lax.rem(jnp.maximum(feature - VEC, 0), H * P_SIZE), P_SIZE),
    )
    return jnp.where(of == head, 1.0, 0.0).astype(F32), feature < VEC


def spread(values, mask):
    rows, count = values.shape
    return (values.astype(F32)[:, None, :] * mask[None]).reshape(rows * HP, count)


def head_column(ref, scale, count):
    index = lax.broadcasted_iota(jnp.int32, (HP, count), 0)
    column = jnp.zeros((HP, count), F32)
    for h in range(H):
        column = jnp.where(index == h, ref[h] * scale, column)
    return column


def head_row(ref, scale, count):
    index = lax.broadcasted_iota(jnp.int32, (count, HP), 1)
    row = jnp.zeros((count, HP), F32)
    for h in range(H):
        row = jnp.where(index == h, ref[h] * scale, row)
    return row


def key_line(ref):
    begin = lax.axis_index("col") * 2
    return jnp.concatenate([ref[pl.ds(begin, 1), :], ref[pl.ds(begin + 1, 1), :]], axis=1)


def score_kernel(
    offsets,
    mask_s,
    chain_s,
    head_weight,
    chain_bias,
    mask_v,
    chain_v,
    query_single,
    key_single,
    query_weight,
    key_weight,
    pair_weight,
    pair,
    grad_single,
    grad_point,
    grad_pairs,
    exp_out,
    up_out,
    key_out,
    query_out,
    heads_out,
    stats_out,
    key_qk,
    key_v,
    key_norm,
    both,
    stat,
    spread_pairs,
):
    step = pl.program_id(0)

    @pl.when(step == 0)
    def _():
        feats = lax.dot_general(
            key_weight[...], key_single[...], (((0,), (1,)), ((), ())), preferred_element_type=F32
        ).astype(BF16)
        key_qk[0:VEC] = feats[0:VEC]
        key_qk[VEC:QF] = feats[2 * VEC : 2 * VEC + QPTS]
        key_v[0:VEC] = feats[VEC : 2 * VEC]
        key_v[VEC:] = feats[2 * VEC + QPTS :]
        key_out[...] = key_qk[...]
        points = feats[2 * VEC : 2 * VEC + QPTS].astype(F32)
        key_norm[...] = dot(
            head_mask(QPTS, H * P_SIZE, P_SIZE), points * points, NN, HIGHEST
        )
        unit = jnp.where(
            lax.broadcasted_iota(jnp.int32, (HP, H), 0)
            == lax.broadcasted_iota(jnp.int32, (HP, H), 1),
            1.0,
            0.0,
        ).astype(BF16)
        both[0:HP] = dot(unit, pair_weight[...], NT).astype(BF16)
        spread_pairs[...] = jnp.zeros_like(spread_pairs)
        stat[...] = jnp.zeros_like(stat)

    mask, is_vec = query_mask()
    query = dot(query_single[...], query_weight[...]).astype(BF16)
    query_out[...] = query
    rows = spread(query, mask)
    vec_rows = jnp.where(is_vec[0:1], rows, 0.0)
    point_rows = rows - vec_rows
    query_norm = jnp.sum(point_rows * point_rows, axis=1, keepdims=True)
    scalar = dot(vec_rows.astype(BF16), key_qk[...])
    cross = dot(point_rows.astype(BF16), key_qk[...])
    upstream = dot(spread(grad_single[...], head_mask(VEC, VEC, C)).astype(BF16), key_v[0:VEC])
    upstream += dot(
        spread(grad_point[...], head_mask(VPTS, H * PV, PV)).astype(BF16), key_v[VEC:]
    )
    pairs = grad_pairs[...].astype(F32)
    for h in range(H):
        spread_pairs[:, h, :] = pairs[:, DZ * h : DZ * (h + 1)]
    heads = spread_pairs[...].astype(BF16)
    heads_out[...] = heads

    point_coef = head_column(head_weight, POINT_SCALE, KB)
    bias = head_column(chain_bias, 1.0, KB)
    key_live = key_line(mask_v) == 1
    key_chain = key_line(chain_v)
    begin = offsets[lax.axis_index("row")] + step * STEP
    lane = lax.broadcasted_iota(jnp.int32, (HP, 128), 1)
    for i in range(STEP):
        at = slice(HP * i, HP * (i + 1))
        left = jnp.concatenate([both[0:HP], heads[i]], axis=0)
        tile = dot(left, pair[i], NT)
        distance = query_norm[at] + key_norm[...] - 2.0 * cross[at]
        logits = LOGIT_WEIGHT * (scalar[at] * C ** (-0.5) + tile[0:HP] - point_coef * distance)
        same = jnp.where(key_chain == chain_s[begin + i], 1.0, 0.0)
        logits = logits + bias * same
        live = jnp.where(key_live, mask_s[begin + i], 0) == 1
        logits = jnp.where(live, logits, MASKED_LOGIT)
        up = upstream[at] + tile[HP:]
        top = jnp.max(logits, axis=1, keepdims=True)
        terms = jnp.exp(logits - top)
        total = jnp.sum(terms, axis=1, keepdims=True)
        moment = jnp.sum(terms * up, axis=1, keepdims=True)
        exp_out[at] = terms
        up_out[at] = up
        stat[at] = jnp.where(lane == 0, top, jnp.where(lane == 1, total, moment))
    for half in range(2):
        turned = stat[128 * half : 128 * (half + 1)].T
        for k in range(3):
            stats_out[k, pl.ds(2 * step + half, 1), :] = turned[k : k + 1]


def grad_kernel(
    offsets,
    mask_s,
    head_weight,
    mask_v,
    parts,
    own,
    exp_terms,
    up,
    key_qk,
    query,
    query_single,
    query_weight,
    key_weight,
    grad_single,
    grad_point,
    weight_out,
    score_out,
    kept_out,
    given_out,
    single_out,
    key_grad,
    key_single_grad,
    query_weight_grad,
):
    row_top = parts[0, 0]
    for s in range(1, COLS):
        row_top = jnp.maximum(row_top, parts[s, 0])
    row_total = jnp.zeros_like(row_top)
    moment = jnp.zeros_like(row_top)
    for s in range(COLS):
        share = jnp.exp(parts[s, 0] - row_top)
        row_total += share * parts[s, 1]
        moment += share * parts[s, 2]
    factor = jnp.exp(own[0] - row_top) / row_total
    centre = moment / row_total
    columns = jnp.concatenate([factor, centre], axis=0).T
    key_live = jnp.where(key_line(mask_v) == 1, 1.0, 0.0)
    begin = offsets[lax.axis_index("row")]
    col_score = jnp.zeros((HP, KB), F32)
    row_score = []
    for i in range(QB):
        at = slice(HP * i, HP * (i + 1))
        chunk, off = i // 8, HP * (i % 8)
        fac = columns[off : off + HP, chunk : chunk + 1]
        mid = columns[off : off + HP, 8 + chunk : 9 + chunk]
        weights = exp_terms[at] * fac
        live = jnp.where(mask_s[begin + i] == 1, 1.0, 0.0)
        score = (weights * (up[at] - mid) * (key_live * live)).astype(BF16)
        weight_out[at] = weights.astype(BF16)
        score_out[at] = score
        score = score.astype(F32)
        col_score += score
        row_score.append(jnp.sum(score, axis=1, keepdims=True))
    row_score = jnp.concatenate(row_score, axis=0)

    mask, is_vec = query_mask()
    is_vec = is_vec[0:1]
    rows = spread(query[...], mask)
    scores = score_out[...]
    weights = weight_out[...]
    grad_coef = -2.0 * LOGIT_WEIGHT * POINT_SCALE
    key_points = head_mask(QPTS, H * P_SIZE, P_SIZE, axis=0)
    coef = jnp.sum(key_points * head_row(head_weight, grad_coef, QPTS), axis=1, keepdims=True)
    raw = dot(rows.astype(BF16), scores, TN)
    key_grad[0:VEC] = SCALE_QK * raw[0:VEC]
    key_grad[VEC : 2 * VEC] = dot(
        spread(grad_single[...], head_mask(VEC, VEC, C)).astype(BF16), weights, TN
    )
    key_grad[2 * VEC : 2 * VEC + QPTS] = coef * (
        key_qk[VEC:QF].astype(F32) * dot(key_points, col_score, NN, HIGHEST) - raw[VEC:QF]
    )
    key_grad[2 * VEC + QPTS : KF] = dot(
        spread(grad_point[...], head_mask(VPTS, H * PV, PV)).astype(BF16), weights, TN
    )
    key_grad[KF:] = jnp.zeros((ROWS * FEATS - KF, KB), F32)
    key_single_grad[...] = two_part_dot(key_weight[...], key_grad[0:KF], NN)
    raw = dot(scores, key_qk[...], NT)
    head_coef = head_column(head_weight, grad_coef, QF)
    head_coef = jnp.concatenate([head_coef] * QB, axis=0)
    masks = jnp.concatenate([mask] * QB, axis=0)
    raw = jnp.where(is_vec, SCALE_QK * raw, head_coef * (rows * row_score - raw)) * masks
    query_grad = jnp.sum(raw.reshape(QB, HP, QF), axis=1)
    single = two_part_dot(query_weight[...], query_grad, NT, values_first=True)
    for k in range(3):
        single_out[QB * k : QB * (k + 1)] = single[:, 128 * k : 128 * (k + 1)]
    query_weight_grad[0:QF] = two_part_dot(query_single[...], query_grad, TN, values_first=True)
    query_weight_grad[QF:] = jnp.zeros((ROWS * 24 - QF, DS), F32)
    core = lax.rem(lax.axis_index("row"), 2)
    for out, parity in ((kept_out, core), (given_out, 1 - core)):
        for q in range(ROWS // 2):
            r = 2 * q + parity
            at = pl.ds(pl.multiple_of(FEATS * r, 8), FEATS)
            for k in range(2):
                out[q, FEATS * k : FEATS * (k + 1)] = key_grad[at, 128 * k : 128 * (k + 1)]
            at = pl.ds(pl.multiple_of(24 * r, 8), 24)
            for k in range(2):
                out[q, 112 + 24 * k : 136 + 24 * k] = key_single_grad[
                    at, 128 * k : 128 * (k + 1)
                ]
            for k in range(3):
                out[q, 160 + 24 * k : 184 + 24 * k] = query_weight_grad[
                    at, 128 * k : 128 * (k + 1)
                ]


def pair_kernel(pair_weight, pair, weights, scores, heads, pair_out, bias_out, lanes):
    step = pl.program_id(0)

    @pl.when(step == 0)
    def _():
        unit = jnp.where(
            lax.broadcasted_iota(jnp.int32, (HP, H), 0)
            == lax.broadcasted_iota(jnp.int32, (HP, H), 1),
            1.0,
            0.0,
        ).astype(BF16)
        values = LOGIT_WEIGHT * dot(unit, pair_weight[...], NT)
        high = values.astype(BF16)
        lanes[0:HP] = high
        lanes[HP:] = (values - high.astype(F32)).astype(BF16)
        bias_out[...] = jnp.zeros_like(bias_out)

    total = jnp.zeros((HP, DZ), F32)
    for i in range(STEP):
        at = slice(HP * i, HP * (i + 1))
        score = scores[at]
        left = jnp.concatenate([weights[at], score, score], axis=0)
        right = jnp.concatenate([heads[i], lanes[...]], axis=0)
        pair_out[i] = dot(left, right, TN).astype(BF16)
        total += dot(score, pair[i])
    bias_out[...] += LOGIT_WEIGHT * total


def whole(shape):
    return pl.BlockSpec(shape, lambda s: (0,) * len(shape))


def rows_of(*shape):
    return pl.BlockSpec(shape, lambda s: (s,) + (0,) * (len(shape) - 1))


SCALARS = pl.BlockSpec(memory_space=pltpu.SMEM)
VECTORS = pl.BlockSpec(memory_space=pltpu.VMEM)
PARAMS = pltpu.CompilerParams(
    dimension_semantics=("arbitrary",), vmem_limit_bytes=48 * 1024 * 1024
)


def scores_of(
    offsets, mask, chain, head_weight, chain_bias, query_single, key_single, query_weight,
    key_weight, pair_weight, pair, grad_single, grad_point, grad_pairs,
):
    return pl.pallas_call(
        score_kernel,
        grid=(STEPS,),
        out_shape=(
            jax.ShapeDtypeStruct((ALL, KB), F32),
            jax.ShapeDtypeStruct((ALL, KB), F32),
            jax.ShapeDtypeStruct((QF, KB), BF16),
            jax.ShapeDtypeStruct((QB, QF), BF16),
            jax.ShapeDtypeStruct((QB, HP, DZ), BF16),
            jax.ShapeDtypeStruct((3, 8, 128), F32),
        ),
        in_specs=[SCALARS] * 5
        + [
            whole((32, 128)),
            whole((32, 128)),
            rows_of(STEP, DS),
            whole((KB, DS)),
            whole((DS, QF)),
            whole((DS, KF)),
            whole((DZ, H)),
            rows_of(STEP, KB, DZ),
            rows_of(STEP, VEC),
            rows_of(STEP, VPTS),
            rows_of(STEP, H * DZ),
        ],
        out_specs=(
            rows_of(SLAB, KB),
            rows_of(SLAB, KB),
            whole((QF, KB)),
            rows_of(STEP, QF),
            rows_of(STEP, HP, DZ),
            whole((3, 8, 128)),
        ),
        scratch_shapes=[
            pltpu.VMEM((QF, KB), BF16),
            pltpu.VMEM((VEC + VPTS, KB), BF16),
            pltpu.VMEM((HP, KB), F32),
            pltpu.VMEM((HP, DZ), BF16),
            pltpu.VMEM((SLAB, 128), F32),
            pltpu.VMEM((STEP, HP, DZ), F32),
        ],
        compiler_params=PARAMS,
        cost_estimate=pl.CostEstimate(
            flops=2_000_000_000, bytes_accessed=8_000_000, transcendentals=262144
        ),
        name="row_scores",
    )(
        offsets, mask, chain, head_weight, chain_bias, mask.reshape(32, 128),
        chain.reshape(32, 128), query_single, key_single, query_weight, key_weight,
        pair_weight, pair, grad_single, grad_point, grad_pairs,
    )


def grads_of(
    offsets, mask, head_weight, parts, own, exp_terms, up, key_qk, query, query_single,
    query_weight, key_weight, grad_single, grad_point,
):
    return pl.pallas_call(
        grad_kernel,
        out_shape=(
            jax.ShapeDtypeStruct((ALL, KB), BF16),
            jax.ShapeDtypeStruct((ALL, KB), BF16),
            jax.ShapeDtypeStruct((ROWS // 2, SHARE, 128), F32),
            jax.ShapeDtypeStruct((ROWS // 2, SHARE, 128), F32),
            jax.ShapeDtypeStruct((3 * QB, 128), F32),
        ),
        in_specs=[SCALARS] * 3 + [VECTORS] * 12,
        out_specs=(VECTORS,) * 5,
        scratch_shapes=[
            pltpu.VMEM((ROWS * FEATS, KB), F32),
            pltpu.VMEM((DS, KB), F32),
            pltpu.VMEM((ROWS * 24, DS), F32),
        ],
        compiler_params=pltpu.CompilerParams(vmem_limit_bytes=48 * 1024 * 1024),
        cost_estimate=pl.CostEstimate(
            flops=3_000_000_000, bytes_accessed=8_000_000, transcendentals=20000
        ),
        name="feature_grads",
    )(
        offsets, mask, head_weight, mask.reshape(32, 128), parts, own, exp_terms, up, key_qk,
        query, query_single, query_weight, key_weight, grad_single, grad_point,
    )


def pair_grads_of(pair_weight, pair, weights, scores, heads):
    return pl.pallas_call(
        pair_kernel,
        grid=(STEPS,),
        out_shape=(
            jax.ShapeDtypeStruct((QB, KB, DZ), BF16),
            jax.ShapeDtypeStruct((HP, DZ), F32),
        ),
        in_specs=[
            whole((DZ, H)),
            rows_of(STEP, KB, DZ),
            rows_of(SLAB, KB),
            rows_of(SLAB, KB),
            rows_of(STEP, HP, DZ),
        ],
        out_specs=(rows_of(STEP, KB, DZ), whole((HP, DZ))),
        scratch_shapes=[pltpu.VMEM((2 * HP, DZ), BF16)],
        compiler_params=PARAMS,
        cost_estimate=pl.CostEstimate(
            flops=2_000_000_000, bytes_accessed=10_000_000, transcendentals=0
        ),
        name="pair_grads",
    )(pair_weight, pair, weights, scores, heads)


CHIPS = [[2 * i + core for i in range(ROWS // 2)] for core in range(2)]


def other_core(values):
    return lax.ppermute(values, "row", [(i, i ^ 1) for i in range(ROWS)])


def exchange(values, axis, groups=None):
    return lax.all_to_all(values, axis, 0, 0, axis_index_groups=groups)


def gather(values, axis, parts, groups=None):
    return exchange(jnp.broadcast_to(values[None], (parts, *values.shape)), axis, groups)


def gather_row(values):
    own = gather(values, "row", ROWS // 2, CHIPS)
    other = other_core(own)
    first = lax.axis_index("row") % 2 == 0
    return jnp.where(first, own, other), jnp.where(first, other, own)


def scatter_row(kept, given):
    return jnp.sum(exchange(kept + other_core(given), "row", CHIPS), axis=0)


def sum_col(values):
    share = jnp.sum(exchange(values.reshape(COLS, -1, values.shape[1]), "col"), axis=0)
    return gather(share, "col", COLS).reshape(values.shape)


def lanes_of(values):
    return [values[..., 128 * k : 128 * (k + 1)] for k in range(values.shape[-1] // 128)]


def joined(values, rows):
    return jnp.concatenate(
        [values[..., k : k + rows, :] for k in range(0, values.shape[-2], rows)], axis=-1
    )


def local(
    query_single,
    key_single,
    query_weight,
    key_weight,
    pair_weight,
    head_weight,
    chain_bias,
    pair,
    residue_mask,
    chain_index,
    strip_offsets,
    grad_single_out,
    grad_point_out,
    grad_pair_out,
):
    terms, up, key_qk, query, heads, own = scores_of(
        strip_offsets, residue_mask, chain_index, head_weight, chain_bias, query_single,
        key_single, query_weight, key_weight, pair_weight, pair, grad_single_out,
        grad_point_out, grad_pair_out,
    )
    with jax.named_scope("row_statistics"):
        parts = gather(own, "col", COLS)
    weights, scores, kept, given, query_single_part = grads_of(
        strip_offsets, residue_mask, head_weight, parts, own, terms, up, key_qk, query,
        query_single, query_weight, key_weight, grad_single_out, grad_point_out,
    )
    with jax.named_scope("row_sum"):
        summed = scatter_row(kept, given)
    grad_pair, bias_part = pair_grads_of(pair_weight, pair, weights, scores, heads)
    key_grad = joined(summed[: 2 * FEATS], FEATS)
    key_share = jnp.dot(key_grad, key_single.astype(F32), precision=HIGHEST)
    with jax.named_scope("col_sum"):
        share = jnp.concatenate(
            lanes_of(key_share)
            + [bias_part, summed[160:232], query_single_part]
            + [jnp.zeros((64, 128), F32)],
            axis=0,
        )
        share = sum_col(share)
    grad_query_single = joined(share[256:448], 64)
    with jax.named_scope("row_gather"):
        even, odd = gather_row(jnp.concatenate([share[:256], summed[112:160]], axis=0))
        full = jnp.stack([even, odd], axis=1).reshape(ROWS, 304, 128)
        grad_key_weight = joined(full[:, :168], FEATS).reshape(ROWS * FEATS, -1)[:KF].T
        grad_pair_weight = jnp.sum(full[:, 168 : 168 + H], axis=0).T
        grad_query_weight = joined(full[:, 184:256], 24).reshape(ROWS * 24, -1)[:QF].T
        grad_key_single = joined(full[:, 256:], 24).reshape(ROWS * 24, -1).T
    return (
        grad_query_single,
        grad_key_single,
        grad_query_weight,
        grad_key_weight,
        grad_pair_weight,
        grad_pair,
    )


def solution(mesh):
    in_specs = (
        P("row", None),
        P("col", None),
        P(),
        P(),
        P(),
        P(),
        P(),
        P("row", "col", None),
        P(),
        P(),
        P(),
        P("row", None),
        P("row", None),
        P("row", None),
    )
    out_specs = (P("row", None), P("col", None), P(), P(), P(), P("row", "col", None))
    return jax.shard_map(local, mesh=mesh, in_specs=in_specs, out_specs=out_specs, check_vma=False)
```

```python
import math

import jax
import jax.numpy as jnp
from jax import lax
from jax.experimental import pallas as pl
from jax.experimental.pallas import tpu as pltpu
from jax.sharding import PartitionSpec as P

H = 12
C = 16
P_SIZE = 4
PV = 8
DZ = 128
DS = 384
QB = 64
KB = 256
QF = 336
KF = 816
VEC = H * C
QPTS = 3 * H * P_SIZE
VPTS = 3 * H * PV
ROWS = 16
COLS = 16
HP = 16
STEP = 16
STEPS = QB // STEP
SLAB = STEP * HP
ALL = QB * HP
FEATS = 56
SHARE = 232

LOGIT_WEIGHT = math.sqrt(1.0 / 3.0)
MASKED_LOGIT = -100000.0
SCALE_QK = LOGIT_WEIGHT * C ** (-0.5)
POINT_SCALE = math.sqrt(2.0 / (9.0 * P_SIZE)) / 2.0
F32 = jnp.float32
BF16 = jnp.bfloat16
HIGHEST = lax.Precision.HIGHEST

NN = (((1,), (0,)), ((), ()))
NT = (((1,), (1,)), ((), ()))
TN = (((0,), (0,)), ((), ()))


def dot(a, b, dims=NN, precision=None):
    return lax.dot_general(a, b, dims, precision=precision, preferred_element_type=F32)


def two_part_dot(fixed, values, dims, values_first=False):
    high = values.astype(BF16)
    low = (values - high.astype(F32)).astype(BF16)
    if values_first:
        return dot(high, fixed, dims) + dot(low, fixed, dims)
    return dot(fixed, high, dims) + dot(fixed, low, dims)


def head_mask(count, group, size, offset=0, axis=1):
    shape = (HP, count) if axis == 1 else (count, HP)
    feature = lax.broadcasted_iota(jnp.int32, shape, axis)
    head = lax.broadcasted_iota(jnp.int32, shape, 1 - axis)
    return jnp.where(lax.div(lax.rem(feature, group), size) == head, 1.0, 0.0).astype(F32)


def query_mask():
    shape = (HP, QF)
    feature = lax.broadcasted_iota(jnp.int32, shape, 1)
    head = lax.broadcasted_iota(jnp.int32, shape, 0)
    of = jnp.where(
        feature < VEC,
        lax.div(feature, C),
        lax.div(lax.rem(jnp.maximum(feature - VEC, 0), H * P_SIZE), P_SIZE),
    )
    return jnp.where(of == head, 1.0, 0.0).astype(F32), feature < VEC


def spread(values, mask):
    rows, count = values.shape
    return (values.astype(F32)[:, None, :] * mask[None]).reshape(rows * HP, count)


def head_column(ref, scale, count):
    index = lax.broadcasted_iota(jnp.int32, (HP, count), 0)
    column = jnp.zeros((HP, count), F32)
    for h in range(H):
        column = jnp.where(index == h, ref[h] * scale, column)
    return column


def head_row(ref, scale, count):
    index = lax.broadcasted_iota(jnp.int32, (count, HP), 1)
    row = jnp.zeros((count, HP), F32)
    for h in range(H):
        row = jnp.where(index == h, ref[h] * scale, row)
    return row


def key_line(ref):
    begin = lax.axis_index("col") * 2
    return jnp.concatenate([ref[pl.ds(begin, 1), :], ref[pl.ds(begin + 1, 1), :]], axis=1)


def score_kernel(
    offsets,
    mask_s,
    chain_s,
    head_weight,
    chain_bias,
    mask_v,
    chain_v,
    query_single,
    key_single,
    query_weight,
    key_weight,
    pair_weight,
    pair,
    grad_single,
    grad_point,
    grad_pairs,
    exp_out,
    up_out,
    key_out,
    query_out,
    heads_out,
    stats_out,
    key_qk,
    key_v,
    key_norm,
    both,
    stat,
    spread_pairs,
):
    step = pl.program_id(0)

    @pl.when(step == 0)
    def _():
        feats = dot(key_weight[...], key_single[...], NT).astype(BF16)
        key_qk[0:VEC] = feats[0:VEC]
        key_qk[VEC:QF] = feats[2 * VEC : 2 * VEC + QPTS]
        key_v[0:VEC] = feats[VEC : 2 * VEC]
        key_v[VEC:] = feats[2 * VEC + QPTS :]
        key_out[...] = key_qk[...]
        points = feats[2 * VEC : 2 * VEC + QPTS].astype(F32)
        key_norm[...] = dot(
            head_mask(QPTS, H * P_SIZE, P_SIZE), points * points, NN, HIGHEST
        )
        unit = jnp.where(
            lax.broadcasted_iota(jnp.int32, (HP, H), 0)
            == lax.broadcasted_iota(jnp.int32, (HP, H), 1),
            1.0,
            0.0,
        ).astype(BF16)
        both[0:HP] = dot(unit, pair_weight[...]).astype(BF16)
        spread_pairs[...] = jnp.zeros_like(spread_pairs)
        stat[...] = jnp.zeros_like(stat)

    mask, is_vec = query_mask()
    query = dot(query_single[...], query_weight[...], NT).astype(BF16)
    query_out[...] = query
    rows = spread(query, mask)
    vec_rows = jnp.where(is_vec[0:1], rows, 0.0)
    point_rows = rows - vec_rows
    query_norm = jnp.sum(point_rows * point_rows, axis=1, keepdims=True)
    scalar = dot(vec_rows.astype(BF16), key_qk[...])
    cross = dot(point_rows.astype(BF16), key_qk[...])
    upstream = dot(spread(grad_single[...], head_mask(VEC, VEC, C)).astype(BF16), key_v[0:VEC])
    upstream += dot(
        spread(grad_point[...], head_mask(VPTS, H * PV, PV)).astype(BF16), key_v[VEC:]
    )
    pairs = grad_pairs[...].astype(F32)
    for h in range(H):
        spread_pairs[:, h, :] = pairs[:, DZ * h : DZ * (h + 1)]
    heads = spread_pairs[...].astype(BF16)
    heads_out[...] = heads

    point_coef = head_column(head_weight, POINT_SCALE, KB)
    bias = head_column(chain_bias, 1.0, KB)
    key_live = key_line(mask_v) == 1
    key_chain = key_line(chain_v)
    begin = offsets[lax.axis_index("row")] + step * STEP
    lane = lax.broadcasted_iota(jnp.int32, (HP, 128), 1)
    for i in range(STEP):
        at = slice(HP * i, HP * (i + 1))
        left = jnp.concatenate([both[0:HP], heads[i]], axis=0)
        tile = dot(left, pair[i], NT)
        distance = query_norm[at] + key_norm[...] - 2.0 * cross[at]
        logits = LOGIT_WEIGHT * (scalar[at] * C ** (-0.5) + tile[0:HP] - point_coef * distance)
        same = jnp.where(key_chain == chain_s[begin + i], 1.0, 0.0)
        logits = logits + bias * same
        live = jnp.where(key_live, mask_s[begin + i], 0) == 1
        logits = jnp.where(live, logits, MASKED_LOGIT)
        up = upstream[at] + tile[HP:]
        top = jnp.max(logits, axis=1, keepdims=True)
        terms = jnp.exp(logits - top)
        total = jnp.sum(terms, axis=1, keepdims=True)
        moment = jnp.sum(terms * up, axis=1, keepdims=True)
        exp_out[at] = terms
        up_out[at] = up
        stat[at] = jnp.where(lane == 0, top, jnp.where(lane == 1, total, moment))
    for half in range(2):
        turned = stat[128 * half : 128 * (half + 1)].T
        for k in range(3):
            stats_out[k, pl.ds(2 * step + half, 1), :] = turned[k : k + 1]


def grad_kernel(
    offsets,
    mask_s,
    head_weight,
    mask_v,
    parts,
    own,
    exp_terms,
    up,
    key_qk,
    query,
    query_single,
    query_weight,
    key_weight,
    grad_single,
    grad_point,
    weight_out,
    score_out,
    kept_out,
    given_out,
    single_out,
    key_grad,
    key_single_grad,
    query_weight_grad,
):
    row_top = parts[0, 0]
    for s in range(1, COLS):
        row_top = jnp.maximum(row_top, parts[s, 0])
    row_total = jnp.zeros_like(row_top)
    moment = jnp.zeros_like(row_top)
    for s in range(COLS):
        share = jnp.exp(parts[s, 0] - row_top)
        row_total += share * parts[s, 1]
        moment += share * parts[s, 2]
    factor = jnp.exp(own[0] - row_top) / row_total
    centre = moment / row_total
    columns = jnp.concatenate([factor, centre], axis=0).T
    key_live = jnp.where(key_line(mask_v) == 1, 1.0, 0.0)
    begin = offsets[lax.axis_index("row")]
    col_score = jnp.zeros((HP, KB), F32)
    row_score = []
    for i in range(QB):
        at = slice(HP * i, HP * (i + 1))
        chunk, off = i // 8, HP * (i % 8)
        fac = columns[off : off + HP, chunk : chunk + 1]
        mid = columns[off : off + HP, 8 + chunk : 9 + chunk]
        weights = exp_terms[at] * fac
        live = jnp.where(mask_s[begin + i] == 1, 1.0, 0.0)
        score = (weights * (up[at] - mid) * (key_live * live)).astype(BF16)
        weight_out[at] = weights.astype(BF16)
        score_out[at] = score
        score = score.astype(F32)
        col_score += score
        row_score.append(jnp.sum(score, axis=1, keepdims=True))
    row_score = jnp.concatenate(row_score, axis=0)

    mask, is_vec = query_mask()
    is_vec = is_vec[0:1]
    rows = spread(query[...], mask)
    scores = score_out[...]
    weights = weight_out[...]
    grad_coef = -2.0 * LOGIT_WEIGHT * POINT_SCALE
    key_points = head_mask(QPTS, H * P_SIZE, P_SIZE, axis=0)
    coef = jnp.sum(key_points * head_row(head_weight, grad_coef, QPTS), axis=1, keepdims=True)
    raw = dot(rows.astype(BF16), scores, TN)
    key_grad[0:VEC] = SCALE_QK * raw[0:VEC]
    key_grad[VEC : 2 * VEC] = dot(
        spread(grad_single[...], head_mask(VEC, VEC, C)).astype(BF16), weights, TN
    )
    key_grad[2 * VEC : 2 * VEC + QPTS] = coef * (
        key_qk[VEC:QF].astype(F32) * dot(key_points, col_score, NN, HIGHEST) - raw[VEC:QF]
    )
    key_grad[2 * VEC + QPTS : KF] = dot(
        spread(grad_point[...], head_mask(VPTS, H * PV, PV)).astype(BF16), weights, TN
    )
    key_grad[KF:] = jnp.zeros((ROWS * FEATS - KF, KB), F32)
    key_single_grad[...] = two_part_dot(key_weight[...], key_grad[0:KF], TN, values_first=True)
    raw = dot(scores, key_qk[...], NT)
    head_coef = head_column(head_weight, grad_coef, QF)
    head_coef = jnp.concatenate([head_coef] * QB, axis=0)
    masks = jnp.concatenate([mask] * QB, axis=0)
    raw = jnp.where(is_vec, SCALE_QK * raw, head_coef * (rows * row_score - raw)) * masks
    query_grad = jnp.sum(raw.reshape(QB, HP, QF), axis=1)
    single = two_part_dot(query_weight[...], query_grad, NN, values_first=True)
    for k in range(3):
        single_out[QB * k : QB * (k + 1)] = single[:, 128 * k : 128 * (k + 1)]
    query_weight_grad[0:QF] = two_part_dot(query_single[...], query_grad, TN, values_first=True)
    query_weight_grad[QF:] = jnp.zeros((ROWS * 24 - QF, DS), F32)
    core = lax.rem(lax.axis_index("row"), 2)
    for out, parity in ((kept_out, core), (given_out, 1 - core)):
        for q in range(ROWS // 2):
            r = 2 * q + parity
            at = pl.ds(pl.multiple_of(FEATS * r, 8), FEATS)
            for k in range(2):
                out[q, FEATS * k : FEATS * (k + 1)] = key_grad[at, 128 * k : 128 * (k + 1)]
            at = pl.ds(pl.multiple_of(16 * r, 8), 16)
            for k in range(3):
                out[q, 112 + 16 * k : 128 + 16 * k] = key_single_grad[
                    at, 128 * k : 128 * (k + 1)
                ]
            at = pl.ds(pl.multiple_of(24 * r, 8), 24)
            for k in range(3):
                out[q, 160 + 24 * k : 184 + 24 * k] = query_weight_grad[
                    at, 128 * k : 128 * (k + 1)
                ]


def pair_kernel(pair_weight, pair, weights, scores, heads, pair_out, bias_out, lanes):
    step = pl.program_id(0)

    @pl.when(step == 0)
    def _():
        unit = jnp.where(
            lax.broadcasted_iota(jnp.int32, (HP, H), 0)
            == lax.broadcasted_iota(jnp.int32, (HP, H), 1),
            1.0,
            0.0,
        ).astype(BF16)
        values = LOGIT_WEIGHT * dot(unit, pair_weight[...])
        high = values.astype(BF16)
        lanes[0:HP] = high
        lanes[HP:] = (values - high.astype(F32)).astype(BF16)
        bias_out[...] = jnp.zeros_like(bias_out)

    total = jnp.zeros((HP, DZ), F32)
    for i in range(STEP):
        at = slice(HP * i, HP * (i + 1))
        score = scores[at]
        left = jnp.concatenate([weights[at], score, score], axis=0)
        right = jnp.concatenate([heads[i], lanes[...]], axis=0)
        pair_out[i] = dot(left, right, TN).astype(BF16)
        total += dot(score, pair[i])
    bias_out[...] += LOGIT_WEIGHT * total


def assemble_kernel(own, other, share, key_out, query_out, single_out, query_single_out, pair_out):
    first = lax.rem(lax.axis_index("row"), 2) == 0
    lane = pl.program_id(0)

    def chunk(r, begin, count):
        at = pl.ds(pl.multiple_of(begin, 8), count)
        mine, theirs = own[r // 2, at], other[r // 2, at]
        if r % 2 == 1:
            mine, theirs = theirs, mine
        return jnp.where(first, mine, theirs)

    for r in range(ROWS):
        count = min(FEATS, KF - FEATS * r)
        if count > 0:
            key_out[FEATS * r : FEATS * r + count] = chunk(r, FEATS * lane, count)
        if r < QF // 24:
            query_out[24 * r : 24 * (r + 1)] = chunk(r, 184 + 24 * lane, 24)
        single_out[16 * r : 16 * (r + 1)] = chunk(r, 256 + 16 * lane, 16)
    query_single_out[...] = share[pl.ds(pl.multiple_of(256 + QB * lane, 8), QB)]

    @pl.when(lane == 0)
    def _():
        total = chunk(0, 168, 16)
        for r in range(1, ROWS):
            total += chunk(r, 168, 16)
        pair_out[...] = total[0:H]


def assembled(own, other, share):
    lanes = lambda rows: pl.BlockSpec((rows, 128), lambda k: (0, k))
    return pl.pallas_call(
        assemble_kernel,
        grid=(3,),
        out_shape=(
            jax.ShapeDtypeStruct((KF, DS), F32),
            jax.ShapeDtypeStruct((QF, DS), F32),
            jax.ShapeDtypeStruct((KB, DS), F32),
            jax.ShapeDtypeStruct((QB, DS), F32),
            jax.ShapeDtypeStruct((H, DZ), F32),
        ),
        in_specs=[VECTORS] * 3,
        out_specs=(lanes(KF), lanes(QF), lanes(KB), lanes(QB), whole((H, DZ))),
        compiler_params=PARAMS,
        name="assemble",
    )(own, other, share)


def whole(shape):
    return pl.BlockSpec(shape, lambda s: (0,) * len(shape))


def rows_of(*shape):
    return pl.BlockSpec(shape, lambda s: (s,) + (0,) * (len(shape) - 1))


SCALARS = pl.BlockSpec(memory_space=pltpu.SMEM)
VECTORS = pl.BlockSpec(memory_space=pltpu.VMEM)
MIB = 1024 * 1024
PARAMS = pltpu.CompilerParams(dimension_semantics=("arbitrary",), vmem_limit_bytes=48 * MIB)


def scores_of(
    offsets, mask, chain, head_weight, chain_bias, query_single, key_single, query_weight,
    key_weight, pair_weight, pair, grad_single, grad_point, grad_pairs,
):
    return pl.pallas_call(
        score_kernel,
        grid=(STEPS,),
        out_shape=(
            jax.ShapeDtypeStruct((ALL, KB), F32),
            jax.ShapeDtypeStruct((ALL, KB), F32),
            jax.ShapeDtypeStruct((QF, KB), BF16),
            jax.ShapeDtypeStruct((QB, QF), BF16),
            jax.ShapeDtypeStruct((QB, HP, DZ), BF16),
            jax.ShapeDtypeStruct((3, 8, 128), F32),
        ),
        in_specs=[SCALARS] * 5
        + [
            whole((32, 128)),
            whole((32, 128)),
            rows_of(STEP, DS),
            whole((KB, DS)),
            whole((QF, DS)),
            whole((KF, DS)),
            whole((H, DZ)),
            rows_of(STEP, KB, DZ),
            rows_of(STEP, VEC),
            rows_of(STEP, VPTS),
            rows_of(STEP, H * DZ),
        ],
        out_specs=(
            rows_of(SLAB, KB),
            rows_of(SLAB, KB),
            whole((QF, KB)),
            rows_of(STEP, QF),
            rows_of(STEP, HP, DZ),
            whole((3, 8, 128)),
        ),
        scratch_shapes=[
            pltpu.VMEM((QF, KB), BF16),
            pltpu.VMEM((VEC + VPTS, KB), BF16),
            pltpu.VMEM((HP, KB), F32),
            pltpu.VMEM((HP, DZ), BF16),
            pltpu.VMEM((SLAB, 128), F32),
            pltpu.VMEM((STEP, HP, DZ), F32),
        ],
        compiler_params=PARAMS,
        cost_estimate=pl.CostEstimate(
            flops=2_000_000_000, bytes_accessed=8_000_000, transcendentals=262144
        ),
        name="row_scores",
    )(
        offsets, mask, chain, head_weight, chain_bias, mask.reshape(32, 128),
        chain.reshape(32, 128), query_single, key_single, query_weight, key_weight,
        pair_weight, pair, grad_single, grad_point, grad_pairs,
    )


def grads_of(
    offsets, mask, head_weight, parts, own, exp_terms, up, key_qk, query, query_single,
    query_weight, key_weight, grad_single, grad_point,
):
    return pl.pallas_call(
        grad_kernel,
        out_shape=(
            jax.ShapeDtypeStruct((ALL, KB), BF16),
            jax.ShapeDtypeStruct((ALL, KB), BF16),
            jax.ShapeDtypeStruct((ROWS // 2, SHARE, 128), F32),
            jax.ShapeDtypeStruct((ROWS // 2, SHARE, 128), F32),
            jax.ShapeDtypeStruct((3 * QB, 128), F32),
        ),
        in_specs=[SCALARS] * 3 + [VECTORS] * 12,
        out_specs=(VECTORS,) * 5,
        scratch_shapes=[
            pltpu.VMEM((ROWS * FEATS, KB), F32),
            pltpu.VMEM((KB, DS), F32),
            pltpu.VMEM((ROWS * 24, DS), F32),
        ],
        compiler_params=pltpu.CompilerParams(vmem_limit_bytes=24 * MIB),
        cost_estimate=pl.CostEstimate(
            flops=3_000_000_000, bytes_accessed=8_000_000, transcendentals=20000
        ),
        name="feature_grads",
    )(
        offsets, mask, head_weight, mask.reshape(32, 128), parts, own, exp_terms, up, key_qk,
        query, query_single, query_weight, key_weight, grad_single, grad_point,
    )


def pair_grads_of(pair_weight, pair, weights, scores, heads):
    return pl.pallas_call(
        pair_kernel,
        grid=(STEPS,),
        out_shape=(
            jax.ShapeDtypeStruct((QB, KB, DZ), BF16),
            jax.ShapeDtypeStruct((HP, DZ), F32),
        ),
        in_specs=[
            whole((H, DZ)),
            rows_of(STEP, KB, DZ),
            rows_of(SLAB, KB),
            rows_of(SLAB, KB),
            rows_of(STEP, HP, DZ),
        ],
        out_specs=(rows_of(STEP, KB, DZ), whole((HP, DZ))),
        scratch_shapes=[pltpu.VMEM((2 * HP, DZ), BF16)],
        compiler_params=PARAMS,
        cost_estimate=pl.CostEstimate(
            flops=2_000_000_000, bytes_accessed=10_000_000, transcendentals=0
        ),
        name="pair_grads",
    )(pair_weight, pair, weights, scores, heads)


CHIPS = [[2 * i + core for i in range(ROWS // 2)] for core in range(2)]


ALONG_X = [[4 * x + z for x in range(4)] for z in range(4)]
ALONG_Z = [[4 * x + z for z in range(4)] for x in range(4)]


def other_core(values):
    return lax.ppermute(values, "row", [(i, i ^ 1) for i in range(ROWS)])


def exchange(values, axis, groups=None):
    return lax.all_to_all(values, axis, 0, 0, axis_index_groups=groups)


def gather(values, axis, parts, groups=None):
    return exchange(jnp.broadcast_to(values[None], (parts, *values.shape)), axis, groups)


def scatter_row(kept, given):
    return jnp.sum(exchange(kept + other_core(given), "row", CHIPS), axis=0)


def sum_col(values):
    share = exchange(values.reshape(4, -1, values.shape[1]), "col", ALONG_X)
    share = jnp.sum(share, axis=0)
    share = jnp.sum(gather(share, "col", 4, ALONG_Z), axis=0)
    return gather(share, "col", 4, ALONG_X).reshape(values.shape)


def lanes_of(values):
    return [values[..., 128 * k : 128 * (k + 1)] for k in range(values.shape[-1] // 128)]


def joined(values, rows):
    return jnp.concatenate(
        [values[..., k : k + rows, :] for k in range(0, values.shape[-2], rows)], axis=-1
    )


def local(
    query_single,
    key_single,
    query_weight,
    key_weight,
    pair_weight,
    head_weight,
    chain_bias,
    pair,
    residue_mask,
    chain_index,
    strip_offsets,
    grad_single_out,
    grad_point_out,
    grad_pair_out,
):
    query_weight, key_weight, pair_weight = query_weight.T, key_weight.T, pair_weight.T
    terms, up, key_qk, query, heads, own = scores_of(
        strip_offsets, residue_mask, chain_index, head_weight, chain_bias, query_single,
        key_single, query_weight, key_weight, pair_weight, pair, grad_single_out,
        grad_point_out, grad_pair_out,
    )
    with jax.named_scope("row_statistics"):
        parts = gather(own, "col", COLS)
    weights, scores, kept, given, query_single_part = grads_of(
        strip_offsets, residue_mask, head_weight, parts, own, terms, up, key_qk, query,
        query_single, query_weight, key_weight, grad_single_out, grad_point_out,
    )
    with jax.named_scope("row_sum"):
        summed = scatter_row(kept, given)
    grad_pair, bias_part = pair_grads_of(pair_weight, pair, weights, scores, heads)
    key_grad = joined(summed[: 2 * FEATS], FEATS)
    key_share = jnp.dot(key_grad, key_single.astype(F32), precision=HIGHEST)
    with jax.named_scope("col_sum"):
        share = jnp.concatenate(
            lanes_of(key_share) + [bias_part, summed[160:232], query_single_part], axis=0
        )
        share = sum_col(share)
    with jax.named_scope("row_gather"):
        own = jnp.concatenate([share[:256], summed[112:160]], axis=0)
        own = gather(own, "row", ROWS // 2, CHIPS)
        results = assembled(own, other_core(own), share)
    key_weight_grad, query_weight_grad, key_single_grad, query_single_grad, pair_weight_grad = results
    return (
        query_single_grad,
        key_single_grad,
        query_weight_grad.T,
        key_weight_grad.T,
        pair_weight_grad.T,
        grad_pair,
    )


def solution(mesh):
    in_specs = (
        P("row", None),
        P("col", None),
        P(),
        P(),
        P(),
        P(),
        P(),
        P("row", "col", None),
        P(),
        P(),
        P(),
        P("row", None),
        P("row", None),
        P("row", None),
    )
    out_specs = (P("row", None), P("col", None), P(), P(), P(), P("row", "col", None))
    return jax.shard_map(local, mesh=mesh, in_specs=in_specs, out_specs=out_specs, check_vma=False)
```

```python
import math

import jax
import jax.numpy as jnp
from jax import lax
from jax.experimental import pallas as pl
from jax.experimental.pallas import tpu as pltpu
from jax.sharding import PartitionSpec as P

H = 12
C = 16
P_SIZE = 4
PV = 8
DZ = 128
DS = 384
QB = 64
KB = 256
QF = 336
KF = 816
VEC = H * C
QPTS = 3 * H * P_SIZE
VPTS = 3 * H * PV
ROWS = 16
COLS = 16
HP = 16
STEP = 16
STEPS = QB // STEP
SLAB = STEP * HP
ALL = QB * HP
FEATS = 56
SHARE = 232

LOGIT_WEIGHT = math.sqrt(1.0 / 3.0)
MASKED_LOGIT = -100000.0
SCALE_QK = LOGIT_WEIGHT * C ** (-0.5)
POINT_SCALE = math.sqrt(2.0 / (9.0 * P_SIZE)) / 2.0
F32 = jnp.float32
BF16 = jnp.bfloat16
HIGHEST = lax.Precision.HIGHEST

NN = (((1,), (0,)), ((), ()))
NT = (((1,), (1,)), ((), ()))
TN = (((0,), (0,)), ((), ()))


def dot(a, b, dims=NN, precision=None):
    return lax.dot_general(a, b, dims, precision=precision, preferred_element_type=F32)


def two_part_dot(fixed, values, dims, values_first=False):
    high = values.astype(BF16)
    low = (values - high.astype(F32)).astype(BF16)
    if values_first:
        return dot(high, fixed, dims) + dot(low, fixed, dims)
    return dot(fixed, high, dims) + dot(fixed, low, dims)


def head_mask(count, group, size, offset=0, axis=1):
    shape = (HP, count) if axis == 1 else (count, HP)
    feature = lax.broadcasted_iota(jnp.int32, shape, axis)
    head = lax.broadcasted_iota(jnp.int32, shape, 1 - axis)
    return jnp.where(lax.div(lax.rem(feature, group), size) == head, 1.0, 0.0).astype(F32)


def query_mask():
    shape = (HP, QF)
    feature = lax.broadcasted_iota(jnp.int32, shape, 1)
    head = lax.broadcasted_iota(jnp.int32, shape, 0)
    of = jnp.where(
        feature < VEC,
        lax.div(feature, C),
        lax.div(lax.rem(jnp.maximum(feature - VEC, 0), H * P_SIZE), P_SIZE),
    )
    return jnp.where(of == head, 1.0, 0.0).astype(F32), feature < VEC


def spread(values, mask):
    rows, count = values.shape
    return (values.astype(F32)[:, None, :] * mask[None]).reshape(rows * HP, count)


def head_column(ref, scale, count):
    index = lax.broadcasted_iota(jnp.int32, (HP, count), 0)
    column = jnp.zeros((HP, count), F32)
    for h in range(H):
        column = jnp.where(index == h, ref[h] * scale, column)
    return column


def head_row(ref, scale, count):
    index = lax.broadcasted_iota(jnp.int32, (count, HP), 1)
    row = jnp.zeros((count, HP), F32)
    for h in range(H):
        row = jnp.where(index == h, ref[h] * scale, row)
    return row


def key_line(ref):
    begin = lax.axis_index("col") * 2
    return jnp.concatenate([ref[pl.ds(begin, 1), :], ref[pl.ds(begin + 1, 1), :]], axis=1)


def score_kernel(
    offsets,
    mask_s,
    chain_s,
    head_weight,
    chain_bias,
    mask_v,
    chain_v,
    query_single,
    key_single,
    query_weight,
    key_weight,
    pair_weight,
    pair,
    grad_single,
    grad_point,
    grad_pairs,
    exp_out,
    up_out,
    key_out,
    query_out,
    heads_out,
    stats_out,
    key_qk,
    key_v,
    key_norm,
    both,
    stat,
    spread_pairs,
):
    step = pl.program_id(0)

    @pl.when(step == 0)
    def _():
        feats = dot(key_weight[...], key_single[...], NT).astype(BF16)
        key_qk[0:VEC] = feats[0:VEC]
        key_qk[VEC:QF] = feats[2 * VEC : 2 * VEC + QPTS]
        key_v[0:VEC] = feats[VEC : 2 * VEC]
        key_v[VEC:] = feats[2 * VEC + QPTS :]
        key_out[...] = key_qk[...]
        points = feats[2 * VEC : 2 * VEC + QPTS].astype(F32)
        key_norm[...] = dot(
            head_mask(QPTS, H * P_SIZE, P_SIZE), points * points, NN, HIGHEST
        )
        unit = jnp.where(
            lax.broadcasted_iota(jnp.int32, (HP, H), 0)
            == lax.broadcasted_iota(jnp.int32, (HP, H), 1),
            1.0,
            0.0,
        ).astype(BF16)
        both[0:HP] = dot(unit, pair_weight[...]).astype(BF16)
        spread_pairs[...] = jnp.zeros_like(spread_pairs)
        stat[...] = jnp.zeros_like(stat)

    mask, is_vec = query_mask()
    query = dot(query_single[...], query_weight[...], NT).astype(BF16)
    query_out[...] = query
    rows = spread(query, mask)
    vec_rows = jnp.where(is_vec[0:1], rows, 0.0)
    point_rows = rows - vec_rows
    query_norm = jnp.sum(point_rows * point_rows, axis=1, keepdims=True)
    scalar = dot(vec_rows.astype(BF16), key_qk[...])
    cross = dot(point_rows.astype(BF16), key_qk[...])
    upstream = dot(spread(grad_single[...], head_mask(VEC, VEC, C)).astype(BF16), key_v[0:VEC])
    upstream += dot(
        spread(grad_point[...], head_mask(VPTS, H * PV, PV)).astype(BF16), key_v[VEC:]
    )
    pairs = grad_pairs[...].astype(F32)
    for h in range(H):
        spread_pairs[:, h, :] = pairs[:, DZ * h : DZ * (h + 1)]
    heads = spread_pairs[...].astype(BF16)
    heads_out[...] = heads

    point_coef = head_column(head_weight, POINT_SCALE, KB)
    bias = head_column(chain_bias, 1.0, KB)
    key_live = key_line(mask_v) == 1
    key_chain = key_line(chain_v)
    begin = offsets[lax.axis_index("row")] + step * STEP
    lane = lax.broadcasted_iota(jnp.int32, (HP, 128), 1)
    for i in range(STEP):
        at = slice(HP * i, HP * (i + 1))
        left = jnp.concatenate([both[0:HP], heads[i]], axis=0)
        tile = dot(left, pair[i], NT)
        distance = query_norm[at] + key_norm[...] - 2.0 * cross[at]
        logits = LOGIT_WEIGHT * (scalar[at] * C ** (-0.5) + tile[0:HP] - point_coef * distance)
        same = jnp.where(key_chain == chain_s[begin + i], 1.0, 0.0)
        logits = logits + bias * same
        live = jnp.where(key_live, mask_s[begin + i], 0) == 1
        logits = jnp.where(live, logits, MASKED_LOGIT)
        up = upstream[at] + tile[HP:]
        top = jnp.max(logits, axis=1, keepdims=True)
        terms = jnp.exp(logits - top)
        total = jnp.sum(terms, axis=1, keepdims=True)
        moment = jnp.sum(terms * up, axis=1, keepdims=True)
        exp_out[at] = terms
        up_out[at] = up
        stat[at] = jnp.where(lane == 0, top, jnp.where(lane == 1, total, moment))
    for half in range(2):
        turned = stat[128 * half : 128 * (half + 1)].T
        for k in range(3):
            stats_out[k, pl.ds(2 * step + half, 1), :] = turned[k : k + 1]


def spread_kernel(query, grad_single, grad_point, out):
    column = lax.broadcasted_iota(jnp.int32, (QB, ALL), 1)
    row = lax.broadcasted_iota(jnp.int32, (QB, ALL), 0)
    copies = jnp.where(lax.div(column, HP) == row, 1.0, 0.0).astype(BF16)

    def put(begin, values, group, size):
        count = values.shape[1]
        feature = lax.broadcasted_iota(jnp.int32, (count, ALL), 0)
        head = lax.rem(lax.broadcasted_iota(jnp.int32, (count, ALL), 1), HP)
        of = lax.div(lax.rem(feature, group), size)
        out[begin : begin + count] = jnp.where(
            of == head, dot(values, copies, TN), 0.0
        ).astype(BF16)

    put(0, query[:, 0:VEC], VEC, C)
    put(VEC, query[:, VEC:], H * P_SIZE, P_SIZE)
    put(QF, grad_single[...], VEC, C)
    put(QF + VEC, grad_point[...], H * PV, PV)


def grad_kernel(
    offsets,
    mask_s,
    head_weight,
    mask_v,
    parts,
    own,
    exp_terms,
    up,
    key_qk,
    query,
    query_single,
    query_weight,
    key_weight,
    columns_of,
    weight_out,
    score_out,
    kept_out,
    given_out,
    single_out,
    key_grad,
    key_single_grad,
    query_weight_grad,
):
    row_top = parts[0, 0]
    for s in range(1, COLS):
        row_top = jnp.maximum(row_top, parts[s, 0])
    row_total = jnp.zeros_like(row_top)
    moment = jnp.zeros_like(row_top)
    for s in range(COLS):
        share = jnp.exp(parts[s, 0] - row_top)
        row_total += share * parts[s, 1]
        moment += share * parts[s, 2]
    factor = jnp.exp(own[0] - row_top) / row_total
    centre = moment / row_total
    columns = jnp.concatenate([factor, centre], axis=0).T
    key_live = jnp.where(key_line(mask_v) == 1, 1.0, 0.0)
    begin = offsets[lax.axis_index("row")]
    col_score = jnp.zeros((HP, KB), F32)
    row_score = []
    for i in range(QB):
        at = slice(HP * i, HP * (i + 1))
        chunk, off = i // 8, HP * (i % 8)
        fac = columns[off : off + HP, chunk : chunk + 1]
        mid = columns[off : off + HP, 8 + chunk : 9 + chunk]
        weights = exp_terms[at] * fac
        live = jnp.where(mask_s[begin + i] == 1, 1.0, 0.0)
        score = (weights * (up[at] - mid) * (key_live * live)).astype(BF16)
        weight_out[at] = weights.astype(BF16)
        score_out[at] = score
        score = score.astype(F32)
        col_score += score
        row_score.append(jnp.sum(score, axis=1, keepdims=True))
    row_score = jnp.concatenate(row_score, axis=0)

    mask, is_vec = query_mask()
    is_vec = is_vec[0:1]
    rows = spread(query[...], mask)
    scores = score_out[...]
    weights = weight_out[...]
    grad_coef = -2.0 * LOGIT_WEIGHT * POINT_SCALE
    key_points = head_mask(QPTS, H * P_SIZE, P_SIZE, axis=0)
    coef = jnp.sum(key_points * head_row(head_weight, grad_coef, QPTS), axis=1, keepdims=True)
    raw = dot(columns_of[0:QF], scores)
    key_grad[0:VEC] = SCALE_QK * raw[0:VEC]
    key_grad[VEC : 2 * VEC] = dot(columns_of[QF : QF + VEC], weights)
    key_grad[2 * VEC : 2 * VEC + QPTS] = coef * (
        key_qk[VEC:QF].astype(F32) * dot(key_points, col_score, NN, HIGHEST) - raw[VEC:QF]
    )
    key_grad[2 * VEC + QPTS : KF] = dot(columns_of[QF + VEC :], weights)
    key_grad[KF:] = jnp.zeros((ROWS * FEATS - KF, KB), F32)
    key_single_grad[...] = two_part_dot(key_weight[...], key_grad[0:KF], TN, values_first=True)
    raw = dot(scores, key_qk[...], NT)
    head_coef = head_column(head_weight, grad_coef, QF)
    head_coef = jnp.concatenate([head_coef] * QB, axis=0)
    masks = jnp.concatenate([mask] * QB, axis=0)
    raw = jnp.where(is_vec, SCALE_QK * raw, head_coef * (rows * row_score - raw)) * masks
    query_grad = jnp.sum(raw.reshape(QB, HP, QF), axis=1)
    single = two_part_dot(query_weight[...], query_grad, NN, values_first=True)
    for k in range(3):
        single_out[QB * k : QB * (k + 1)] = single[:, 128 * k : 128 * (k + 1)]
    query_weight_grad[0:QF] = two_part_dot(query_single[...], query_grad, TN, values_first=True)
    query_weight_grad[QF:] = jnp.zeros((ROWS * 24 - QF, DS), F32)
    core = lax.rem(lax.axis_index("row"), 2)
    for out, parity in ((kept_out, core), (given_out, 1 - core)):
        for q in range(ROWS // 2):
            r = 2 * q + parity
            at = pl.ds(pl.multiple_of(FEATS * r, 8), FEATS)
            for k in range(2):
                out[q, FEATS * k : FEATS * (k + 1)] = key_grad[at, 128 * k : 128 * (k + 1)]
            at = pl.ds(pl.multiple_of(16 * r, 8), 16)
            for k in range(3):
                out[q, 112 + 16 * k : 128 + 16 * k] = key_single_grad[
                    at, 128 * k : 128 * (k + 1)
                ]
            at = pl.ds(pl.multiple_of(24 * r, 8), 24)
            for k in range(3):
                out[q, 160 + 24 * k : 184 + 24 * k] = query_weight_grad[
                    at, 128 * k : 128 * (k + 1)
                ]


def pair_kernel(pair_weight, pair, weights, scores, heads, pair_out, bias_out, lanes):
    step = pl.program_id(0)

    @pl.when(step == 0)
    def _():
        unit = jnp.where(
            lax.broadcasted_iota(jnp.int32, (HP, H), 0)
            == lax.broadcasted_iota(jnp.int32, (HP, H), 1),
            1.0,
            0.0,
        ).astype(BF16)
        values = LOGIT_WEIGHT * dot(unit, pair_weight[...])
        high = values.astype(BF16)
        lanes[0:HP] = high
        lanes[HP:] = (values - high.astype(F32)).astype(BF16)
        bias_out[...] = jnp.zeros_like(bias_out)

    total = jnp.zeros((HP, DZ), F32)
    for i in range(STEP):
        at = slice(HP * i, HP * (i + 1))
        score = scores[at]
        left = jnp.concatenate([weights[at], score, score], axis=0)
        right = jnp.concatenate([heads[i], lanes[...]], axis=0)
        pair_out[i] = dot(left, right, TN).astype(BF16)
        total += dot(score, pair[i])
    bias_out[...] += LOGIT_WEIGHT * total


def assemble_kernel(own, other, share, key_out, query_out, single_out, query_single_out, pair_out):
    first = lax.rem(lax.axis_index("row"), 2) == 0
    lane = pl.program_id(0)

    def chunk(r, begin, count):
        at = pl.ds(pl.multiple_of(begin, 8), count)
        mine, theirs = own[r // 2, at], other[r // 2, at]
        if r % 2 == 1:
            mine, theirs = theirs, mine
        return jnp.where(first, mine, theirs)

    for r in range(ROWS):
        count = min(FEATS, KF - FEATS * r)
        if count > 0:
            key_out[FEATS * r : FEATS * r + count] = chunk(r, FEATS * lane, count)
        if r < QF // 24:
            query_out[24 * r : 24 * (r + 1)] = chunk(r, 184 + 24 * lane, 24)
        single_out[16 * r : 16 * (r + 1)] = chunk(r, 256 + 16 * lane, 16)
    query_single_out[...] = share[pl.ds(pl.multiple_of(256 + QB * lane, 8), QB)]

    @pl.when(lane == 0)
    def _():
        total = chunk(0, 168, 16)
        for r in range(1, ROWS):
            total += chunk(r, 168, 16)
        pair_out[...] = total[0:H]


def assembled(own, other, share):
    lanes = lambda rows: pl.BlockSpec((rows, 128), lambda k: (0, k))
    return pl.pallas_call(
        assemble_kernel,
        grid=(3,),
        out_shape=(
            jax.ShapeDtypeStruct((KF, DS), F32),
            jax.ShapeDtypeStruct((QF, DS), F32),
            jax.ShapeDtypeStruct((KB, DS), F32),
            jax.ShapeDtypeStruct((QB, DS), F32),
            jax.ShapeDtypeStruct((H, DZ), F32),
        ),
        in_specs=[VECTORS] * 3,
        out_specs=(lanes(KF), lanes(QF), lanes(KB), lanes(QB), whole((H, DZ))),
        compiler_params=limit(16),
        name="assemble",
    )(own, other, share)


def whole(shape):
    return pl.BlockSpec(shape, lambda s: (0,) * len(shape))


def rows_of(*shape):
    return pl.BlockSpec(shape, lambda s: (s,) + (0,) * (len(shape) - 1))


SCALARS = pl.BlockSpec(memory_space=pltpu.SMEM)
VECTORS = pl.BlockSpec(memory_space=pltpu.VMEM)
MIB = 1024 * 1024


def limit(mib):
    return pltpu.CompilerParams(vmem_limit_bytes=mib * MIB)


def scores_of(
    offsets, mask, chain, head_weight, chain_bias, query_single, key_single, query_weight,
    key_weight, pair_weight, pair, grad_single, grad_point, grad_pairs,
):
    return pl.pallas_call(
        score_kernel,
        grid=(STEPS,),
        out_shape=(
            jax.ShapeDtypeStruct((ALL, KB), F32),
            jax.ShapeDtypeStruct((ALL, KB), F32),
            jax.ShapeDtypeStruct((QF, KB), BF16),
            jax.ShapeDtypeStruct((QB, QF), BF16),
            jax.ShapeDtypeStruct((QB, HP, DZ), BF16),
            jax.ShapeDtypeStruct((3, 8, 128), F32),
        ),
        in_specs=[SCALARS] * 5
        + [
            whole((32, 128)),
            whole((32, 128)),
            rows_of(STEP, DS),
            whole((KB, DS)),
            whole((QF, DS)),
            whole((KF, DS)),
            whole((H, DZ)),
            rows_of(STEP, KB, DZ),
            rows_of(STEP, VEC),
            rows_of(STEP, VPTS),
            rows_of(STEP, H * DZ),
        ],
        out_specs=(
            rows_of(SLAB, KB),
            rows_of(SLAB, KB),
            whole((QF, KB)),
            rows_of(STEP, QF),
            rows_of(STEP, HP, DZ),
            whole((3, 8, 128)),
        ),
        scratch_shapes=[
            pltpu.VMEM((QF, KB), BF16),
            pltpu.VMEM((VEC + VPTS, KB), BF16),
            pltpu.VMEM((HP, KB), F32),
            pltpu.VMEM((HP, DZ), BF16),
            pltpu.VMEM((SLAB, 128), F32),
            pltpu.VMEM((STEP, HP, DZ), F32),
        ],
        compiler_params=limit(60),
        cost_estimate=pl.CostEstimate(
            flops=2_000_000_000, bytes_accessed=8_000_000, transcendentals=262144
        ),
        name="row_scores",
    )(
        offsets, mask, chain, head_weight, chain_bias, mask.reshape(32, 128),
        chain.reshape(32, 128), query_single, key_single, query_weight, key_weight,
        pair_weight, pair, grad_single, grad_point, grad_pairs,
    )


def grads_of(
    offsets, mask, head_weight, parts, own, exp_terms, up, key_qk, query, query_single,
    query_weight, key_weight, columns,
):
    return pl.pallas_call(
        grad_kernel,
        out_shape=(
            jax.ShapeDtypeStruct((ALL, KB), BF16),
            jax.ShapeDtypeStruct((ALL, KB), BF16),
            jax.ShapeDtypeStruct((ROWS // 2, SHARE, 128), F32),
            jax.ShapeDtypeStruct((ROWS // 2, SHARE, 128), F32),
            jax.ShapeDtypeStruct((3 * QB, 128), F32),
        ),
        in_specs=[SCALARS] * 3 + [VECTORS] * 11,
        out_specs=(VECTORS,) * 5,
        scratch_shapes=[
            pltpu.VMEM((ROWS * FEATS, KB), F32),
            pltpu.VMEM((KB, DS), F32),
            pltpu.VMEM((ROWS * 24, DS), F32),
        ],
        compiler_params=limit(24),
        cost_estimate=pl.CostEstimate(
            flops=3_000_000_000, bytes_accessed=8_000_000, transcendentals=20000
        ),
        name="feature_grads",
    )(
        offsets, mask, head_weight, mask.reshape(32, 128), parts, own, exp_terms, up, key_qk,
        query, query_single, query_weight, key_weight, columns,
    )


def spread_of(query, grad_single, grad_point):
    return pl.pallas_call(
        spread_kernel,
        out_shape=jax.ShapeDtypeStruct((QF + VEC + VPTS, ALL), BF16),
        in_specs=[VECTORS] * 3,
        out_specs=VECTORS,
        compiler_params=limit(16),
        cost_estimate=pl.CostEstimate(
            flops=400_000_000, bytes_accessed=4_000_000, transcendentals=0
        ),
        name="spread_features",
    )(query, grad_single, grad_point)


def pair_grads_of(pair_weight, pair, weights, scores, heads):
    return pl.pallas_call(
        pair_kernel,
        grid=(STEPS,),
        out_shape=(
            jax.ShapeDtypeStruct((QB, KB, DZ), BF16),
            jax.ShapeDtypeStruct((HP, DZ), F32),
        ),
        in_specs=[
            whole((H, DZ)),
            rows_of(STEP, KB, DZ),
            rows_of(SLAB, KB),
            rows_of(SLAB, KB),
            rows_of(STEP, HP, DZ),
        ],
        out_specs=(rows_of(STEP, KB, DZ), whole((HP, DZ))),
        scratch_shapes=[pltpu.VMEM((2 * HP, DZ), BF16)],
        compiler_params=limit(40),
        cost_estimate=pl.CostEstimate(
            flops=2_000_000_000, bytes_accessed=10_000_000, transcendentals=0
        ),
        name="pair_grads",
    )(pair_weight, pair, weights, scores, heads)


CHIPS = [[2 * i + core for i in range(ROWS // 2)] for core in range(2)]


ALONG_X = [[4 * x + z for x in range(4)] for z in range(4)]
ALONG_Z = [[4 * x + z for z in range(4)] for x in range(4)]


def other_core(values):
    return lax.ppermute(values, "row", [(i, i ^ 1) for i in range(ROWS)])


def exchange(values, axis, groups=None):
    return lax.all_to_all(values, axis, 0, 0, axis_index_groups=groups)


def gather(values, axis, parts, groups=None):
    return exchange(jnp.broadcast_to(values[None], (parts, *values.shape)), axis, groups)


def scatter_row(kept, given):
    return jnp.sum(exchange(kept + other_core(given), "row", CHIPS), axis=0)


def sum_col(values):
    share = exchange(values.reshape(4, -1, values.shape[1]), "col", ALONG_X)
    share = jnp.sum(share, axis=0)
    share = jnp.sum(gather(share, "col", 4, ALONG_Z), axis=0)
    return gather(share, "col", 4, ALONG_X).reshape(values.shape)


def lanes_of(values):
    return [values[..., 128 * k : 128 * (k + 1)] for k in range(values.shape[-1] // 128)]


def joined(values, rows):
    return jnp.concatenate(
        [values[..., k : k + rows, :] for k in range(0, values.shape[-2], rows)], axis=-1
    )


def local(
    query_single,
    key_single,
    query_weight,
    key_weight,
    pair_weight,
    head_weight,
    chain_bias,
    pair,
    residue_mask,
    chain_index,
    strip_offsets,
    grad_single_out,
    grad_point_out,
    grad_pair_out,
):
    query_weight, key_weight, pair_weight = query_weight.T, key_weight.T, pair_weight.T
    terms, up, key_qk, query, heads, own = scores_of(
        strip_offsets, residue_mask, chain_index, head_weight, chain_bias, query_single,
        key_single, query_weight, key_weight, pair_weight, pair, grad_single_out,
        grad_point_out, grad_pair_out,
    )
    columns = spread_of(query, grad_single_out, grad_point_out)
    with jax.named_scope("row_statistics"):
        parts = gather(own, "col", COLS)
    weights, scores, kept, given, query_single_part = grads_of(
        strip_offsets, residue_mask, head_weight, parts, own, terms, up, key_qk, query,
        query_single, query_weight, key_weight, columns,
    )
    with jax.named_scope("row_sum"):
        summed = scatter_row(kept, given)
    grad_pair, bias_part = pair_grads_of(pair_weight, pair, weights, scores, heads)
    key_grad = joined(summed[: 2 * FEATS], FEATS)
    key_share = jnp.dot(key_grad, key_single.astype(F32), precision=HIGHEST)
    with jax.named_scope("col_sum"):
        share = jnp.concatenate(
            lanes_of(key_share) + [bias_part, summed[160:232], query_single_part], axis=0
        )
        share = sum_col(share)
    with jax.named_scope("row_gather"):
        own = jnp.concatenate([share[:256], summed[112:160]], axis=0)
        own = gather(own, "row", ROWS // 2, CHIPS)
        results = assembled(own, other_core(own), share)
    key_weight_grad, query_weight_grad, key_single_grad, query_single_grad, pair_weight_grad = results
    return (
        query_single_grad,
        key_single_grad,
        query_weight_grad.T,
        key_weight_grad.T,
        pair_weight_grad.T,
        grad_pair,
    )


def solution(mesh):
    in_specs = (
        P("row", None),
        P("col", None),
        P(),
        P(),
        P(),
        P(),
        P(),
        P("row", "col", None),
        P(),
        P(),
        P(),
        P("row", None),
        P("row", None),
        P("row", None),
    )
    out_specs = (P("row", None), P("col", None), P(), P(), P(), P("row", "col", None))
    return jax.shard_map(local, mesh=mesh, in_specs=in_specs, out_specs=out_specs, check_vma=False)
```

```python
import functools
import math

import jax
import jax.numpy as jnp
from jax import lax
from jax.experimental import pallas as pl
from jax.experimental.pallas import tpu as pltpu
from jax.sharding import PartitionSpec as P

H = 12
C = 16
P_SIZE = 4
PV = 8
DZ = 128
DS = 384
QB = 64
KB = 256
QF = 336
KF = 816
VEC = H * C
QPTS = 3 * H * P_SIZE
VPTS = 3 * H * PV
ROWS = 16
COLS = 16
HP = 16
STEP = 16
STEPS = QB // STEP
SLAB = STEP * HP
ALL = QB * HP
FEATS = KF // ROWS
QFEATS = QF // ROWS
SHARE = 216

LOGIT_WEIGHT = math.sqrt(1.0 / 3.0)
MASKED_LOGIT = -100000.0
SCALE_QK = LOGIT_WEIGHT * C ** (-0.5)
POINT_SCALE = math.sqrt(2.0 / (9.0 * P_SIZE)) / 2.0
F32 = jnp.float32
BF16 = jnp.bfloat16
HIGHEST = lax.Precision.HIGHEST

NN = (((1,), (0,)), ((), ()))
NT = (((1,), (1,)), ((), ()))
TN = (((0,), (0,)), ((), ()))


def dot(a, b, dims=NN, precision=None):
    return lax.dot_general(a, b, dims, precision=precision, preferred_element_type=F32)


def two_part_dot(fixed, values, dims, values_first=False):
    high = values.astype(BF16)
    low = (values - high.astype(F32)).astype(BF16)
    if values_first:
        return dot(high, fixed, dims) + dot(low, fixed, dims)
    return dot(fixed, high, dims) + dot(fixed, low, dims)


def head_mask(count, group, size, offset=0, axis=1):
    shape = (HP, count) if axis == 1 else (count, HP)
    feature = lax.broadcasted_iota(jnp.int32, shape, axis)
    head = lax.broadcasted_iota(jnp.int32, shape, 1 - axis)
    return jnp.where(lax.div(lax.rem(feature, group), size) == head, 1.0, 0.0).astype(F32)


def query_mask():
    shape = (HP, QF)
    feature = lax.broadcasted_iota(jnp.int32, shape, 1)
    head = lax.broadcasted_iota(jnp.int32, shape, 0)
    of = jnp.where(
        feature < VEC,
        lax.div(feature, C),
        lax.div(lax.rem(jnp.maximum(feature - VEC, 0), H * P_SIZE), P_SIZE),
    )
    return jnp.where(of == head, 1.0, 0.0).astype(F32), feature < VEC


def spread(values, mask):
    rows, count = values.shape
    return (values.astype(F32)[:, None, :] * mask[None]).reshape(rows * HP, count)


def head_column(ref, scale, count):
    index = lax.broadcasted_iota(jnp.int32, (HP, count), 0)
    column = jnp.zeros((HP, count), F32)
    for h in range(H):
        column = jnp.where(index == h, ref[h] * scale, column)
    return column


def head_row(ref, scale, count):
    index = lax.broadcasted_iota(jnp.int32, (count, HP), 1)
    row = jnp.zeros((count, HP), F32)
    for h in range(H):
        row = jnp.where(index == h, ref[h] * scale, row)
    return row


def key_line(ref):
    begin = lax.axis_index("col") * 2
    return jnp.concatenate([ref[pl.ds(begin, 1), :], ref[pl.ds(begin + 1, 1), :]], axis=1)


def score_kernel(
    offsets,
    mask_s,
    chain_s,
    head_weight,
    chain_bias,
    mask_v,
    chain_v,
    query_single,
    key_single,
    query_weight,
    key_weight,
    pair_weight,
    pair,
    grad_single,
    grad_point,
    grad_pairs,
    exp_out,
    up_out,
    key_out,
    query_out,
    heads_out,
    stats_out,
    key_qk,
    key_v,
    key_norm,
    both,
    stat,
    spread_pairs,
    stats,
):
    step = pl.program_id(0)

    @pl.when(step == 0)
    def _():
        feats = dot(key_weight[...], key_single[...], NT).astype(BF16)
        key_qk[0:VEC] = feats[0:VEC]
        key_qk[VEC:QF] = feats[2 * VEC : 2 * VEC + QPTS]
        key_v[0:VEC] = feats[VEC : 2 * VEC]
        key_v[VEC:] = feats[2 * VEC + QPTS :]
        key_out[...] = key_qk[...]
        points = feats[2 * VEC : 2 * VEC + QPTS].astype(F32)
        key_norm[...] = dot(
            head_mask(QPTS, H * P_SIZE, P_SIZE), points * points, NN, HIGHEST
        )
        unit = jnp.where(
            lax.broadcasted_iota(jnp.int32, (HP, H), 0)
            == lax.broadcasted_iota(jnp.int32, (HP, H), 1),
            1.0,
            0.0,
        ).astype(BF16)
        both[0:HP] = dot(unit, pair_weight[...]).astype(BF16)
        spread_pairs[...] = jnp.zeros_like(spread_pairs)
        stat[...] = jnp.zeros_like(stat)

    mask, is_vec = query_mask()
    query = dot(query_single[...], query_weight[...], NT).astype(BF16)
    query_out[...] = query
    rows = spread(query, mask)
    vec_rows = jnp.where(is_vec[0:1], rows, 0.0)
    point_rows = rows - vec_rows
    query_norm = jnp.sum(point_rows * point_rows, axis=1, keepdims=True)
    scalar = dot(vec_rows.astype(BF16), key_qk[...])
    cross = dot(point_rows.astype(BF16), key_qk[...])
    upstream = dot(spread(grad_single[...], head_mask(VEC, VEC, C)).astype(BF16), key_v[0:VEC])
    upstream += dot(
        spread(grad_point[...], head_mask(VPTS, H * PV, PV)).astype(BF16), key_v[VEC:]
    )
    pairs = grad_pairs[...].astype(F32)
    for h in range(H):
        spread_pairs[:, h, :] = pairs[:, DZ * h : DZ * (h + 1)]
    heads = spread_pairs[...].astype(BF16)
    heads_out[...] = heads

    point_coef = head_column(head_weight, POINT_SCALE, KB)
    bias = head_column(chain_bias, 1.0, KB)
    key_live = key_line(mask_v) == 1
    key_chain = key_line(chain_v)
    begin = offsets[lax.axis_index("row")] + step * STEP
    lane = lax.broadcasted_iota(jnp.int32, (HP, 128), 1)
    for i in range(STEP):
        at = slice(HP * i, HP * (i + 1))
        left = jnp.concatenate([both[0:HP], heads[i]], axis=0)
        tile = dot(left, pair[i], NT)
        distance = query_norm[at] + key_norm[...] - 2.0 * cross[at]
        logits = LOGIT_WEIGHT * (scalar[at] * C ** (-0.5) + tile[0:HP] - point_coef * distance)
        same = jnp.where(key_chain == chain_s[begin + i], 1.0, 0.0)
        logits = logits + bias * same
        live = jnp.where(key_live, mask_s[begin + i], 0) == 1
        logits = jnp.where(live, logits, MASKED_LOGIT)
        up = upstream[at] + tile[HP:]
        top = jnp.max(logits, axis=1, keepdims=True)
        terms = jnp.exp(logits - top)
        total = jnp.sum(terms, axis=1, keepdims=True)
        moment = jnp.sum(terms * up, axis=1, keepdims=True)
        exp_out[at] = terms
        up_out[at] = up
        stat[at] = jnp.where(lane == 0, top, jnp.where(lane == 1, total, moment))
    for half in range(2):
        turned = stat[128 * half : 128 * (half + 1)].T
        for k in range(3):
            stats[k, pl.ds(2 * step + half, 1), :] = turned[k : k + 1]

    @pl.when(step == STEPS - 1)
    def _():
        for s in range(COLS):
            stats_out[s] = stats[...]


def spread_kernel(query, grad_single, grad_point, out):
    column = lax.broadcasted_iota(jnp.int32, (QB, ALL), 1)
    row = lax.broadcasted_iota(jnp.int32, (QB, ALL), 0)
    copies = jnp.where(lax.div(column, HP) == row, 1.0, 0.0).astype(BF16)

    def put(begin, values, group, size):
        count = values.shape[1]
        feature = lax.broadcasted_iota(jnp.int32, (count, ALL), 0)
        head = lax.rem(lax.broadcasted_iota(jnp.int32, (count, ALL), 1), HP)
        of = lax.div(lax.rem(feature, group), size)
        out[begin : begin + count] = jnp.where(
            of == head, dot(values, copies, TN), 0.0
        ).astype(BF16)

    put(0, query[:, 0:VEC], VEC, C)
    put(VEC, query[:, VEC:], H * P_SIZE, P_SIZE)
    put(QF, grad_single[...], VEC, C)
    put(QF + VEC, grad_point[...], H * PV, PV)


def grad_kernel(
    offsets,
    mask_s,
    head_weight,
    mask_v,
    parts,
    exp_terms,
    up,
    key_qk,
    query,
    query_single,
    query_weight,
    key_weight,
    columns_of,
    weight_out,
    score_out,
    kept_out,
    given_out,
    single_out,
    key_grad,
    key_single_grad,
    query_weight_grad,
):
    row_top = parts[0, 0]
    for s in range(1, COLS):
        row_top = jnp.maximum(row_top, parts[s, 0])
    row_total = jnp.zeros_like(row_top)
    moment = jnp.zeros_like(row_top)
    for s in range(COLS):
        share = jnp.exp(parts[s, 0] - row_top)
        row_total += share * parts[s, 1]
        moment += share * parts[s, 2]
    factor = jnp.exp(parts[lax.axis_index("col"), 0] - row_top) / row_total
    centre = moment / row_total
    columns = jnp.concatenate([factor, centre], axis=0).T
    key_live = jnp.where(key_line(mask_v) == 1, 1.0, 0.0)
    begin = offsets[lax.axis_index("row")]
    col_score = jnp.zeros((HP, KB), F32)
    row_score = []
    for i in range(QB):
        at = slice(HP * i, HP * (i + 1))
        chunk, off = i // 8, HP * (i % 8)
        fac = columns[off : off + HP, chunk : chunk + 1]
        mid = columns[off : off + HP, 8 + chunk : 9 + chunk]
        weights = exp_terms[at] * fac
        live = jnp.where(mask_s[begin + i] == 1, 1.0, 0.0)
        score = (weights * (up[at] - mid) * (key_live * live)).astype(BF16)
        weight_out[at] = weights.astype(BF16)
        score_out[at] = score
        score = score.astype(F32)
        col_score += score
        row_score.append(jnp.sum(score, axis=1, keepdims=True))
    row_score = jnp.concatenate(row_score, axis=0)

    mask, is_vec = query_mask()
    is_vec = is_vec[0:1]
    rows = spread(query[...], mask)
    scores = score_out[...]
    weights = weight_out[...]
    grad_coef = -2.0 * LOGIT_WEIGHT * POINT_SCALE
    key_points = head_mask(QPTS, H * P_SIZE, P_SIZE, axis=0)
    coef = jnp.sum(key_points * head_row(head_weight, grad_coef, QPTS), axis=1, keepdims=True)
    raw = dot(columns_of[0:QF], scores)
    key_grad[0:VEC] = SCALE_QK * raw[0:VEC]
    key_grad[VEC : 2 * VEC] = dot(columns_of[QF : QF + VEC], weights)
    key_grad[2 * VEC : 2 * VEC + QPTS] = coef * (
        key_qk[VEC:QF].astype(F32) * dot(key_points, col_score, NN, HIGHEST) - raw[VEC:QF]
    )
    key_grad[2 * VEC + QPTS : KF] = dot(columns_of[QF + VEC :], weights)
    key_single_grad[...] = two_part_dot(key_weight[...], key_grad[...], TN, values_first=True)
    raw = dot(scores, key_qk[...], NT)
    head_coef = head_column(head_weight, grad_coef, QF)
    head_coef = jnp.concatenate([head_coef] * QB, axis=0)
    masks = jnp.concatenate([mask] * QB, axis=0)
    raw = jnp.where(is_vec, SCALE_QK * raw, head_coef * (rows * row_score - raw)) * masks
    query_grad = jnp.sum(raw.reshape(QB, HP, QF), axis=1)
    single = two_part_dot(query_weight[...], query_grad, NN, values_first=True)
    for k in range(3):
        single_out[QB * k : QB * (k + 1)] = single[:, 128 * k : 128 * (k + 1)]
    query_weight_grad[...] = two_part_dot(query_single[...], query_grad, TN, values_first=True)
    first = lax.rem(lax.axis_index("row"), 2) == 0

    def put(q, begin, source, count, k):
        lanes = slice(128 * k, 128 * (k + 1))
        even = source[count * 2 * q : count * (2 * q + 1), lanes]
        odd = source[count * (2 * q + 1) : count * (2 * q + 2), lanes]
        at = slice(begin + count * k, begin + count * (k + 1))
        kept_out[q, at] = jnp.where(first, even, odd)
        given_out[q, at] = jnp.where(first, odd, even)

    for q in range(ROWS // 2):
        for k in range(2):
            put(q, 0, key_grad, FEATS, k)
        for k in range(3):
            put(q, 2 * FEATS, key_single_grad, 16, k)
            put(q, 2 * FEATS + 48, query_weight_grad, QFEATS, k)
        for out in (kept_out, given_out):
            out[q, 2 * FEATS + 48 + 3 * QFEATS :] = jnp.zeros((3, 128), F32)


def pair_kernel(pair_weight, pair, weights, scores, heads, pair_out, bias_out, lanes):
    step = pl.program_id(0)

    @pl.when(step == 0)
    def _():
        unit = jnp.where(
            lax.broadcasted_iota(jnp.int32, (HP, H), 0)
            == lax.broadcasted_iota(jnp.int32, (HP, H), 1),
            1.0,
            0.0,
        ).astype(BF16)
        values = LOGIT_WEIGHT * dot(unit, pair_weight[...])
        high = values.astype(BF16)
        lanes[0:HP] = high
        lanes[HP:] = (values - high.astype(F32)).astype(BF16)
        bias_out[...] = jnp.zeros_like(bias_out)

    total = jnp.zeros((HP, DZ), F32)
    for i in range(STEP):
        at = slice(HP * i, HP * (i + 1))
        score = scores[at]
        left = jnp.concatenate([weights[at], score, score], axis=0)
        right = jnp.concatenate([heads[i], lanes[...]], axis=0)
        pair_out[i] = dot(left, right, TN).astype(BF16)
        total += dot(score, pair[i])
    bias_out[...] += LOGIT_WEIGHT * total


def assemble_kernel(own, other, share, key_out, query_out, single_out, query_single_out, pair_out):
    first = lax.rem(lax.axis_index("row"), 2) == 0
    lane = pl.program_id(0)

    def chunk(r, begin, count):
        mine, theirs = own[r // 2, begin : begin + count], other[r // 2, begin : begin + count]
        if r % 2 == 1:
            mine, theirs = theirs, mine
        return jnp.where(first, mine, theirs)

    def put(k):
        for r in range(ROWS):
            key_out[FEATS * r : FEATS * (r + 1)] = chunk(r, FEATS * k, FEATS)
            query_out[QFEATS * r : QFEATS * (r + 1)] = chunk(r, 165 + QFEATS * k, QFEATS)
            single_out[16 * r : 16 * (r + 1)] = chunk(r, 228 + 16 * k, 16)
        query_single_out[...] = share[228 + QB * k : 228 + QB * (k + 1)]

    for k in range(3):
        pl.when(lane == k)(functools.partial(put, k))

    @pl.when(lane == 0)
    def _():
        total = chunk(0, 153, H)
        for r in range(1, ROWS):
            total += chunk(r, 153, H)
        pair_out[...] = total


def assembled(own, other, share):
    lanes = lambda rows: pl.BlockSpec((rows, 128), lambda k: (0, k))
    return pl.pallas_call(
        assemble_kernel,
        grid=(3,),
        out_shape=(
            jax.ShapeDtypeStruct((KF, DS), F32),
            jax.ShapeDtypeStruct((QF, DS), F32),
            jax.ShapeDtypeStruct((KB, DS), F32),
            jax.ShapeDtypeStruct((QB, DS), F32),
            jax.ShapeDtypeStruct((H, DZ), F32),
        ),
        in_specs=[VECTORS] * 3,
        out_specs=(lanes(KF), lanes(QF), lanes(KB), lanes(QB), whole((H, DZ))),
        compiler_params=limit(16),
        name="assemble",
    )(own, other, share)


def whole(shape):
    return pl.BlockSpec(shape, lambda s: (0,) * len(shape))


def rows_of(*shape):
    return pl.BlockSpec(shape, lambda s: (s,) + (0,) * (len(shape) - 1))


SCALARS = pl.BlockSpec(memory_space=pltpu.SMEM)
VECTORS = pl.BlockSpec(memory_space=pltpu.VMEM)
MIB = 1024 * 1024


def limit(mib):
    return pltpu.CompilerParams(vmem_limit_bytes=mib * MIB)


def scores_of(
    offsets, mask, chain, head_weight, chain_bias, query_single, key_single, query_weight,
    key_weight, pair_weight, pair, grad_single, grad_point, grad_pairs,
):
    return pl.pallas_call(
        score_kernel,
        grid=(STEPS,),
        out_shape=(
            jax.ShapeDtypeStruct((ALL, KB), F32),
            jax.ShapeDtypeStruct((ALL, KB), F32),
            jax.ShapeDtypeStruct((QF, KB), BF16),
            jax.ShapeDtypeStruct((QB, QF), BF16),
            jax.ShapeDtypeStruct((QB, HP, DZ), BF16),
            jax.ShapeDtypeStruct((COLS, 3, 8, 128), F32),
        ),
        in_specs=[SCALARS] * 5
        + [
            whole((32, 128)),
            whole((32, 128)),
            rows_of(STEP, DS),
            whole((KB, DS)),
            whole((QF, DS)),
            whole((KF, DS)),
            whole((H, DZ)),
            rows_of(STEP, KB, DZ),
            rows_of(STEP, VEC),
            rows_of(STEP, VPTS),
            rows_of(STEP, H * DZ),
        ],
        out_specs=(
            rows_of(SLAB, KB),
            rows_of(SLAB, KB),
            whole((QF, KB)),
            rows_of(STEP, QF),
            rows_of(STEP, HP, DZ),
            whole((COLS, 3, 8, 128)),
        ),
        scratch_shapes=[
            pltpu.VMEM((QF, KB), BF16),
            pltpu.VMEM((VEC + VPTS, KB), BF16),
            pltpu.VMEM((HP, KB), F32),
            pltpu.VMEM((HP, DZ), BF16),
            pltpu.VMEM((SLAB, 128), F32),
            pltpu.VMEM((STEP, HP, DZ), F32),
            pltpu.VMEM((3, 8, 128), F32),
        ],
        compiler_params=limit(60),
        cost_estimate=pl.CostEstimate(
            flops=2_000_000_000, bytes_accessed=8_000_000, transcendentals=262144
        ),
        name="row_scores",
    )(
        offsets, mask, chain, head_weight, chain_bias, mask.reshape(32, 128),
        chain.reshape(32, 128), query_single, key_single, query_weight, key_weight,
        pair_weight, pair, grad_single, grad_point, grad_pairs,
    )


def grads_of(
    offsets, mask, head_weight, parts, exp_terms, up, key_qk, query, query_single,
    query_weight, key_weight, columns,
):
    return pl.pallas_call(
        grad_kernel,
        out_shape=(
            jax.ShapeDtypeStruct((ALL, KB), BF16),
            jax.ShapeDtypeStruct((ALL, KB), BF16),
            jax.ShapeDtypeStruct((ROWS // 2, SHARE, 128), F32),
            jax.ShapeDtypeStruct((ROWS // 2, SHARE, 128), F32),
            jax.ShapeDtypeStruct((3 * QB, 128), F32),
        ),
        in_specs=[SCALARS] * 3 + [VECTORS] * 10,
        out_specs=(VECTORS,) * 5,
        scratch_shapes=[
            pltpu.VMEM((KF, KB), F32),
            pltpu.VMEM((KB, DS), F32),
            pltpu.VMEM((QF, DS), F32),
        ],
        compiler_params=limit(24),
        cost_estimate=pl.CostEstimate(
            flops=3_000_000_000, bytes_accessed=8_000_000, transcendentals=20000
        ),
        name="feature_grads",
    )(
        offsets, mask, head_weight, mask.reshape(32, 128), parts, exp_terms, up, key_qk,
        query, query_single, query_weight, key_weight, columns,
    )


def spread_of(query, grad_single, grad_point):
    return pl.pallas_call(
        spread_kernel,
        out_shape=jax.ShapeDtypeStruct((QF + VEC + VPTS, ALL), BF16),
        in_specs=[VECTORS] * 3,
        out_specs=VECTORS,
        compiler_params=limit(16),
        cost_estimate=pl.CostEstimate(
            flops=400_000_000, bytes_accessed=4_000_000, transcendentals=0
        ),
        name="spread_features",
    )(query, grad_single, grad_point)


def pair_grads_of(pair_weight, pair, weights, scores, heads):
    return pl.pallas_call(
        pair_kernel,
        grid=(STEPS,),
        out_shape=(
            jax.ShapeDtypeStruct((QB, KB, DZ), BF16),
            jax.ShapeDtypeStruct((HP, DZ), F32),
        ),
        in_specs=[
            whole((H, DZ)),
            rows_of(STEP, KB, DZ),
            rows_of(SLAB, KB),
            rows_of(SLAB, KB),
            rows_of(STEP, HP, DZ),
        ],
        out_specs=(rows_of(STEP, KB, DZ), whole((HP, DZ))),
        scratch_shapes=[pltpu.VMEM((2 * HP, DZ), BF16)],
        compiler_params=limit(40),
        cost_estimate=pl.CostEstimate(
            flops=2_000_000_000, bytes_accessed=10_000_000, transcendentals=0
        ),
        name="pair_grads",
    )(pair_weight, pair, weights, scores, heads)


CHIPS = [[2 * i + core for i in range(ROWS // 2)] for core in range(2)]


ALONG_X = [[4 * x + z for x in range(4)] for z in range(4)]
ALONG_Z = [[4 * x + z for z in range(4)] for x in range(4)]


def other_core(values):
    return lax.ppermute(values, "row", [(i, i ^ 1) for i in range(ROWS)])


def exchange(values, axis, groups=None):
    return lax.all_to_all(values, axis, 0, 0, axis_index_groups=groups)


def gather(values, axis, parts, groups=None):
    return exchange(jnp.broadcast_to(values[None], (parts, *values.shape)), axis, groups)


def scatter_row(kept, given):
    return jnp.sum(exchange(kept + other_core(given), "row", CHIPS), axis=0)


def sum_col(values):
    share = exchange(values.reshape(4, -1, values.shape[1]), "col", ALONG_X)
    share = jnp.sum(share, axis=0)
    share = jnp.sum(gather(share, "col", 4, ALONG_Z), axis=0)
    return gather(share, "col", 4, ALONG_X).reshape(values.shape)


def lanes_of(values):
    return [values[..., 128 * k : 128 * (k + 1)] for k in range(values.shape[-1] // 128)]


def joined(values, rows):
    return jnp.concatenate(
        [values[..., k : k + rows, :] for k in range(0, values.shape[-2], rows)], axis=-1
    )


def local(
    query_single,
    key_single,
    query_weight,
    key_weight,
    pair_weight,
    head_weight,
    chain_bias,
    pair,
    residue_mask,
    chain_index,
    strip_offsets,
    grad_single_out,
    grad_point_out,
    grad_pair_out,
):
    query_weight, key_weight, pair_weight = query_weight.T, key_weight.T, pair_weight.T
    terms, up, key_qk, query, heads, own = scores_of(
        strip_offsets, residue_mask, chain_index, head_weight, chain_bias, query_single,
        key_single, query_weight, key_weight, pair_weight, pair, grad_single_out,
        grad_point_out, grad_pair_out,
    )
    columns = spread_of(query, grad_single_out, grad_point_out)
    with jax.named_scope("row_statistics"):
        parts = exchange(own, "col")
    weights, scores, kept, given, query_single_part = grads_of(
        strip_offsets, residue_mask, head_weight, parts, terms, up, key_qk, query,
        query_single, query_weight, key_weight, columns,
    )
    with jax.named_scope("row_sum"):
        summed = scatter_row(kept, given)
    grad_pair, bias_part = pair_grads_of(pair_weight, pair, weights, scores, heads)
    key_grad = joined(summed[: 2 * FEATS], FEATS)
    key_share = jnp.dot(key_grad, key_single.astype(F32), precision=HIGHEST)
    with jax.named_scope("col_sum"):
        share = jnp.concatenate(
            lanes_of(key_share)
            + [bias_part[:H], summed[150:213], query_single_part, jnp.zeros((28, 128), F32)],
            axis=0,
        )
        share = sum_col(share)
    with jax.named_scope("row_gather"):
        own = jnp.concatenate(
            [share[:228], summed[102:150], jnp.zeros((4, 128), F32)], axis=0
        )
        own = gather(own, "row", ROWS // 2, CHIPS)
        results = assembled(own, other_core(own), share)
    key_weight_grad, query_weight_grad, key_single_grad, query_single_grad, pair_weight_grad = results
    return (
        query_single_grad,
        key_single_grad,
        query_weight_grad.T,
        key_weight_grad.T,
        pair_weight_grad.T,
        grad_pair,
    )


def solution(mesh):
    in_specs = (
        P("row", None),
        P("col", None),
        P(),
        P(),
        P(),
        P(),
        P(),
        P("row", "col", None),
        P(),
        P(),
        P(),
        P("row", None),
        P("row", None),
        P("row", None),
    )
    out_specs = (P("row", None), P("col", None), P(), P(), P(), P("row", "col", None))
    return jax.shard_map(local, mesh=mesh, in_specs=in_specs, out_specs=out_specs, check_vma=False)
```

```python
import functools
import math

import jax
import jax.numpy as jnp
from jax import lax
from jax.experimental import pallas as pl
from jax.experimental.pallas import tpu as pltpu
from jax.sharding import PartitionSpec as P

H = 12
C = 16
P_SIZE = 4
PV = 8
DZ = 128
DS = 384
QB = 64
KB = 256
QF = 336
KF = 816
VEC = H * C
QPTS = 3 * H * P_SIZE
VPTS = 3 * H * PV
ROWS = 16
COLS = 16
HP = 16
STEP = 16
STEPS = QB // STEP
SLAB = STEP * HP
ALL = QB * HP
FEATS = KF // ROWS
QFEATS = QF // ROWS
SHARE = 216

LOGIT_WEIGHT = math.sqrt(1.0 / 3.0)
MASKED_LOGIT = -100000.0
SCALE_QK = LOGIT_WEIGHT * C ** (-0.5)
POINT_SCALE = math.sqrt(2.0 / (9.0 * P_SIZE)) / 2.0
F32 = jnp.float32
BF16 = jnp.bfloat16
HIGHEST = lax.Precision.HIGHEST

NN = (((1,), (0,)), ((), ()))
NT = (((1,), (1,)), ((), ()))
TN = (((0,), (0,)), ((), ()))


def dot(a, b, dims=NN, precision=None):
    return lax.dot_general(a, b, dims, precision=precision, preferred_element_type=F32)


def two_part_dot(fixed, values, dims, values_first=False):
    high = values.astype(BF16)
    low = (values - high.astype(F32)).astype(BF16)
    if values_first:
        return dot(high, fixed, dims) + dot(low, fixed, dims)
    return dot(fixed, high, dims) + dot(fixed, low, dims)


def head_mask(count, group, size, offset=0, axis=1):
    shape = (HP, count) if axis == 1 else (count, HP)
    feature = lax.broadcasted_iota(jnp.int32, shape, axis)
    head = lax.broadcasted_iota(jnp.int32, shape, 1 - axis)
    return jnp.where(lax.div(lax.rem(feature, group), size) == head, 1.0, 0.0).astype(F32)


def query_mask():
    shape = (HP, QF)
    feature = lax.broadcasted_iota(jnp.int32, shape, 1)
    head = lax.broadcasted_iota(jnp.int32, shape, 0)
    of = jnp.where(
        feature < VEC,
        lax.div(feature, C),
        lax.div(lax.rem(jnp.maximum(feature - VEC, 0), H * P_SIZE), P_SIZE),
    )
    return jnp.where(of == head, 1.0, 0.0).astype(F32), feature < VEC


def spread(values, mask):
    rows, count = values.shape
    return (values.astype(F32)[:, None, :] * mask[None]).reshape(rows * HP, count)


def head_column(ref, scale, count):
    index = lax.broadcasted_iota(jnp.int32, (HP, count), 0)
    column = jnp.zeros((HP, count), F32)
    for h in range(H):
        column = jnp.where(index == h, ref[h] * scale, column)
    return column


def head_row(ref, scale, count):
    index = lax.broadcasted_iota(jnp.int32, (count, HP), 1)
    row = jnp.zeros((count, HP), F32)
    for h in range(H):
        row = jnp.where(index == h, ref[h] * scale, row)
    return row


def key_line(ref):
    begin = lax.axis_index("col") * 2
    return jnp.concatenate([ref[pl.ds(begin, 1), :], ref[pl.ds(begin + 1, 1), :]], axis=1)


def score_kernel(
    offsets,
    mask_s,
    chain_s,
    head_weight,
    chain_bias,
    mask_v,
    chain_v,
    query_single,
    key_single,
    query_weight,
    key_weight,
    pair_weight,
    pair,
    grad_single,
    grad_point,
    grad_pairs,
    exp_out,
    up_out,
    key_out,
    query_out,
    heads_out,
    stats_out,
    key_qk,
    key_v,
    key_norm,
    both,
    stat,
    spread_pairs,
    stats,
):
    step = pl.program_id(0)

    @pl.when(step == 0)
    def _():
        feats = dot(key_weight[...], key_single[...], NT).astype(BF16)
        key_qk[0:VEC] = feats[0:VEC]
        key_qk[VEC:QF] = feats[2 * VEC : 2 * VEC + QPTS]
        key_v[0:VEC] = feats[VEC : 2 * VEC]
        key_v[VEC:] = feats[2 * VEC + QPTS :]
        key_out[...] = key_qk[...]
        points = feats[2 * VEC : 2 * VEC + QPTS].astype(F32)
        key_norm[...] = dot(
            head_mask(QPTS, H * P_SIZE, P_SIZE), points * points, NN, HIGHEST
        )
        unit = jnp.where(
            lax.broadcasted_iota(jnp.int32, (HP, H), 0)
            == lax.broadcasted_iota(jnp.int32, (HP, H), 1),
            1.0,
            0.0,
        ).astype(BF16)
        both[0:HP] = dot(unit, pair_weight[...]).astype(BF16)
        spread_pairs[...] = jnp.zeros_like(spread_pairs)
        stat[...] = jnp.zeros_like(stat)

    mask, is_vec = query_mask()
    query = dot(query_single[...], query_weight[...], NT).astype(BF16)
    query_out[...] = query
    rows = spread(query, mask)
    vec_rows = jnp.where(is_vec[0:1], rows, 0.0)
    point_rows = rows - vec_rows
    query_norm = jnp.sum(point_rows * point_rows, axis=1, keepdims=True)
    scalar = dot(vec_rows.astype(BF16), key_qk[...])
    cross = dot(point_rows.astype(BF16), key_qk[...])
    upstream = dot(spread(grad_single[...], head_mask(VEC, VEC, C)).astype(BF16), key_v[0:VEC])
    upstream += dot(
        spread(grad_point[...], head_mask(VPTS, H * PV, PV)).astype(BF16), key_v[VEC:]
    )
    pairs = grad_pairs[...].astype(F32)
    for h in range(H):
        spread_pairs[:, h, :] = pairs[:, DZ * h : DZ * (h + 1)]
    heads = spread_pairs[...].astype(BF16)
    heads_out[...] = heads

    point_coef = head_column(head_weight, POINT_SCALE, KB)
    bias = head_column(chain_bias, 1.0, KB)
    key_live = key_line(mask_v) == 1
    key_chain = key_line(chain_v)
    begin = offsets[lax.axis_index("row")] + step * STEP
    lane = lax.broadcasted_iota(jnp.int32, (HP, 128), 1)
    for i in range(STEP):
        at = slice(HP * i, HP * (i + 1))
        left = jnp.concatenate([both[0:HP], heads[i]], axis=0)
        tile = dot(left, pair[i], NT)
        distance = query_norm[at] + key_norm[...] - 2.0 * cross[at]
        logits = LOGIT_WEIGHT * (scalar[at] * C ** (-0.5) + tile[0:HP] - point_coef * distance)
        same = jnp.where(key_chain == chain_s[begin + i], 1.0, 0.0)
        logits = logits + bias * same
        live = jnp.where(key_live, mask_s[begin + i], 0) == 1
        logits = jnp.where(live, logits, MASKED_LOGIT)
        up = upstream[at] + tile[HP:]
        top = jnp.max(logits, axis=1, keepdims=True)
        terms = jnp.exp(logits - top)
        total = jnp.sum(terms, axis=1, keepdims=True)
        moment = jnp.sum(terms * up, axis=1, keepdims=True)
        exp_out[at] = terms
        up_out[at] = up
        stat[at] = jnp.where(lane == 0, top, jnp.where(lane == 1, total, moment))
    for half in range(2):
        turned = stat[128 * half : 128 * (half + 1)].T
        for k in range(3):
            stats[k, pl.ds(2 * step + half, 1), :] = turned[k : k + 1]

    @pl.when(step == STEPS - 1)
    def _():
        for s in range(COLS):
            stats_out[s] = stats[...]


def spread_kernel(query, grad_single, grad_point, out):
    column = lax.broadcasted_iota(jnp.int32, (QB, ALL), 1)
    row = lax.broadcasted_iota(jnp.int32, (QB, ALL), 0)
    copies = jnp.where(lax.div(column, HP) == row, 1.0, 0.0).astype(BF16)

    def put(begin, values, group, size):
        count = values.shape[1]
        feature = lax.broadcasted_iota(jnp.int32, (count, ALL), 0)
        head = lax.rem(lax.broadcasted_iota(jnp.int32, (count, ALL), 1), HP)
        of = lax.div(lax.rem(feature, group), size)
        out[begin : begin + count] = jnp.where(
            of == head, dot(values, copies, TN), 0.0
        ).astype(BF16)

    put(0, query[:, 0:VEC], VEC, C)
    put(VEC, query[:, VEC:], H * P_SIZE, P_SIZE)
    put(QF, grad_single[...], VEC, C)
    put(QF + VEC, grad_point[...], H * PV, PV)


def grad_kernel(
    offsets,
    mask_s,
    head_weight,
    mask_v,
    parts,
    exp_terms,
    up,
    key_qk,
    query,
    query_single,
    query_weight,
    key_weight,
    columns_of,
    weight_out,
    score_out,
    kept_out,
    given_out,
    single_out,
    key_grad,
    key_single_grad,
    query_weight_grad,
):
    row_top = parts[0, 0]
    for s in range(1, COLS):
        row_top = jnp.maximum(row_top, parts[s, 0])
    row_total = jnp.zeros_like(row_top)
    moment = jnp.zeros_like(row_top)
    for s in range(COLS):
        share = jnp.exp(parts[s, 0] - row_top)
        row_total += share * parts[s, 1]
        moment += share * parts[s, 2]
    factor = jnp.exp(parts[lax.axis_index("col"), 0] - row_top) / row_total
    centre = moment / row_total
    columns = jnp.concatenate([factor, centre], axis=0).T
    key_live = jnp.where(key_line(mask_v) == 1, 1.0, 0.0)
    begin = offsets[lax.axis_index("row")]
    col_score = jnp.zeros((HP, KB), F32)
    row_score = []
    for i in range(QB):
        at = slice(HP * i, HP * (i + 1))
        chunk, off = i // 8, HP * (i % 8)
        fac = columns[off : off + HP, chunk : chunk + 1]
        mid = columns[off : off + HP, 8 + chunk : 9 + chunk]
        weights = exp_terms[at] * fac
        live = jnp.where(mask_s[begin + i] == 1, 1.0, 0.0)
        score = (weights * (up[at] - mid) * (key_live * live)).astype(BF16)
        weight_out[at] = weights.astype(BF16)
        score_out[at] = score
        score = score.astype(F32)
        col_score += score
        row_score.append(jnp.sum(score, axis=1, keepdims=True))
    row_score = jnp.concatenate(row_score, axis=0)

    mask, is_vec = query_mask()
    is_vec = is_vec[0:1]
    rows = spread(query[...], mask)
    scores = score_out[...]
    weights = weight_out[...]
    grad_coef = -2.0 * LOGIT_WEIGHT * POINT_SCALE
    key_points = head_mask(QPTS, H * P_SIZE, P_SIZE, axis=0)
    coef = jnp.sum(key_points * head_row(head_weight, grad_coef, QPTS), axis=1, keepdims=True)
    raw = dot(columns_of[0:QF], scores)
    key_grad[0:VEC] = SCALE_QK * raw[0:VEC]
    key_grad[VEC : 2 * VEC] = dot(columns_of[QF : QF + VEC], weights)
    key_grad[2 * VEC : 2 * VEC + QPTS] = coef * (
        key_qk[VEC:QF].astype(F32) * dot(key_points, col_score, NN, HIGHEST) - raw[VEC:QF]
    )
    key_grad[2 * VEC + QPTS : KF] = dot(columns_of[QF + VEC :], weights)
    key_single_grad[...] = two_part_dot(key_weight[...], key_grad[...], TN, values_first=True)
    raw = dot(scores, key_qk[...], NT)
    head_coef = head_column(head_weight, grad_coef, QF)
    head_coef = jnp.concatenate([head_coef] * QB, axis=0)
    masks = jnp.concatenate([mask] * QB, axis=0)
    raw = jnp.where(is_vec, SCALE_QK * raw, head_coef * (rows * row_score - raw)) * masks
    query_grad = jnp.sum(raw.reshape(QB, HP, QF), axis=1)
    single = two_part_dot(query_weight[...], query_grad, NN, values_first=True)
    for k in range(3):
        single_out[QB * k : QB * (k + 1)] = single[:, 128 * k : 128 * (k + 1)]
    query_weight_grad[...] = two_part_dot(query_single[...], query_grad, TN, values_first=True)
    first = lax.rem(lax.axis_index("row"), 2) == 0

    def put(q, begin, source, count, k):
        lanes = slice(128 * k, 128 * (k + 1))
        even = source[count * 2 * q : count * (2 * q + 1), lanes]
        odd = source[count * (2 * q + 1) : count * (2 * q + 2), lanes]
        at = slice(begin + count * k, begin + count * (k + 1))
        kept_out[q, at] = jnp.where(first, even, odd)
        given_out[q, at] = jnp.where(first, odd, even)

    for q in range(ROWS // 2):
        for k in range(2):
            put(q, 0, key_grad, FEATS, k)
        for k in range(3):
            put(q, 2 * FEATS, key_single_grad, 16, k)
            put(q, 2 * FEATS + 48, query_weight_grad, QFEATS, k)
        for out in (kept_out, given_out):
            out[q, 2 * FEATS + 48 + 3 * QFEATS :] = jnp.zeros((3, 128), F32)


def pair_kernel(pair_weight, pair, weights, scores, heads, pair_out, bias_out, lanes):
    step = pl.program_id(0)

    @pl.when(step == 0)
    def _():
        unit = jnp.where(
            lax.broadcasted_iota(jnp.int32, (HP, H), 0)
            == lax.broadcasted_iota(jnp.int32, (HP, H), 1),
            1.0,
            0.0,
        ).astype(BF16)
        values = LOGIT_WEIGHT * dot(unit, pair_weight[...])
        high = values.astype(BF16)
        lanes[0:HP] = high
        lanes[HP:] = (values - high.astype(F32)).astype(BF16)
        bias_out[...] = jnp.zeros_like(bias_out)

    total = jnp.zeros((HP, DZ), F32)
    for i in range(STEP):
        at = slice(HP * i, HP * (i + 1))
        score = scores[at]
        left = jnp.concatenate([weights[at], score, score], axis=0)
        right = jnp.concatenate([heads[i], lanes[...]], axis=0)
        pair_out[i] = dot(left, right, TN).astype(BF16)
        total += dot(score, pair[i])
    bias_out[...] += LOGIT_WEIGHT * total


def share_kernel(
    got, key_single, bias_part, query_single_part, share_out, single_out, total
):
    value = got[0]
    for s in range(1, ROWS // 2):
        value += got[s]
    total[...] = value
    key_grad = jnp.concatenate([total[0:56], total[FEATS : FEATS + 56]], axis=1)
    key_share = two_part_dot(key_single[...], key_grad, NN, values_first=True)
    for k in range(3):
        share_out[FEATS * k : FEATS * (k + 1)] = key_share[0:FEATS, 128 * k : 128 * (k + 1)]
    share_out[153:165] = bias_part[0:H]
    share_out[165:228] = total[150:213]
    share_out[228:420] = query_single_part[...]
    share_out[420:] = jnp.zeros((28, 128), F32)
    single_out[0:48] = total[102:150]
    single_out[48:] = jnp.zeros((4, 128), F32)


def share_of(got, key_single, bias_part, query_single_part):
    return pl.pallas_call(
        share_kernel,
        out_shape=(
            jax.ShapeDtypeStruct((448, 128), F32),
            jax.ShapeDtypeStruct((52, 128), F32),
        ),
        in_specs=[VECTORS] * 4,
        out_specs=(VECTORS,) * 2,
        scratch_shapes=[pltpu.VMEM((SHARE, 128), F32)],
        compiler_params=limit(16),
        name="row_share",
    )(got, key_single, bias_part, query_single_part)


def assemble_kernel(own, other, share, key_out, query_out, single_out, query_single_out, pair_out):
    first = lax.rem(lax.axis_index("row"), 2) == 0
    lane = pl.program_id(0)

    def chunk(r, begin, count):
        mine, theirs = own[r // 2, begin : begin + count], other[r // 2, begin : begin + count]
        if r % 2 == 1:
            mine, theirs = theirs, mine
        return jnp.where(first, mine, theirs)

    def put(k):
        for r in range(ROWS):
            key_out[FEATS * r : FEATS * (r + 1)] = chunk(r, FEATS * k, FEATS)
            query_out[QFEATS * r : QFEATS * (r + 1)] = chunk(r, 165 + QFEATS * k, QFEATS)
            single_out[16 * r : 16 * (r + 1)] = chunk(r, 228 + 16 * k, 16)
        query_single_out[...] = share[228 + QB * k : 228 + QB * (k + 1)]

    for k in range(3):
        pl.when(lane == k)(functools.partial(put, k))

    @pl.when(lane == 0)
    def _():
        total = chunk(0, 153, H)
        for r in range(1, ROWS):
            total += chunk(r, 153, H)
        pair_out[...] = total


def assembled(own, other, share):
    lanes = lambda rows: pl.BlockSpec((rows, 128), lambda k: (0, k))
    return pl.pallas_call(
        assemble_kernel,
        grid=(3,),
        out_shape=(
            jax.ShapeDtypeStruct((KF, DS), F32),
            jax.ShapeDtypeStruct((QF, DS), F32),
            jax.ShapeDtypeStruct((KB, DS), F32),
            jax.ShapeDtypeStruct((QB, DS), F32),
            jax.ShapeDtypeStruct((H, DZ), F32),
        ),
        in_specs=[VECTORS] * 3,
        out_specs=(lanes(KF), lanes(QF), lanes(KB), lanes(QB), whole((H, DZ))),
        compiler_params=limit(16),
        name="assemble",
    )(own, other, share)


def whole(shape):
    return pl.BlockSpec(shape, lambda s: (0,) * len(shape))


def rows_of(*shape):
    return pl.BlockSpec(shape, lambda s: (s,) + (0,) * (len(shape) - 1))


SCALARS = pl.BlockSpec(memory_space=pltpu.SMEM)
VECTORS = pl.BlockSpec(memory_space=pltpu.VMEM)
MIB = 1024 * 1024


def limit(mib):
    return pltpu.CompilerParams(vmem_limit_bytes=mib * MIB)


def scores_of(
    offsets, mask, chain, head_weight, chain_bias, query_single, key_single, query_weight,
    key_weight, pair_weight, pair, grad_single, grad_point, grad_pairs,
):
    return pl.pallas_call(
        score_kernel,
        grid=(STEPS,),
        out_shape=(
            jax.ShapeDtypeStruct((ALL, KB), F32),
            jax.ShapeDtypeStruct((ALL, KB), F32),
            jax.ShapeDtypeStruct((QF, KB), BF16),
            jax.ShapeDtypeStruct((QB, QF), BF16),
            jax.ShapeDtypeStruct((QB, HP, DZ), BF16),
            jax.ShapeDtypeStruct((COLS, 3, 8, 128), F32),
        ),
        in_specs=[SCALARS] * 5
        + [
            whole((32, 128)),
            whole((32, 128)),
            rows_of(STEP, DS),
            whole((KB, DS)),
            whole((QF, DS)),
            whole((KF, DS)),
            whole((H, DZ)),
            rows_of(STEP, KB, DZ),
            rows_of(STEP, VEC),
            rows_of(STEP, VPTS),
            rows_of(STEP, H * DZ),
        ],
        out_specs=(
            rows_of(SLAB, KB),
            rows_of(SLAB, KB),
            whole((QF, KB)),
            rows_of(STEP, QF),
            rows_of(STEP, HP, DZ),
            whole((COLS, 3, 8, 128)),
        ),
        scratch_shapes=[
            pltpu.VMEM((QF, KB), BF16),
            pltpu.VMEM((VEC + VPTS, KB), BF16),
            pltpu.VMEM((HP, KB), F32),
            pltpu.VMEM((HP, DZ), BF16),
            pltpu.VMEM((SLAB, 128), F32),
            pltpu.VMEM((STEP, HP, DZ), F32),
            pltpu.VMEM((3, 8, 128), F32),
        ],
        compiler_params=limit(60),
        cost_estimate=pl.CostEstimate(
            flops=2_000_000_000, bytes_accessed=8_000_000, transcendentals=262144
        ),
        name="row_scores",
    )(
        offsets, mask, chain, head_weight, chain_bias, mask.reshape(32, 128),
        chain.reshape(32, 128), query_single, key_single, query_weight, key_weight,
        pair_weight, pair, grad_single, grad_point, grad_pairs,
    )


def grads_of(
    offsets, mask, head_weight, parts, exp_terms, up, key_qk, query, query_single,
    query_weight, key_weight, columns,
):
    return pl.pallas_call(
        grad_kernel,
        out_shape=(
            jax.ShapeDtypeStruct((ALL, KB), BF16),
            jax.ShapeDtypeStruct((ALL, KB), BF16),
            jax.ShapeDtypeStruct((ROWS // 2, SHARE, 128), F32),
            jax.ShapeDtypeStruct((ROWS // 2, SHARE, 128), F32),
            jax.ShapeDtypeStruct((3 * QB, 128), F32),
        ),
        in_specs=[SCALARS] * 3 + [VECTORS] * 10,
        out_specs=(VECTORS,) * 5,
        scratch_shapes=[
            pltpu.VMEM((KF, KB), F32),
            pltpu.VMEM((KB, DS), F32),
            pltpu.VMEM((QF, DS), F32),
        ],
        compiler_params=limit(24),
        cost_estimate=pl.CostEstimate(
            flops=3_000_000_000, bytes_accessed=8_000_000, transcendentals=20000
        ),
        name="feature_grads",
    )(
        offsets, mask, head_weight, mask.reshape(32, 128), parts, exp_terms, up, key_qk,
        query, query_single, query_weight, key_weight, columns,
    )


def spread_of(query, grad_single, grad_point):
    return pl.pallas_call(
        spread_kernel,
        out_shape=jax.ShapeDtypeStruct((QF + VEC + VPTS, ALL), BF16),
        in_specs=[VECTORS] * 3,
        out_specs=VECTORS,
        compiler_params=limit(16),
        cost_estimate=pl.CostEstimate(
            flops=400_000_000, bytes_accessed=4_000_000, transcendentals=0
        ),
        name="spread_features",
    )(query, grad_single, grad_point)


def pair_grads_of(pair_weight, pair, weights, scores, heads):
    return pl.pallas_call(
        pair_kernel,
        grid=(STEPS,),
        out_shape=(
            jax.ShapeDtypeStruct((QB, KB, DZ), BF16),
            jax.ShapeDtypeStruct((HP, DZ), F32),
        ),
        in_specs=[
            whole((H, DZ)),
            rows_of(STEP, KB, DZ),
            rows_of(SLAB, KB),
            rows_of(SLAB, KB),
            rows_of(STEP, HP, DZ),
        ],
        out_specs=(rows_of(STEP, KB, DZ), whole((HP, DZ))),
        scratch_shapes=[pltpu.VMEM((2 * HP, DZ), BF16)],
        compiler_params=limit(40),
        cost_estimate=pl.CostEstimate(
            flops=2_000_000_000, bytes_accessed=10_000_000, transcendentals=0
        ),
        name="pair_grads",
    )(pair_weight, pair, weights, scores, heads)


CHIPS = [[2 * i + core for i in range(ROWS // 2)] for core in range(2)]


ALONG_X = [[4 * x + z for x in range(4)] for z in range(4)]
ALONG_Z = [[4 * x + z for z in range(4)] for x in range(4)]


def other_core(values):
    return lax.ppermute(values, "row", [(i, i ^ 1) for i in range(ROWS)])


def exchange(values, axis, groups=None):
    return lax.all_to_all(values, axis, 0, 0, axis_index_groups=groups)


def gather(values, axis, parts, groups=None):
    return exchange(jnp.broadcast_to(values[None], (parts, *values.shape)), axis, groups)


def scatter_row(kept, given):
    return exchange(kept + other_core(given), "row", CHIPS)


def sum_col(values):
    share = exchange(values.reshape(4, -1, values.shape[1]), "col", ALONG_X)
    share = jnp.sum(share, axis=0)
    share = jnp.sum(gather(share, "col", 4, ALONG_Z), axis=0)
    return gather(share, "col", 4, ALONG_X).reshape(values.shape)


def local(
    query_single,
    key_single,
    query_weight,
    key_weight,
    pair_weight,
    head_weight,
    chain_bias,
    pair,
    residue_mask,
    chain_index,
    strip_offsets,
    grad_single_out,
    grad_point_out,
    grad_pair_out,
):
    query_weight, key_weight, pair_weight = query_weight.T, key_weight.T, pair_weight.T
    terms, up, key_qk, query, heads, own = scores_of(
        strip_offsets, residue_mask, chain_index, head_weight, chain_bias, query_single,
        key_single, query_weight, key_weight, pair_weight, pair, grad_single_out,
        grad_point_out, grad_pair_out,
    )
    columns = spread_of(query, grad_single_out, grad_point_out)
    with jax.named_scope("row_statistics"):
        parts = exchange(own, "col")
    weights, scores, kept, given, query_single_part = grads_of(
        strip_offsets, residue_mask, head_weight, parts, terms, up, key_qk, query,
        query_single, query_weight, key_weight, columns,
    )
    with jax.named_scope("row_sum"):
        got = scatter_row(kept, given)
    grad_pair, bias_part = pair_grads_of(pair_weight, pair, weights, scores, heads)
    share, single = share_of(got, key_single, bias_part, query_single_part)
    with jax.named_scope("col_sum"):
        share = sum_col(share)
    with jax.named_scope("row_gather"):
        own = jnp.concatenate(
            [share[:228], single], axis=0
        )
        own = gather(own, "row", ROWS // 2, CHIPS)
        results = assembled(own, other_core(own), share)
    key_weight_grad, query_weight_grad, key_single_grad, query_single_grad, pair_weight_grad = results
    return (
        query_single_grad,
        key_single_grad,
        query_weight_grad.T,
        key_weight_grad.T,
        pair_weight_grad.T,
        grad_pair,
    )


def solution(mesh):
    in_specs = (
        P("row", None),
        P("col", None),
        P(),
        P(),
        P(),
        P(),
        P(),
        P("row", "col", None),
        P(),
        P(),
        P(),
        P("row", None),
        P("row", None),
        P("row", None),
    )
    out_specs = (P("row", None), P("col", None), P(), P(), P(), P("row", "col", None))
    return jax.shard_map(local, mesh=mesh, in_specs=in_specs, out_specs=out_specs, check_vma=False)
```

```python
import functools
import math

import jax
import jax.numpy as jnp
from jax import lax
from jax.experimental import pallas as pl
from jax.experimental.pallas import tpu as pltpu
from jax.sharding import PartitionSpec as P

H = 12
C = 16
P_SIZE = 4
PV = 8
DZ = 128
DS = 384
QB = 64
KB = 256
QF = 336
KF = 816
VEC = H * C
QPTS = 3 * H * P_SIZE
VPTS = 3 * H * PV
ROWS = 16
COLS = 16
HP = 16
STEP = 16
STEPS = QB // STEP
SLAB = STEP * HP
ALL = QB * HP
FEATS = KF // ROWS
QFEATS = QF // ROWS
SHARE = 216

LOGIT_WEIGHT = math.sqrt(1.0 / 3.0)
MASKED_LOGIT = -100000.0
SCALE_QK = LOGIT_WEIGHT * C ** (-0.5)
POINT_SCALE = math.sqrt(2.0 / (9.0 * P_SIZE)) / 2.0
F32 = jnp.float32
BF16 = jnp.bfloat16
HIGHEST = lax.Precision.HIGHEST

NN = (((1,), (0,)), ((), ()))
NT = (((1,), (1,)), ((), ()))
TN = (((0,), (0,)), ((), ()))


def dot(a, b, dims=NN, precision=None):
    return lax.dot_general(a, b, dims, precision=precision, preferred_element_type=F32)


def two_part_dot(fixed, values, dims, values_first=False):
    high = values.astype(BF16)
    low = (values - high.astype(F32)).astype(BF16)
    if values_first:
        return dot(high, fixed, dims) + dot(low, fixed, dims)
    return dot(fixed, high, dims) + dot(fixed, low, dims)


def head_mask(count, group, size, offset=0, axis=1):
    shape = (HP, count) if axis == 1 else (count, HP)
    feature = lax.broadcasted_iota(jnp.int32, shape, axis)
    head = lax.broadcasted_iota(jnp.int32, shape, 1 - axis)
    return jnp.where(lax.div(lax.rem(feature, group), size) == head, 1.0, 0.0).astype(F32)


def query_mask():
    shape = (HP, QF)
    feature = lax.broadcasted_iota(jnp.int32, shape, 1)
    head = lax.broadcasted_iota(jnp.int32, shape, 0)
    of = jnp.where(
        feature < VEC,
        lax.div(feature, C),
        lax.div(lax.rem(jnp.maximum(feature - VEC, 0), H * P_SIZE), P_SIZE),
    )
    return jnp.where(of == head, 1.0, 0.0).astype(F32), feature < VEC


def spread(values, mask):
    rows, count = values.shape
    return (values.astype(F32)[:, None, :] * mask[None]).reshape(rows * HP, count)


def head_column(ref, scale, count):
    index = lax.broadcasted_iota(jnp.int32, (HP, count), 0)
    column = jnp.zeros((HP, count), F32)
    for h in range(H):
        column = jnp.where(index == h, ref[h] * scale, column)
    return column


def head_row(ref, scale, count):
    index = lax.broadcasted_iota(jnp.int32, (count, HP), 1)
    row = jnp.zeros((count, HP), F32)
    for h in range(H):
        row = jnp.where(index == h, ref[h] * scale, row)
    return row


def key_line(ref):
    begin = lax.axis_index("col") * 2
    return jnp.concatenate([ref[pl.ds(begin, 1), :], ref[pl.ds(begin + 1, 1), :]], axis=1)


def score_kernel(
    offsets,
    mask_s,
    chain_s,
    head_weight,
    chain_bias,
    mask_v,
    chain_v,
    query_single,
    key_single,
    query_weight,
    key_weight,
    pair_weight,
    pair,
    grad_single,
    grad_point,
    grad_pairs,
    exp_out,
    up_out,
    key_out,
    query_out,
    heads_out,
    stats_out,
    key_qk,
    key_v,
    key_norm,
    both,
    stat,
    spread_pairs,
    stats,
):
    step = pl.program_id(0)

    @pl.when(step == 0)
    def _():
        feats = dot(key_weight[...], key_single[...], NT).astype(BF16)
        key_qk[0:VEC] = feats[0:VEC]
        key_qk[VEC:QF] = feats[2 * VEC : 2 * VEC + QPTS]
        key_v[0:VEC] = feats[VEC : 2 * VEC]
        key_v[VEC:] = feats[2 * VEC + QPTS :]
        key_out[...] = key_qk[...]
        points = feats[2 * VEC : 2 * VEC + QPTS].astype(F32)
        key_norm[...] = dot(
            head_mask(QPTS, H * P_SIZE, P_SIZE), points * points, NN, HIGHEST
        )
        unit = jnp.where(
            lax.broadcasted_iota(jnp.int32, (HP, H), 0)
            == lax.broadcasted_iota(jnp.int32, (HP, H), 1),
            1.0,
            0.0,
        ).astype(BF16)
        both[0:HP] = dot(unit, pair_weight[...]).astype(BF16)
        spread_pairs[...] = jnp.zeros_like(spread_pairs)
        stat[...] = jnp.zeros_like(stat)

    mask, is_vec = query_mask()
    query = dot(query_single[...], query_weight[...], NT).astype(BF16)
    query_out[...] = query
    rows = spread(query, mask)
    vec_rows = jnp.where(is_vec[0:1], rows, 0.0)
    point_rows = rows - vec_rows
    query_norm = jnp.sum(point_rows * point_rows, axis=1, keepdims=True)
    scalar = dot(vec_rows.astype(BF16), key_qk[...])
    cross = dot(point_rows.astype(BF16), key_qk[...])
    upstream = dot(spread(grad_single[...], head_mask(VEC, VEC, C)).astype(BF16), key_v[0:VEC])
    upstream += dot(
        spread(grad_point[...], head_mask(VPTS, H * PV, PV)).astype(BF16), key_v[VEC:]
    )
    pairs = grad_pairs[...].astype(F32)
    for h in range(H):
        spread_pairs[:, h, :] = pairs[:, DZ * h : DZ * (h + 1)]
    heads = spread_pairs[...].astype(BF16)
    heads_out[...] = heads

    point_coef = head_column(head_weight, POINT_SCALE, KB)
    bias = head_column(chain_bias, 1.0, KB)
    key_live = key_line(mask_v) == 1
    key_chain = key_line(chain_v)
    begin = offsets[lax.axis_index("row")] + step * STEP
    lane = lax.broadcasted_iota(jnp.int32, (HP, 128), 1)
    for i in range(STEP):
        at = slice(HP * i, HP * (i + 1))
        left = jnp.concatenate([both[0:HP], heads[i]], axis=0)
        tile = dot(left, pair[i], NT)
        distance = query_norm[at] + key_norm[...] - 2.0 * cross[at]
        logits = LOGIT_WEIGHT * (scalar[at] * C ** (-0.5) + tile[0:HP] - point_coef * distance)
        same = jnp.where(key_chain == chain_s[begin + i], 1.0, 0.0)
        logits = logits + bias * same
        live = jnp.where(key_live, mask_s[begin + i], 0) == 1
        logits = jnp.where(live, logits, MASKED_LOGIT)
        up = upstream[at] + tile[HP:]
        top = jnp.max(logits, axis=1, keepdims=True)
        terms = jnp.exp(logits - top)
        total = jnp.sum(terms, axis=1, keepdims=True)
        moment = jnp.sum(terms * up, axis=1, keepdims=True)
        exp_out[at] = terms
        up_out[at] = up
        stat[at] = jnp.where(lane == 0, top, jnp.where(lane == 1, total, moment))
    for half in range(2):
        turned = stat[128 * half : 128 * (half + 1)].T
        for k in range(3):
            stats[k, pl.ds(2 * step + half, 1), :] = turned[k : k + 1]

    @pl.when(step == STEPS - 1)
    def _():
        for s in range(COLS):
            stats_out[s] = stats[...]


def spread_features(query, grad_single, grad_point, out):
    column = lax.broadcasted_iota(jnp.int32, (QB, ALL), 1)
    row = lax.broadcasted_iota(jnp.int32, (QB, ALL), 0)
    copies = jnp.where(lax.div(column, HP) == row, 1.0, 0.0).astype(BF16)

    def put(begin, values, group, size):
        count = values.shape[1]
        feature = lax.broadcasted_iota(jnp.int32, (count, ALL), 0)
        head = lax.rem(lax.broadcasted_iota(jnp.int32, (count, ALL), 1), HP)
        of = lax.div(lax.rem(feature, group), size)
        out[begin : begin + count] = jnp.where(
            of == head, dot(values, copies, TN), 0.0
        ).astype(BF16)

    put(0, query[:, 0:VEC], VEC, C)
    put(VEC, query[:, VEC:], H * P_SIZE, P_SIZE)
    put(QF, grad_single[...], VEC, C)
    put(QF + VEC, grad_point[...], H * PV, PV)


def grad_kernel(
    offsets,
    mask_s,
    head_weight,
    mask_v,
    parts,
    exp_terms,
    up,
    key_qk,
    query,
    query_single,
    query_weight,
    key_weight,
    grad_single,
    grad_point,
    weight_out,
    score_out,
    kept_out,
    given_out,
    single_out,
    key_grad,
    key_single_grad,
    query_weight_grad,
    columns_of,
):
    spread_features(query, grad_single, grad_point, columns_of)
    row_top = parts[0, 0]
    for s in range(1, COLS):
        row_top = jnp.maximum(row_top, parts[s, 0])
    row_total = jnp.zeros_like(row_top)
    moment = jnp.zeros_like(row_top)
    for s in range(COLS):
        share = jnp.exp(parts[s, 0] - row_top)
        row_total += share * parts[s, 1]
        moment += share * parts[s, 2]
    factor = jnp.exp(parts[lax.axis_index("col"), 0] - row_top) / row_total
    centre = moment / row_total
    columns = jnp.concatenate([factor, centre], axis=0).T
    key_live = jnp.where(key_line(mask_v) == 1, 1.0, 0.0)
    begin = offsets[lax.axis_index("row")]
    col_score = jnp.zeros((HP, KB), F32)
    row_score = []
    for i in range(QB):
        at = slice(HP * i, HP * (i + 1))
        chunk, off = i // 8, HP * (i % 8)
        fac = columns[off : off + HP, chunk : chunk + 1]
        mid = columns[off : off + HP, 8 + chunk : 9 + chunk]
        weights = exp_terms[at] * fac
        live = jnp.where(mask_s[begin + i] == 1, 1.0, 0.0)
        score = (weights * (up[at] - mid) * (key_live * live)).astype(BF16)
        weight_out[at] = weights.astype(BF16)
        score_out[at] = score
        score = score.astype(F32)
        col_score += score
        row_score.append(jnp.sum(score, axis=1, keepdims=True))
    row_score = jnp.concatenate(row_score, axis=0)

    mask, is_vec = query_mask()
    is_vec = is_vec[0:1]
    rows = spread(query[...], mask)
    scores = score_out[...]
    weights = weight_out[...]
    grad_coef = -2.0 * LOGIT_WEIGHT * POINT_SCALE
    key_points = head_mask(QPTS, H * P_SIZE, P_SIZE, axis=0)
    coef = jnp.sum(key_points * head_row(head_weight, grad_coef, QPTS), axis=1, keepdims=True)
    raw = dot(columns_of[0:QF], scores)
    key_grad[0:VEC] = SCALE_QK * raw[0:VEC]
    key_grad[VEC : 2 * VEC] = dot(columns_of[QF : QF + VEC], weights)
    key_grad[2 * VEC : 2 * VEC + QPTS] = coef * (
        key_qk[VEC:QF].astype(F32) * dot(key_points, col_score, NN, HIGHEST) - raw[VEC:QF]
    )
    key_grad[2 * VEC + QPTS : KF] = dot(columns_of[QF + VEC :], weights)
    key_single_grad[...] = two_part_dot(key_weight[...], key_grad[...], TN, values_first=True)
    raw = dot(scores, key_qk[...], NT)
    head_coef = head_column(head_weight, grad_coef, QF)
    head_coef = jnp.concatenate([head_coef] * QB, axis=0)
    masks = jnp.concatenate([mask] * QB, axis=0)
    raw = jnp.where(is_vec, SCALE_QK * raw, head_coef * (rows * row_score - raw)) * masks
    query_grad = jnp.sum(raw.reshape(QB, HP, QF), axis=1)
    single = two_part_dot(query_weight[...], query_grad, NN, values_first=True)
    for k in range(3):
        single_out[QB * k : QB * (k + 1)] = single[:, 128 * k : 128 * (k + 1)]
    query_weight_grad[...] = two_part_dot(query_single[...], query_grad, TN, values_first=True)
    first = lax.rem(lax.axis_index("row"), 2) == 0

    def put(q, begin, source, count, k):
        lanes = slice(128 * k, 128 * (k + 1))
        even = source[count * 2 * q : count * (2 * q + 1), lanes]
        odd = source[count * (2 * q + 1) : count * (2 * q + 2), lanes]
        at = slice(begin + count * k, begin + count * (k + 1))
        kept_out[q, at] = jnp.where(first, even, odd)
        given_out[q, at] = jnp.where(first, odd, even)

    for q in range(ROWS // 2):
        for k in range(2):
            put(q, 0, key_grad, FEATS, k)
        for k in range(3):
            put(q, 2 * FEATS, key_single_grad, 16, k)
            put(q, 2 * FEATS + 48, query_weight_grad, QFEATS, k)
        for out in (kept_out, given_out):
            out[q, 2 * FEATS + 48 + 3 * QFEATS :] = jnp.zeros((3, 128), F32)


def pair_kernel(pair_weight, pair, weights, scores, heads, pair_out, bias_out, lanes):
    step = pl.program_id(0)

    @pl.when(step == 0)
    def _():
        unit = jnp.where(
            lax.broadcasted_iota(jnp.int32, (HP, H), 0)
            == lax.broadcasted_iota(jnp.int32, (HP, H), 1),
            1.0,
            0.0,
        ).astype(BF16)
        values = LOGIT_WEIGHT * dot(unit, pair_weight[...])
        high = values.astype(BF16)
        lanes[0:HP] = high
        lanes[HP:] = (values - high.astype(F32)).astype(BF16)
        bias_out[...] = jnp.zeros_like(bias_out)

    total = jnp.zeros((HP, DZ), F32)
    for i in range(STEP):
        at = slice(HP * i, HP * (i + 1))
        score = scores[at]
        left = jnp.concatenate([weights[at], score, score], axis=0)
        right = jnp.concatenate([heads[i], lanes[...]], axis=0)
        pair_out[i] = dot(left, right, TN).astype(BF16)
        total += dot(score, pair[i])
    bias_out[...] += LOGIT_WEIGHT * total


def share_kernel(
    got, key_single, bias_part, query_single_part, share_out, single_out, total
):
    value = got[0]
    for s in range(1, ROWS // 2):
        value += got[s]
    total[...] = value
    key_grad = jnp.concatenate([total[0:56], total[FEATS : FEATS + 56]], axis=1)
    key_share = two_part_dot(key_single[...], key_grad, NN, values_first=True)
    for k in range(3):
        share_out[FEATS * k : FEATS * (k + 1)] = key_share[0:FEATS, 128 * k : 128 * (k + 1)]
    share_out[153:165] = bias_part[0:H]
    share_out[165:228] = total[150:213]
    share_out[228:420] = query_single_part[...]
    share_out[420:] = jnp.zeros((28, 128), F32)
    single_out[0:48] = total[102:150]
    single_out[48:] = jnp.zeros((4, 128), F32)


def share_of(got, key_single, bias_part, query_single_part):
    return pl.pallas_call(
        share_kernel,
        out_shape=(
            jax.ShapeDtypeStruct((448, 128), F32),
            jax.ShapeDtypeStruct((52, 128), F32),
        ),
        in_specs=[VECTORS] * 4,
        out_specs=(VECTORS,) * 2,
        scratch_shapes=[pltpu.VMEM((SHARE, 128), F32)],
        compiler_params=limit(16),
        name="row_share",
    )(got, key_single, bias_part, query_single_part)


def assemble_kernel(own, other, share, key_out, query_out, single_out, query_single_out, pair_out):
    first = lax.rem(lax.axis_index("row"), 2) == 0
    lane = pl.program_id(0)

    def chunk(r, begin, count):
        mine, theirs = own[r // 2, begin : begin + count], other[r // 2, begin : begin + count]
        if r % 2 == 1:
            mine, theirs = theirs, mine
        return jnp.where(first, mine, theirs)

    def put(k):
        for r in range(ROWS):
            key_out[FEATS * r : FEATS * (r + 1)] = chunk(r, FEATS * k, FEATS)
            query_out[QFEATS * r : QFEATS * (r + 1)] = chunk(r, 165 + QFEATS * k, QFEATS)
            single_out[16 * r : 16 * (r + 1)] = chunk(r, 228 + 16 * k, 16)
        query_single_out[...] = share[228 + QB * k : 228 + QB * (k + 1)]

    for k in range(3):
        pl.when(lane == k)(functools.partial(put, k))

    @pl.when(lane == 0)
    def _():
        total = chunk(0, 153, H)
        for r in range(1, ROWS):
            total += chunk(r, 153, H)
        pair_out[...] = total


def assembled(own, other, share):
    lanes = lambda rows: pl.BlockSpec((rows, 128), lambda k: (0, k))
    return pl.pallas_call(
        assemble_kernel,
        grid=(3,),
        out_shape=(
            jax.ShapeDtypeStruct((KF, DS), F32),
            jax.ShapeDtypeStruct((QF, DS), F32),
            jax.ShapeDtypeStruct((KB, DS), F32),
            jax.ShapeDtypeStruct((QB, DS), F32),
            jax.ShapeDtypeStruct((H, DZ), F32),
        ),
        in_specs=[VECTORS] * 3,
        out_specs=(lanes(KF), lanes(QF), lanes(KB), lanes(QB), whole((H, DZ))),
        compiler_params=limit(16),
        name="assemble",
    )(own, other, share)


def whole(shape):
    return pl.BlockSpec(shape, lambda s: (0,) * len(shape))


def rows_of(*shape):
    return pl.BlockSpec(shape, lambda s: (s,) + (0,) * (len(shape) - 1))


SCALARS = pl.BlockSpec(memory_space=pltpu.SMEM)
VECTORS = pl.BlockSpec(memory_space=pltpu.VMEM)
MIB = 1024 * 1024


def limit(mib):
    return pltpu.CompilerParams(vmem_limit_bytes=mib * MIB)


def scores_of(
    offsets, mask, chain, head_weight, chain_bias, query_single, key_single, query_weight,
    key_weight, pair_weight, pair, grad_single, grad_point, grad_pairs,
):
    return pl.pallas_call(
        score_kernel,
        grid=(STEPS,),
        out_shape=(
            jax.ShapeDtypeStruct((ALL, KB), F32),
            jax.ShapeDtypeStruct((ALL, KB), F32),
            jax.ShapeDtypeStruct((QF, KB), BF16),
            jax.ShapeDtypeStruct((QB, QF), BF16),
            jax.ShapeDtypeStruct((QB, HP, DZ), BF16),
            jax.ShapeDtypeStruct((COLS, 3, 8, 128), F32),
        ),
        in_specs=[SCALARS] * 5
        + [
            whole((32, 128)),
            whole((32, 128)),
            rows_of(STEP, DS),
            whole((KB, DS)),
            whole((QF, DS)),
            whole((KF, DS)),
            whole((H, DZ)),
            rows_of(STEP, KB, DZ),
            rows_of(STEP, VEC),
            rows_of(STEP, VPTS),
            rows_of(STEP, H * DZ),
        ],
        out_specs=(
            rows_of(SLAB, KB),
            rows_of(SLAB, KB),
            whole((QF, KB)),
            rows_of(STEP, QF),
            rows_of(STEP, HP, DZ),
            whole((COLS, 3, 8, 128)),
        ),
        scratch_shapes=[
            pltpu.VMEM((QF, KB), BF16),
            pltpu.VMEM((VEC + VPTS, KB), BF16),
            pltpu.VMEM((HP, KB), F32),
            pltpu.VMEM((HP, DZ), BF16),
            pltpu.VMEM((SLAB, 128), F32),
            pltpu.VMEM((STEP, HP, DZ), F32),
            pltpu.VMEM((3, 8, 128), F32),
        ],
        compiler_params=limit(30),
        cost_estimate=pl.CostEstimate(
            flops=2_000_000_000, bytes_accessed=8_000_000, transcendentals=262144
        ),
        name="row_scores",
    )(
        *(
            pltpu.with_memory_space_constraint(x, pltpu.HBM)
            for x in (
                offsets, mask, chain, head_weight, chain_bias,
                mask.reshape(32, 128), chain.reshape(32, 128), query_single, key_single,
                query_weight, key_weight, pair_weight, pair, grad_single, grad_point, grad_pairs,
            )
        ),
    )


def grads_of(
    offsets, mask, head_weight, parts, exp_terms, up, key_qk, query, query_single,
    query_weight, key_weight, grad_single, grad_point,
):
    return pl.pallas_call(
        grad_kernel,
        out_shape=(
            jax.ShapeDtypeStruct((ALL, KB), BF16),
            jax.ShapeDtypeStruct((ALL, KB), BF16),
            jax.ShapeDtypeStruct((ROWS // 2, SHARE, 128), F32),
            jax.ShapeDtypeStruct((ROWS // 2, SHARE, 128), F32),
            jax.ShapeDtypeStruct((3 * QB, 128), F32),
        ),
        in_specs=[SCALARS] * 3 + [VECTORS] * 11,
        out_specs=(VECTORS,) * 5,
        scratch_shapes=[
            pltpu.VMEM((KF, KB), F32),
            pltpu.VMEM((KB, DS), F32),
            pltpu.VMEM((QF, DS), F32),
            pltpu.VMEM((QF + VEC + VPTS, ALL), BF16),
        ],
        compiler_params=limit(24),
        cost_estimate=pl.CostEstimate(
            flops=3_000_000_000, bytes_accessed=8_000_000, transcendentals=20000
        ),
        name="feature_grads",
    )(
        offsets, mask, head_weight, mask.reshape(32, 128), parts, exp_terms, up, key_qk,
        query, query_single, query_weight, key_weight, grad_single, grad_point,
    )


def pair_grads_of(pair_weight, pair, weights, scores, heads):
    return pl.pallas_call(
        pair_kernel,
        grid=(STEPS,),
        out_shape=(
            jax.ShapeDtypeStruct((QB, KB, DZ), BF16),
            jax.ShapeDtypeStruct((HP, DZ), F32),
        ),
        in_specs=[
            whole((H, DZ)),
            rows_of(STEP, KB, DZ),
            rows_of(SLAB, KB),
            rows_of(SLAB, KB),
            rows_of(STEP, HP, DZ),
        ],
        out_specs=(rows_of(STEP, KB, DZ), whole((HP, DZ))),
        scratch_shapes=[pltpu.VMEM((2 * HP, DZ), BF16)],
        compiler_params=limit(40),
        cost_estimate=pl.CostEstimate(
            flops=2_000_000_000, bytes_accessed=10_000_000, transcendentals=0
        ),
        name="pair_grads",
    )(pair_weight, pair, weights, scores, heads)


CHIPS = [[2 * i + core for i in range(ROWS // 2)] for core in range(2)]


ALONG_X = [[4 * x + z for x in range(4)] for z in range(4)]
ALONG_Z = [[4 * x + z for z in range(4)] for x in range(4)]


def other_core(values):
    return lax.ppermute(values, "row", [(i, i ^ 1) for i in range(ROWS)])


def exchange(values, axis, groups=None):
    return lax.all_to_all(values, axis, 0, 0, axis_index_groups=groups)


def gather(values, axis, parts, groups=None):
    return exchange(jnp.broadcast_to(values[None], (parts, *values.shape)), axis, groups)


def scatter_row(kept, given):
    return exchange(kept + other_core(given), "row", CHIPS)


def sum_col(values):
    share = exchange(values.reshape(4, -1, values.shape[1]), "col", ALONG_X)
    share = jnp.sum(share, axis=0)
    share = jnp.sum(gather(share, "col", 4, ALONG_Z), axis=0)
    return gather(share, "col", 4, ALONG_X).reshape(values.shape)


def local(
    query_single,
    key_single,
    query_weight,
    key_weight,
    pair_weight,
    head_weight,
    chain_bias,
    pair,
    residue_mask,
    chain_index,
    strip_offsets,
    grad_single_out,
    grad_point_out,
    grad_pair_out,
):
    query_weight, key_weight, pair_weight = query_weight.T, key_weight.T, pair_weight.T
    terms, up, key_qk, query, heads, own = scores_of(
        strip_offsets, residue_mask, chain_index, head_weight, chain_bias, query_single,
        key_single, query_weight, key_weight, pair_weight, pair, grad_single_out,
        grad_point_out, grad_pair_out,
    )
    with jax.named_scope("row_statistics"):
        parts = exchange(own, "col")
    weights, scores, kept, given, query_single_part = grads_of(
        strip_offsets, residue_mask, head_weight, parts, terms, up, key_qk, query,
        query_single, query_weight, key_weight, grad_single_out, grad_point_out,
    )
    with jax.named_scope("row_sum"):
        got = scatter_row(kept, given)
    grad_pair, bias_part = pair_grads_of(pair_weight, pair, weights, scores, heads)
    share, single = share_of(got, key_single, bias_part, query_single_part)
    with jax.named_scope("col_sum"):
        share = sum_col(share)
    with jax.named_scope("row_gather"):
        own = jnp.concatenate(
            [share[:228], single], axis=0
        )
        own = gather(own, "row", ROWS // 2, CHIPS)
        results = assembled(own, other_core(own), share)
    key_weight_grad, query_weight_grad, key_single_grad, query_single_grad, pair_weight_grad = results
    return (
        query_single_grad,
        key_single_grad,
        query_weight_grad.T,
        key_weight_grad.T,
        pair_weight_grad.T,
        grad_pair,
    )


def solution(mesh):
    in_specs = (
        P("row", None),
        P("col", None),
        P(),
        P(),
        P(),
        P(),
        P(),
        P("row", "col", None),
        P(),
        P(),
        P(),
        P("row", None),
        P("row", None),
        P("row", None),
    )
    out_specs = (P("row", None), P("col", None), P(), P(), P(), P("row", "col", None))
    return jax.shard_map(local, mesh=mesh, in_specs=in_specs, out_specs=out_specs, check_vma=False)
```

```python
import functools
import math

import jax
import jax.numpy as jnp
from jax import lax
from jax.experimental import pallas as pl
from jax.experimental.pallas import tpu as pltpu
from jax.sharding import PartitionSpec as P

H = 12
C = 16
P_SIZE = 4
PV = 8
DZ = 128
DS = 384
QB = 64
KB = 256
QF = 336
KF = 816
VEC = H * C
QPTS = 3 * H * P_SIZE
VPTS = 3 * H * PV
ROWS = 16
COLS = 16
HP = 16
STEP = 16
STEPS = QB // STEP
SLAB = STEP * HP
ALL = QB * HP
FEATS = KF // ROWS
QFEATS = QF // ROWS
SHARE = 216

LOGIT_WEIGHT = math.sqrt(1.0 / 3.0)
MASKED_LOGIT = -100000.0
SCALE_QK = LOGIT_WEIGHT * C ** (-0.5)
POINT_SCALE = math.sqrt(2.0 / (9.0 * P_SIZE)) / 2.0
F32 = jnp.float32
BF16 = jnp.bfloat16
HIGHEST = lax.Precision.HIGHEST

NN = (((1,), (0,)), ((), ()))
NT = (((1,), (1,)), ((), ()))
TN = (((0,), (0,)), ((), ()))


def dot(a, b, dims=NN, precision=None):
    return lax.dot_general(a, b, dims, precision=precision, preferred_element_type=F32)


def two_part_dot(fixed, values, dims, values_first=False):
    high = values.astype(BF16)
    low = (values - high.astype(F32)).astype(BF16)
    if values_first:
        return dot(high, fixed, dims) + dot(low, fixed, dims)
    return dot(fixed, high, dims) + dot(fixed, low, dims)


def head_mask(count, group, size, offset=0, axis=1):
    shape = (HP, count) if axis == 1 else (count, HP)
    feature = lax.broadcasted_iota(jnp.int32, shape, axis)
    head = lax.broadcasted_iota(jnp.int32, shape, 1 - axis)
    return jnp.where(lax.div(lax.rem(feature, group), size) == head, 1.0, 0.0).astype(F32)


def query_mask():
    shape = (HP, QF)
    feature = lax.broadcasted_iota(jnp.int32, shape, 1)
    head = lax.broadcasted_iota(jnp.int32, shape, 0)
    of = jnp.where(
        feature < VEC,
        lax.div(feature, C),
        lax.div(lax.rem(jnp.maximum(feature - VEC, 0), H * P_SIZE), P_SIZE),
    )
    return jnp.where(of == head, 1.0, 0.0).astype(F32), feature < VEC


def spread(values, mask):
    rows, count = values.shape
    return (values.astype(F32)[:, None, :] * mask[None]).reshape(rows * HP, count)


def head_column(ref, scale, count):
    index = lax.broadcasted_iota(jnp.int32, (HP, count), 0)
    column = jnp.zeros((HP, count), F32)
    for h in range(H):
        column = jnp.where(index == h, ref[h] * scale, column)
    return column


def head_row(ref, scale, count):
    index = lax.broadcasted_iota(jnp.int32, (count, HP), 1)
    row = jnp.zeros((count, HP), F32)
    for h in range(H):
        row = jnp.where(index == h, ref[h] * scale, row)
    return row


def key_line(ref):
    begin = lax.axis_index("col") * 2
    return jnp.concatenate([ref[pl.ds(begin, 1), :], ref[pl.ds(begin + 1, 1), :]], axis=1)


def score_kernel(
    offsets,
    mask_s,
    chain_s,
    head_weight,
    chain_bias,
    mask_v,
    chain_v,
    query_single,
    key_single,
    query_weight,
    key_weight,
    pair_weight,
    pair,
    grad_single,
    grad_point,
    grad_pairs,
    exp_out,
    up_out,
    key_out,
    query_out,
    heads_out,
    stats_out,
    key_qk,
    key_v,
    key_norm,
    both,
    stat,
    spread_pairs,
    stats,
):
    step = pl.program_id(0)

    @pl.when(step == 0)
    def _():
        feats = dot(key_weight[...], key_single[...], NT).astype(BF16)
        key_qk[0:VEC] = feats[0:VEC]
        key_qk[VEC:QF] = feats[2 * VEC : 2 * VEC + QPTS]
        key_v[0:VEC] = feats[VEC : 2 * VEC]
        key_v[VEC:] = feats[2 * VEC + QPTS :]
        key_out[...] = key_qk[...]
        points = feats[2 * VEC : 2 * VEC + QPTS].astype(F32)
        key_norm[...] = dot(
            head_mask(QPTS, H * P_SIZE, P_SIZE), points * points, NN, HIGHEST
        )
        unit = jnp.where(
            lax.broadcasted_iota(jnp.int32, (HP, H), 0)
            == lax.broadcasted_iota(jnp.int32, (HP, H), 1),
            1.0,
            0.0,
        ).astype(BF16)
        both[0:HP] = dot(unit, pair_weight[...]).astype(BF16)
        spread_pairs[...] = jnp.zeros_like(spread_pairs)
        stat[...] = jnp.zeros_like(stat)

    mask, is_vec = query_mask()
    query = dot(query_single[...], query_weight[...], NT).astype(BF16)
    query_out[...] = query
    rows = spread(query, mask)
    vec_rows = jnp.where(is_vec[0:1], rows, 0.0)
    point_rows = rows - vec_rows
    query_norm = jnp.sum(point_rows * point_rows, axis=1, keepdims=True)
    scalar = dot(vec_rows.astype(BF16), key_qk[...])
    cross = dot(point_rows.astype(BF16), key_qk[...])
    upstream = dot(spread(grad_single[...], head_mask(VEC, VEC, C)).astype(BF16), key_v[0:VEC])
    upstream += dot(
        spread(grad_point[...], head_mask(VPTS, H * PV, PV)).astype(BF16), key_v[VEC:]
    )
    pairs = grad_pairs[...].astype(F32)
    for h in range(H):
        spread_pairs[:, h, :] = pairs[:, DZ * h : DZ * (h + 1)]
    heads = spread_pairs[...].astype(BF16)
    heads_out[...] = heads

    point_coef = head_column(head_weight, POINT_SCALE, KB)
    bias = head_column(chain_bias, 1.0, KB)
    key_live = key_line(mask_v) == 1
    key_chain = key_line(chain_v)
    begin = offsets[lax.axis_index("row")] + step * STEP
    lane = lax.broadcasted_iota(jnp.int32, (HP, 128), 1)
    for i in range(STEP):
        at = slice(HP * i, HP * (i + 1))
        left = jnp.concatenate([both[0:HP], heads[i]], axis=0)
        tile = dot(left, pair[i], NT)
        distance = query_norm[at] + key_norm[...] - 2.0 * cross[at]
        logits = LOGIT_WEIGHT * (scalar[at] * C ** (-0.5) + tile[0:HP] - point_coef * distance)
        same = jnp.where(key_chain == chain_s[begin + i], 1.0, 0.0)
        logits = logits + bias * same
        live = jnp.where(key_live, mask_s[begin + i], 0) == 1
        logits = jnp.where(live, logits, MASKED_LOGIT)
        up = upstream[at] + tile[HP:]
        top = jnp.max(logits, axis=1, keepdims=True)
        terms = jnp.exp(logits - top)
        total = jnp.sum(terms, axis=1, keepdims=True)
        moment = jnp.sum(terms * up, axis=1, keepdims=True)
        exp_out[at] = terms
        up_out[at] = up
        stat[at] = jnp.where(lane == 0, top, jnp.where(lane == 1, total, moment))
    for half in range(2):
        turned = stat[128 * half : 128 * (half + 1)].T
        for k in range(3):
            stats[k, pl.ds(2 * step + half, 1), :] = turned[k : k + 1]

    @pl.when(step == STEPS - 1)
    def _():
        for s in range(COLS):
            stats_out[s] = stats[...]


def spread_features(query, grad_single, grad_point, out):
    column = lax.broadcasted_iota(jnp.int32, (QB, ALL), 1)
    row = lax.broadcasted_iota(jnp.int32, (QB, ALL), 0)
    copies = jnp.where(lax.div(column, HP) == row, 1.0, 0.0).astype(BF16)

    def put(begin, values, group, size):
        count = values.shape[1]
        feature = lax.broadcasted_iota(jnp.int32, (count, ALL), 0)
        head = lax.rem(lax.broadcasted_iota(jnp.int32, (count, ALL), 1), HP)
        of = lax.div(lax.rem(feature, group), size)
        out[begin : begin + count] = jnp.where(
            of == head, dot(values, copies, TN), 0.0
        ).astype(BF16)

    put(0, query[:, 0:VEC], VEC, C)
    put(VEC, query[:, VEC:], H * P_SIZE, P_SIZE)
    put(QF, grad_single[...], VEC, C)
    put(QF + VEC, grad_point[...], H * PV, PV)


def grad_kernel(
    offsets,
    mask_s,
    head_weight,
    mask_v,
    parts,
    exp_terms,
    up,
    key_qk,
    query,
    query_single,
    query_weight,
    key_weight,
    grad_single,
    grad_point,
    weight_out,
    score_out,
    kept_out,
    given_out,
    single_out,
    key_grad,
    key_single_grad,
    query_weight_grad,
    columns_of,
):
    spread_features(query, grad_single, grad_point, columns_of)
    row_top = parts[0, 0]
    for s in range(1, COLS):
        row_top = jnp.maximum(row_top, parts[s, 0])
    row_total = jnp.zeros_like(row_top)
    moment = jnp.zeros_like(row_top)
    for s in range(COLS):
        share = jnp.exp(parts[s, 0] - row_top)
        row_total += share * parts[s, 1]
        moment += share * parts[s, 2]
    factor = jnp.exp(parts[lax.axis_index("col"), 0] - row_top) / row_total
    centre = moment / row_total
    columns = jnp.concatenate([factor, centre], axis=0).T
    key_live = jnp.where(key_line(mask_v) == 1, 1.0, 0.0)
    begin = offsets[lax.axis_index("row")]
    col_score = jnp.zeros((HP, KB), F32)
    row_score = []
    for i in range(QB):
        at = slice(HP * i, HP * (i + 1))
        chunk, off = i // 8, HP * (i % 8)
        fac = columns[off : off + HP, chunk : chunk + 1]
        mid = columns[off : off + HP, 8 + chunk : 9 + chunk]
        weights = exp_terms[at] * fac
        live = jnp.where(mask_s[begin + i] == 1, 1.0, 0.0)
        score = (weights * (up[at] - mid) * (key_live * live)).astype(BF16)
        weight_out[at] = weights.astype(BF16)
        score_out[at] = score
        score = score.astype(F32)
        col_score += score
        row_score.append(jnp.sum(score, axis=1, keepdims=True))
    row_score = jnp.concatenate(row_score, axis=0)

    mask, is_vec = query_mask()
    is_vec = is_vec[0:1]
    rows = spread(query[...], mask)
    scores = score_out[...]
    weights = weight_out[...]
    grad_coef = -2.0 * LOGIT_WEIGHT * POINT_SCALE
    key_points = head_mask(QPTS, H * P_SIZE, P_SIZE, axis=0)
    coef = jnp.sum(key_points * head_row(head_weight, grad_coef, QPTS), axis=1, keepdims=True)
    raw = dot(columns_of[0:QF], scores)
    key_grad[0:VEC] = SCALE_QK * raw[0:VEC]
    key_grad[VEC : 2 * VEC] = dot(columns_of[QF : QF + VEC], weights)
    key_grad[2 * VEC : 2 * VEC + QPTS] = coef * (
        key_qk[VEC:QF].astype(F32) * dot(key_points, col_score, NN, HIGHEST) - raw[VEC:QF]
    )
    key_grad[2 * VEC + QPTS : KF] = dot(columns_of[QF + VEC :], weights)
    key_single_grad[...] = two_part_dot(key_weight[...], key_grad[...], TN, values_first=True)
    raw = dot(scores, key_qk[...], NT)
    head_coef = head_column(head_weight, grad_coef, QF)
    head_coef = jnp.concatenate([head_coef] * QB, axis=0)
    masks = jnp.concatenate([mask] * QB, axis=0)
    raw = jnp.where(is_vec, SCALE_QK * raw, head_coef * (rows * row_score - raw)) * masks
    query_grad = jnp.sum(raw.reshape(QB, HP, QF), axis=1)
    single = two_part_dot(query_weight[...], query_grad, NN, values_first=True)
    for k in range(3):
        single_out[QB * k : QB * (k + 1)] = single[:, 128 * k : 128 * (k + 1)]
    query_weight_grad[...] = two_part_dot(query_single[...], query_grad, TN, values_first=True)
    first = lax.rem(lax.axis_index("row"), 2) == 0

    def put(q, begin, source, count, k):
        lanes = slice(128 * k, 128 * (k + 1))
        even = source[count * 2 * q : count * (2 * q + 1), lanes]
        odd = source[count * (2 * q + 1) : count * (2 * q + 2), lanes]
        at = slice(begin + count * k, begin + count * (k + 1))
        kept_out[q, at] = jnp.where(first, even, odd)
        given_out[q, at] = jnp.where(first, odd, even)

    for q in range(ROWS // 2):
        for k in range(2):
            put(q, 0, key_grad, FEATS, k)
        for k in range(3):
            put(q, 2 * FEATS, key_single_grad, 16, k)
            put(q, 2 * FEATS + 48, query_weight_grad, QFEATS, k)
        for out in (kept_out, given_out):
            out[q, 2 * FEATS + 48 + 3 * QFEATS :] = jnp.zeros((3, 128), F32)


def pair_kernel(pair_weight, pair, weights, scores, heads, pair_out, bias_out, lanes):
    step = pl.program_id(0)

    @pl.when(step == 0)
    def _():
        unit = jnp.where(
            lax.broadcasted_iota(jnp.int32, (HP, H), 0)
            == lax.broadcasted_iota(jnp.int32, (HP, H), 1),
            1.0,
            0.0,
        ).astype(BF16)
        values = LOGIT_WEIGHT * dot(unit, pair_weight[...])
        high = values.astype(BF16)
        lanes[0:HP] = high
        lanes[HP:] = (values - high.astype(F32)).astype(BF16)
        bias_out[...] = jnp.zeros_like(bias_out)

    total = jnp.zeros((HP, DZ), F32)
    for i in range(STEP):
        at = slice(HP * i, HP * (i + 1))
        score = scores[at]
        left = jnp.concatenate([weights[at], score, score], axis=0)
        right = jnp.concatenate([heads[i], lanes[...]], axis=0)
        pair_out[i] = dot(left, right, TN).astype(BF16)
        total += dot(score, pair[i])
    bias_out[...] += LOGIT_WEIGHT * total


def share_kernel(
    got, key_single, bias_part, query_single_part, share_out, single_out, total
):
    value = got[0]
    for s in range(1, ROWS // 2):
        value += got[s]
    total[...] = value
    key_grad = jnp.concatenate([total[0:56], total[FEATS : FEATS + 56]], axis=1)
    key_share = two_part_dot(key_single[...], key_grad, NN, values_first=True)
    for k in range(3):
        share_out[FEATS * k : FEATS * (k + 1)] = key_share[0:FEATS, 128 * k : 128 * (k + 1)]
    share_out[153:165] = bias_part[0:H]
    share_out[165:228] = total[150:213]
    share_out[228:420] = query_single_part[...]
    share_out[420:] = jnp.zeros((28, 128), F32)
    single_out[0:48] = total[102:150]
    single_out[48:] = jnp.zeros((4, 128), F32)


def share_of(got, key_single, bias_part, query_single_part):
    return pl.pallas_call(
        share_kernel,
        out_shape=(
            jax.ShapeDtypeStruct((448, 128), F32),
            jax.ShapeDtypeStruct((52, 128), F32),
        ),
        in_specs=[VECTORS] * 4,
        out_specs=(VECTORS,) * 2,
        scratch_shapes=[pltpu.VMEM((SHARE, 128), F32)],
        compiler_params=limit(16),
        name="row_share",
    )(got, key_single, bias_part, query_single_part)


def assemble_kernel(own, other, share, key_out, query_out, single_out, query_single_out, pair_out):
    first = lax.rem(lax.axis_index("row"), 2) == 0
    lane = pl.program_id(0)

    def chunk(r, begin, count):
        mine, theirs = own[r // 2, begin : begin + count], other[r // 2, begin : begin + count]
        if r % 2 == 1:
            mine, theirs = theirs, mine
        return jnp.where(first, mine, theirs)

    def put(k):
        for r in range(ROWS):
            key_out[FEATS * r : FEATS * (r + 1)] = chunk(r, FEATS * k, FEATS)
            query_out[QFEATS * r : QFEATS * (r + 1)] = chunk(r, 165 + QFEATS * k, QFEATS)
            single_out[16 * r : 16 * (r + 1)] = chunk(r, 228 + 16 * k, 16)
        query_single_out[...] = share[228 + QB * k : 228 + QB * (k + 1)]

    for k in range(3):
        pl.when(lane == k)(functools.partial(put, k))

    @pl.when(lane == 0)
    def _():
        total = chunk(0, 153, H)
        for r in range(1, ROWS):
            total += chunk(r, 153, H)
        pair_out[...] = total


def assembled(own, other, share):
    lanes = lambda rows: pl.BlockSpec((rows, 128), lambda k: (0, k))
    return pl.pallas_call(
        assemble_kernel,
        grid=(3,),
        out_shape=(
            jax.ShapeDtypeStruct((KF, DS), F32),
            jax.ShapeDtypeStruct((QF, DS), F32),
            jax.ShapeDtypeStruct((KB, DS), F32),
            jax.ShapeDtypeStruct((QB, DS), F32),
            jax.ShapeDtypeStruct((H, DZ), F32),
        ),
        in_specs=[VECTORS] * 3,
        out_specs=(lanes(KF), lanes(QF), lanes(KB), lanes(QB), whole((H, DZ))),
        compiler_params=limit(16),
        name="assemble",
    )(own, other, share)


def whole(shape):
    return pl.BlockSpec(shape, lambda s: (0,) * len(shape))


def rows_of(*shape):
    return pl.BlockSpec(shape, lambda s: (s,) + (0,) * (len(shape) - 1))


SCALARS = pl.BlockSpec(memory_space=pltpu.SMEM)
VECTORS = pl.BlockSpec(memory_space=pltpu.VMEM)
MIB = 1024 * 1024


def limit(mib):
    return pltpu.CompilerParams(vmem_limit_bytes=mib * MIB)


def scores_of(
    offsets, mask, chain, head_weight, chain_bias, query_single, key_single, query_weight,
    key_weight, pair_weight, pair, grad_single, grad_point, grad_pairs,
):
    return pl.pallas_call(
        score_kernel,
        grid=(STEPS,),
        out_shape=(
            jax.ShapeDtypeStruct((ALL, KB), F32),
            jax.ShapeDtypeStruct((ALL, KB), F32),
            jax.ShapeDtypeStruct((QF, KB), BF16),
            jax.ShapeDtypeStruct((QB, QF), BF16),
            jax.ShapeDtypeStruct((QB, HP, DZ), BF16),
            jax.ShapeDtypeStruct((COLS, 3, 8, 128), F32),
        ),
        in_specs=[SCALARS] * 5
        + [
            whole((32, 128)),
            whole((32, 128)),
            rows_of(STEP, DS),
            whole((KB, DS)),
            whole((QF, DS)),
            whole((KF, DS)),
            whole((H, DZ)),
            rows_of(STEP, KB, DZ),
            rows_of(STEP, VEC),
            rows_of(STEP, VPTS),
            rows_of(STEP, H * DZ),
        ],
        out_specs=(
            rows_of(SLAB, KB),
            rows_of(SLAB, KB),
            whole((QF, KB)),
            rows_of(STEP, QF),
            rows_of(STEP, HP, DZ),
            whole((COLS, 3, 8, 128)),
        ),
        scratch_shapes=[
            pltpu.VMEM((QF, KB), BF16),
            pltpu.VMEM((VEC + VPTS, KB), BF16),
            pltpu.VMEM((HP, KB), F32),
            pltpu.VMEM((HP, DZ), BF16),
            pltpu.VMEM((SLAB, 128), F32),
            pltpu.VMEM((STEP, HP, DZ), F32),
            pltpu.VMEM((3, 8, 128), F32),
        ],
        compiler_params=limit(30),
        cost_estimate=pl.CostEstimate(
            flops=2_000_000_000, bytes_accessed=8_000_000, transcendentals=262144
        ),
        name="row_scores",
    )(
        *(
            pltpu.with_memory_space_constraint(x, pltpu.HBM)
            for x in (
                offsets, mask, chain, head_weight, chain_bias,
                mask.reshape(32, 128), chain.reshape(32, 128), query_single, key_single,
                query_weight, key_weight, pair_weight, pair, grad_single, grad_point, grad_pairs,
            )
        ),
    )


def grads_of(
    offsets, mask, head_weight, parts, exp_terms, up, key_qk, query, query_single,
    query_weight, key_weight, grad_single, grad_point,
):
    return pl.pallas_call(
        grad_kernel,
        out_shape=(
            jax.ShapeDtypeStruct((ALL, KB), BF16),
            jax.ShapeDtypeStruct((ALL, KB), BF16),
            jax.ShapeDtypeStruct((ROWS // 2, SHARE, 128), F32),
            jax.ShapeDtypeStruct((ROWS // 2, SHARE, 128), F32),
            jax.ShapeDtypeStruct((3 * QB, 128), F32),
        ),
        in_specs=[SCALARS] * 3 + [VECTORS] * 11,
        out_specs=(VECTORS,) * 5,
        scratch_shapes=[
            pltpu.VMEM((KF, KB), F32),
            pltpu.VMEM((KB, DS), F32),
            pltpu.VMEM((QF, DS), F32),
            pltpu.VMEM((QF + VEC + VPTS, ALL), BF16),
        ],
        compiler_params=limit(24),
        cost_estimate=pl.CostEstimate(
            flops=3_000_000_000, bytes_accessed=8_000_000, transcendentals=20000
        ),
        name="feature_grads",
    )(
        offsets, mask, head_weight, mask.reshape(32, 128), parts, exp_terms, up, key_qk,
        query, query_single, query_weight, key_weight, grad_single, grad_point,
    )


def pair_grads_of(pair_weight, pair, weights, scores, heads):
    return pl.pallas_call(
        pair_kernel,
        grid=(STEPS,),
        out_shape=(
            jax.ShapeDtypeStruct((QB, KB, DZ), BF16),
            jax.ShapeDtypeStruct((HP, DZ), F32),
        ),
        in_specs=[
            whole((H, DZ)),
            rows_of(STEP, KB, DZ),
            rows_of(SLAB, KB),
            rows_of(SLAB, KB),
            rows_of(STEP, HP, DZ),
        ],
        out_specs=(rows_of(STEP, KB, DZ), whole((HP, DZ))),
        scratch_shapes=[pltpu.VMEM((2 * HP, DZ), BF16)],
        compiler_params=limit(40),
        cost_estimate=pl.CostEstimate(
            flops=2_000_000_000, bytes_accessed=10_000_000, transcendentals=0
        ),
        name="pair_grads",
    )(
        pair_weight, pltpu.with_memory_space_constraint(pair, pltpu.HBM), weights, scores, heads
    )


CHIPS = [[2 * i + core for i in range(ROWS // 2)] for core in range(2)]


ALONG_X = [[4 * x + z for x in range(4)] for z in range(4)]
ALONG_Z = [[4 * x + z for z in range(4)] for x in range(4)]


def other_core(values):
    return lax.ppermute(values, "row", [(i, i ^ 1) for i in range(ROWS)])


def exchange(values, axis, groups=None):
    return lax.all_to_all(values, axis, 0, 0, axis_index_groups=groups)


def gather(values, axis, parts, groups=None):
    return exchange(jnp.broadcast_to(values[None], (parts, *values.shape)), axis, groups)


def scatter_row(kept, given):
    return exchange(kept + other_core(given), "row", CHIPS)


def sum_col(values):
    share = exchange(values.reshape(4, -1, values.shape[1]), "col", ALONG_X)
    share = jnp.sum(share, axis=0)
    share = jnp.sum(gather(share, "col", 4, ALONG_Z), axis=0)
    return gather(share, "col", 4, ALONG_X).reshape(values.shape)


def local(
    query_single,
    key_single,
    query_weight,
    key_weight,
    pair_weight,
    head_weight,
    chain_bias,
    pair,
    residue_mask,
    chain_index,
    strip_offsets,
    grad_single_out,
    grad_point_out,
    grad_pair_out,
):
    query_weight, key_weight, pair_weight = query_weight.T, key_weight.T, pair_weight.T
    terms, up, key_qk, query, heads, own = scores_of(
        strip_offsets, residue_mask, chain_index, head_weight, chain_bias, query_single,
        key_single, query_weight, key_weight, pair_weight, pair, grad_single_out,
        grad_point_out, grad_pair_out,
    )
    with jax.named_scope("row_statistics"):
        parts = exchange(own, "col")
    weights, scores, kept, given, query_single_part = grads_of(
        strip_offsets, residue_mask, head_weight, parts, terms, up, key_qk, query,
        query_single, query_weight, key_weight, grad_single_out, grad_point_out,
    )
    with jax.named_scope("row_sum"):
        got = scatter_row(kept, given)
    grad_pair, bias_part = pair_grads_of(pair_weight, pair, weights, scores, heads)
    share, single = share_of(got, key_single, bias_part, query_single_part)
    with jax.named_scope("col_sum"):
        share = sum_col(share)
    with jax.named_scope("row_gather"):
        own = jnp.concatenate(
            [share[:228], single], axis=0
        )
        own = gather(own, "row", ROWS // 2, CHIPS)
        results = assembled(own, other_core(own), share)
    key_weight_grad, query_weight_grad, key_single_grad, query_single_grad, pair_weight_grad = results
    return (
        query_single_grad,
        key_single_grad,
        query_weight_grad.T,
        key_weight_grad.T,
        pair_weight_grad.T,
        grad_pair,
    )


def solution(mesh):
    in_specs = (
        P("row", None),
        P("col", None),
        P(),
        P(),
        P(),
        P(),
        P(),
        P("row", "col", None),
        P(),
        P(),
        P(),
        P("row", None),
        P("row", None),
        P("row", None),
    )
    out_specs = (P("row", None), P("col", None), P(), P(), P(), P("row", "col", None))
    return jax.shard_map(local, mesh=mesh, in_specs=in_specs, out_specs=out_specs, check_vma=False)
```
